128 devices in a mesh: dp: 16 (over x, y_hi, core), tensor: 8 (over z, y_lo).
Axes of the slice: x: 4, y: 4 (y_hi: 2, y_lo: 2; y = y_hi * 2 + y_lo), z: 4, core: 2. Of those that a mesh axis runs over, the one named last changes fastest.
Arguments:
- tokens: bfloat16 [16384, 1536], P(('dp', 'tensor')), may hold values from -6 to 6
- gain_mix: bfloat16 [1536], P('dp'), may hold values from 0.099609375 to 1.8984375
- in_weight: bfloat16 [1536, 3, 1536], P('dp', None, 'tensor'), may hold values from -0.15625 to 0.15625
- conv_kernel: bfloat16 [3, 1536], P(None, 'tensor'), may hold values from -3.5 to 3.5
- out_weight: bfloat16 [1536, 1536], P('tensor', 'dp'), may hold values from -0.15625 to 0.15625
- gain_ffn: bfloat16 [1536], P('dp'), may hold values from 0.099609375 to 1.8984375
- gate_weight: bfloat16 [1536, 6912], P('dp', 'tensor'), may hold values from -0.15625 to 0.15625
- up_weight: bfloat16 [1536, 6912], P('dp', 'tensor'), may hold values from -0.15625 to 0.15625
- down_weight: bfloat16 [6912, 1536], P('tensor', 'dp'), may hold values from -0.078125 to 0.078125
- lengths: int32 [16], P('dp'), may hold values from 256 to 1024, as said below
- cotangent: bfloat16 [16384, 1536], P(('dp', 'tensor')), may hold values from -6 to 6
Outputs:
- layer_out: bfloat16 [16384, 1536], P(('dp', 'tensor'))
- tokens_grad: bfloat16 [16384, 1536], P(('dp', 'tensor'))
- gain_mix_grad: float32 [1536], P(('dp', 'tensor'))
- in_grad: float32 [1536, 3, 1536], P('dp', None, 'tensor')
- kernel_grad: float32 [3, 1536], P(None, ('dp', 'tensor'))
- out_grad: float32 [1536, 1536], P('tensor', 'dp')
- gain_ffn_grad: float32 [1536], P(('dp', 'tensor'))
- gate_grad: float32 [1536, 6912], P('dp', 'tensor')
- up_grad: float32 [1536, 6912], P('dp', 'tensor')
- down_grad: float32 [6912, 1536], P('tensor', 'dp')
The draws below stay inside these ranges and needn't reach their ends.
Inputs may be any that keep to these rules, and one draw needn't show every extreme that they name: `lengths`: lengths run from 256 to 1024; at least 4 sequences have length 1024.
All inputs are finite; a program needn't handle non-finite values.
Results may differ from the reference program's by a relative error of at most 0.025.
Values may be sent and summed in bfloat16 or wider, within the bound.
A program may use at most 128 MiB of HBM per device.

```python
import jax
import jax.numpy as jnp
from jax import lax

D = 1536
FF = 6912
SLOTS = 1024
SEQS = 16
TOKENS = 16384


def draw_lengths(key, part):
    key = jax.random.fold_in(key, 7)
    first_key, second_key = jax.random.split(key)
    base = jax.random.randint(first_key, (SEQS,), SLOTS // 4, SLOTS + 1)
    order = jax.random.permutation(second_key, SEQS)
    full_set = order < max(1, SEQS // 4)
    return jnp.where(full_set, SLOTS, base).astype(jnp.int32)


def block_scale(rng, shape, pieces, smallest, largest):
    level = 1.0
    for axis_at, blocks in pieces:
        draws = jax.random.uniform(jax.random.fold_in(jax.random.fold_in(rng, 6), axis_at), (blocks,), jnp.float32, smallest / len(pieces), largest / len(pieces))
        level = level * jnp.repeat(jnp.exp(draws), shape[axis_at] // blocks).reshape((-1,) + (1,) * (len(shape) - 1 - axis_at))
    return level


def normal_values(stream_key, dims, deviation, reach, cuts=(), kind=jnp.bfloat16):
    level = block_scale(stream_key, dims, cuts, -0.22, 0.18) if cuts else 1.0
    entries = jax.random.normal(stream_key, dims, jnp.float32) * deviation * level
    return jnp.minimum(jnp.maximum(entries, -reach), reach).astype(kind)


def setup_inputs(seed: int = 0) -> dict:
    key_list = jax.random.split(jax.random.key(seed), 12)
    return {
        "tokens": normal_values(key_list[0], (TOKENS, D), 1.0, 6.0, ((0, 128),)),
        "gain_mix": jnp.clip(1.0 + 0.18 * jax.random.normal(key_list[1], (D,), jnp.float32), 0.099609375, 1.8984375).astype(jnp.bfloat16),
        "in_weight": normal_values(key_list[2], (D, 3, D), D ** -0.5, 0.15625, ((0, 16), (2, 8))),
        "conv_kernel": normal_values(key_list[3], (3, D), 3 ** -0.5, 3.5, ((1, 8),)),
        "out_weight": normal_values(key_list[4], (D, D), D ** -0.5, 0.15625, ((0, 8), (1, 16))),
        "gain_ffn": jnp.clip(1.0 + 0.18 * jax.random.normal(key_list[5], (D,), jnp.float32), 0.099609375, 1.8984375).astype(jnp.bfloat16),
        "gate_weight": normal_values(key_list[6], (D, FF), D ** -0.5, 0.15625, ((0, 16), (1, 8))),
        "up_weight": normal_values(key_list[7], (D, FF), D ** -0.5, 0.15625, ((0, 16), (1, 8))),
        "down_weight": normal_values(key_list[8], (FF, D), FF ** -0.5, 0.078125, ((0, 8), (1, 16))),
        "lengths": draw_lengths(jax.random.fold_in(key_list[11], 71), 0),
        "cotangent": normal_values(key_list[10], (TOKENS, D), 1.0, 6.0, ((0, 128),)),
    }


@jax.custom_vjp
def low(v):
    return lax.optimization_barrier(v.astype(jnp.bfloat16)).astype(jnp.float32)

@jax.custom_vjp
def low_back(v):
    return v

def low_keep(v):
    return (low(v), None)

def low_pass(kept, grad):
    return (grad,)

def back_keep(v):
    return (v, None)

def back_low(kept, grad):
    return (low(grad),)
low.defvjp(low_keep, low_pass)
low_back.defvjp(back_keep, back_low)
epsilon = 1e-05
highest = lax.Precision.HIGHEST

def delayed(values, steps):
    padded = jnp.pad(values, ((steps, 0), (0, 0)))
    return padded[:values.shape[0]]

def block_forward(token_rows_wide, gain_mix, in_weight, conv_kernel, out_weight, gain_ffn, gate_weight, up_weight, down_weight, live_mask):
    first_inverse_root = lax.rsqrt(lax.optimization_barrier(jnp.mean(token_rows_wide * token_rows_wide, axis=1, keepdims=True)) + epsilon)
    normalized_rows = low(token_rows_wide * first_inverse_root * gain_mix)
    projected = low_back(jnp.einsum('td,dkc->tkc', normalized_rows, in_weight, precision=highest))
    b_gate = projected[:, 0]
    c_gate = projected[:, 1]
    value_ch = projected[:, 2]
    bx_prod = b_gate * value_ch
    conv_sum = conv_kernel[0] * bx_prod + conv_kernel[1] * delayed(bx_prod, 1) + conv_kernel[2] * delayed(bx_prod, 2)
    mixed = low(c_gate * conv_sum)
    branch = low_back(jnp.dot(mixed, out_weight, precision=highest))
    residual_stream = token_rows_wide + branch
    second_inverse_root = lax.rsqrt(lax.optimization_barrier(jnp.mean(residual_stream * residual_stream, axis=1, keepdims=True)) + epsilon)
    second_normalized_rows = low(residual_stream * second_inverse_root * gain_ffn)
    gate_pre = low_back(jnp.dot(second_normalized_rows, gate_weight, precision=highest))
    up_pre = low_back(jnp.dot(second_normalized_rows, up_weight, precision=highest))
    hidden_act = low(jax.nn.silu(gate_pre) * up_pre)
    ffn_out = low_back(jnp.dot(hidden_act, down_weight, precision=highest))
    return live_mask[:, None] * (residual_stream + ffn_out)

def reference(tokens, gain_mix, in_weight, conv_kernel, out_weight, gain_ffn, gate_weight, up_weight, down_weight, lengths, cotangent):
    weights = tuple((item.astype(jnp.float32) for item in (gain_mix, in_weight, conv_kernel, out_weight, gain_ffn, gate_weight, up_weight, down_weight)))
    token_seqs = tokens.astype(jnp.float32).reshape(SEQS, SLOTS, D)
    cot_seqs = cotangent.astype(jnp.float32).reshape(SEQS, SLOTS, D)
    positions = jnp.arange(SLOTS).astype(jnp.int32)

    def one_sequence(totals, items):
        seq_tokens, seq_cot, seq_len = items
        live_mask = (positions < seq_len).astype(jnp.float32)

        def forward(token_in, *params):
            return block_forward(token_in, *params, live_mask)
        result, pullback = jax.vjp(forward, seq_tokens, *weights)
        grads = pullback(seq_cot)
        totals = tuple((first + second for first, second in zip(totals, grads[1:])))
        return (totals, (result, grads[0]))
    zeros = tuple((jnp.zeros(item.shape, jnp.float32) for item in weights))
    totals, (results, token_grads) = lax.scan(one_sequence, zeros, (token_seqs, cot_seqs, lengths))
    layer_out = results.reshape(TOKENS, D).astype(jnp.bfloat16)
    tokens_grad = token_grads.reshape(TOKENS, D).astype(jnp.bfloat16)
    return (layer_out, tokens_grad, totals[0], totals[1], totals[2], totals[3], totals[4], totals[5], totals[6], totals[7])
```

```python
import functools

import jax
import jax.numpy as jnp
from jax import lax
from jax.experimental import pallas as pl
from jax.experimental.pallas import tpu as pltpu
from jax.sharding import PartitionSpec as P

epsilon = 1e-05
MESH = pl.DeviceIdType.MESH
BF = jnp.bfloat16
F32 = jnp.float32
D = 1536
ROWS = 128
CH = 192
FB = 864
FP = 896
HALF = 48
VMEM_LIMIT = 60 << 20


class Place:
    def __init__(self):
        dp = lax.axis_index("dp")
        t = lax.axis_index("tensor")
        self.x, self.yh, self.c = dp // 4, (dp // 2) % 2, dp % 2
        self.z, self.yl = t // 2, t % 2
        self.y = self.yh * 2 + self.yl
        self.o = 1 - self.c
        self.xp, self.xm, self.x2 = (self.x + 1) % 4, (self.x + 3) % 4, (self.x + 2) % 4
        self.yp, self.ym = (self.y + 1) % 4, (self.y + 3) % 4
        self.yhp, self.yhm = self.yp // 2, self.ym // 2
        self.way = 1 - 2 * self.c
        self.zf = (self.z + self.way + 4) % 4
        self.zb = (self.z - self.way + 4) % 4
        self.zp, self.zm, self.z2 = (self.z + 1) % 4, (self.z + 3) % 4, (self.z + 2) % 4
        self.own = self.c == self.yl
        self.opp = self.c != self.yl

    def at(self, x=None, y=None, z=None, c=None):
        x = self.x if x is None else x
        y = self.y if y is None else y
        z = self.z if z is None else z
        c = self.c if c is None else c
        return (x * 4 + (y // 2) * 2 + c, z * 2 + y % 2)


class Net:
    def __init__(self, place, send, recv, local=None):
        self.p, self.ss, self.rs, self.ls = place, send, recv, local
        self.ns = self.nr = self.nl = 0
        self.pending = []

    def sem(self, n=1):
        k = self.nr
        self.nr += n
        return k

    def send(self, src, dst, recv_index, target, cond=None):
        k = self.ns
        self.ns += 1
        d = pltpu.make_async_remote_copy(
            src_ref=src, dst_ref=dst, send_sem=self.ss.at[k], recv_sem=self.rs.at[recv_index],
            device_id=target, device_id_type=MESH)
        run(cond, d.start)
        self.pending.append((cond, d))

    def copy(self, src, dst, cond=None):
        k = self.nl
        self.nl += 1
        d = pltpu.make_async_copy(src, dst, self.ls.at[k])
        run(cond, d.start)
        return lambda: run(cond, d.wait)

    def got(self, dst, recv_index, cond=None):
        d = pltpu.make_async_remote_copy(
            src_ref=dst, dst_ref=dst, send_sem=self.ss.at[0], recv_sem=self.rs.at[recv_index],
            device_id=self.p.at(c=self.p.o), device_id_type=MESH)
        run(cond, d.wait_recv)

    def finish(self):
        for cond, d in self.pending:
            run(cond, d.wait_send)
        self.pending = []


def run(cond, f):
    if cond is None:
        f()
    else:
        pl.when(cond)(f)


def greet(p, plane, ring):
    bar = pltpu.get_barrier_semaphore()
    who = [p.at(c=p.o)]
    if plane:
        for c in (0, 1):
            who += [p.at(x=p.xp, c=c), p.at(x=p.xm, c=c), p.at(y=p.yp, c=c), p.at(y=p.ym, c=c)]
    if ring:
        who += [p.at(z=p.zp), p.at(z=p.zm)]
    for w in who:
        pl.semaphore_signal(bar, inc=1, device_id=w, device_id_type=MESH)
    pl.semaphore_wait(bar, len(who))


def together(*jobs):
    jobs = list(jobs)
    while jobs:
        for j in list(jobs):
            try:
                next(j)
            except StopIteration:
                jobs.remove(j)


HA, HB = pl.ds(0, HALF), pl.ds(HALF, HALF)


def gather_plane(net, sh, W):
    p = net.p
    i_own, f1, f2, f3, f4 = net.sem(), net.sem(2), net.sem(2), net.sem(2), net.sem(2)
    r1, r2, r3, r4, y1, y2, y3, y4, x1, x2, x3, x4 = (net.sem() for _ in range(12))
    q = p.yl
    done = net.copy(sh, W.at[p.x, p.yh, p.c], p.own)
    net.send(sh.at[HA], W.at[p.x, p.yh, p.c, HA], f1 + p.c, p.at(x=p.xp, c=q))
    net.send(sh.at[HA], W.at[p.x, p.yh, p.c, HA], f2 + p.c, p.at(x=p.xm, c=q))
    net.send(sh.at[HB], W.at[p.x, p.yh, p.c, HB], f3 + p.c, p.at(y=p.yp, c=q))
    net.send(sh.at[HB], W.at[p.x, p.yh, p.c, HB], f4 + p.c, p.at(y=p.ym, c=q))
    net.send(sh, W.at[p.x, p.yh, p.c], i_own, p.at(c=p.o), p.opp)
    yield
    net.got(W.at[p.xm, p.yh, 0, HA], f1 + 0, p.own)
    net.got(W.at[p.x, p.yhm, 0, HB], f3 + 0, p.opp)
    net.send(W.at[p.xm, p.yh, 0, HA], W.at[p.xm, p.yh, 0, HA], r1, p.at(x=p.xp), p.own)
    net.send(W.at[p.x, p.yhm, 0, HB], W.at[p.x, p.yhm, 0, HB], r3, p.at(y=p.yp), p.opp)
    net.got(W.at[p.xp, p.yh, 1, HA], f2 + 1, p.own)
    net.got(W.at[p.x, p.yhp, 1, HB], f4 + 1, p.opp)
    net.send(W.at[p.xp, p.yh, 1, HA], W.at[p.xp, p.yh, 1, HA], r2, p.at(x=p.xm), p.own)
    net.send(W.at[p.x, p.yhp, 1, HB], W.at[p.x, p.yhp, 1, HB], r4, p.at(y=p.ym), p.opp)
    yield
    done()
    net.got(W.at[p.x, p.yh, p.o], i_own, p.own)
    net.got(W.at[p.xm, p.yh, 1, HA], f1 + 1, p.own)
    net.got(W.at[p.xp, p.yh, 0, HA], f2 + 0, p.own)
    net.got(W.at[p.x, p.yhm, 1, HB], f3 + 1, p.opp)
    net.got(W.at[p.x, p.yhp, 0, HB], f4 + 0, p.opp)
    net.got(W.at[p.x2, p.yh, 0, HA], r1, p.own)
    net.got(W.at[p.x2, p.yh, 1, HA], r2, p.own)
    net.send(W.at[:, p.yh, :, HA], W.at[:, p.yh, :, HA], y1, p.at(y=p.yp), p.own)
    net.send(W.at[:, p.yh, :, HA], W.at[:, p.yh, :, HA], y2, p.at(y=p.ym), p.own)
    net.got(W.at[p.x, 1 - p.yh, 0, HB], r3, p.own)
    net.got(W.at[p.x, 1 - p.yh, 1, HB], r4, p.own)
    net.send(W.at[p.x, :, :, HB], W.at[p.x, :, :, HB], x1, p.at(x=p.xp))
    net.send(W.at[p.x, :, :, HB], W.at[p.x, :, :, HB], x2, p.at(x=p.xm))
    yield
    net.got(W.at[:, p.yhm, :, HA], y1, p.opp)
    net.send(W.at[:, p.yhm, 0, HA], W.at[:, p.yhm, 0, HA], y3, p.at(y=p.yp), p.opp)
    net.got(W.at[:, p.yhp, :, HA], y2, p.opp)
    net.send(W.at[:, p.yhp, 1, HA], W.at[:, p.yhp, 1, HA], y4, p.at(y=p.ym), p.opp)
    net.got(W.at[p.xm, :, :, HB], x1)
    net.send(W.at[p.xm, :, 0, HB], W.at[p.xm, :, 0, HB], x3, p.at(x=p.xp))
    net.got(W.at[p.xp, :, :, HB], x2)
    net.send(W.at[p.xp, :, 1, HB], W.at[p.xp, :, 1, HB], x4, p.at(x=p.xm))
    yield
    net.got(W.at[:, 1 - p.yh, 0, HA], y3, p.own)
    net.got(W.at[:, 1 - p.yh, 1, HA], y4, p.own)
    net.got(W.at[p.x2, :, 0, HB], x3)
    net.got(W.at[p.x2, :, 1, HB], x4)


def add(out, *terms):
    lead = out.shape[:-2]
    count = 1
    for s in lead:
        count *= s

    def one(i):
        at = []
        for s in reversed(lead):
            at.append(i % s)
            i = i // s
        at = tuple(reversed(at))
        v = terms[0][at].astype(F32) if at else terms[0][...].astype(F32)
        for t in terms[1:]:
            v = v + (t[at] if at else t[...]).astype(F32)
        if at:
            out[at] = v.astype(out.dtype)
        else:
            out[...] = v.astype(out.dtype)

    if count == 1 and not lead:
        one(0)
    else:
        lax.fori_loop(0, count, lambda i, _: one(i), None)


def plane_scratch(n):
    return [
        pltpu.VMEM((2, 4, HALF, n), BF),
        pltpu.VMEM((2, 4, 2, HALF, n), BF),
        pltpu.VMEM((2, HALF, n), BF),
        pltpu.VMEM((3, HALF, n), BF),
        pltpu.VMEM((2, 2, HALF, n), BF),
        pltpu.VMEM((2, 2, 2, HALF, n), BF),
        pltpu.VMEM((2, HALF, n), BF),
        pltpu.VMEM((3, HALF, n), BF),
    ]


def reduce_plane(net, G, out, RA, RB, RC, F, RX, RY, RZ, H):
    p = net.p
    a0, a1, bp0, bp1, bm0, bm1, c0, c1, g0, g1, g2 = (net.sem() for _ in range(11))
    u0, u1, vp0, vp1, vm0, vm1, w0, w1, h0, h1, h2 = (net.sem() for _ in range(11))
    net.send(G.at[:, 1 - p.yh, 0, HA], RA.at[0], a0, p.at(y=p.ym), p.own)
    net.send(G.at[:, 1 - p.yh, 1, HA], RA.at[1], a1, p.at(y=p.yp), p.own)
    net.send(G.at[p.x2, :, 0, HB], RX.at[0], u0, p.at(x=p.xm))
    net.send(G.at[p.x2, :, 1, HB], RX.at[1], u1, p.at(x=p.xp))
    net.send(G.at[:, p.yhm, 1, HA], RB.at[0, :, 1], bp1, p.at(y=p.ym), p.opp)
    net.send(G.at[:, p.yhp, 0, HA], RB.at[1, :, 0], bm0, p.at(y=p.yp), p.opp)
    net.send(G.at[p.xm, :, 1, HB], RY.at[0, :, 1], vp1, p.at(x=p.xm))
    net.send(G.at[p.xp, :, 0, HB], RY.at[1, :, 0], vm0, p.at(x=p.xp))
    yield

    net.got(RA.at[0], a0, p.opp)
    net.got(RA.at[1], a1, p.opp)

    @pl.when(p.opp)
    def _():
        add(RA.at[0], RA.at[0], G.at[:, p.yhm, 0, HA])
        add(RA.at[1], RA.at[1], G.at[:, p.yhp, 1, HA])

    net.send(RA.at[0], RB.at[0, :, 0], bp0, p.at(y=p.ym), p.opp)
    net.send(RA.at[1], RB.at[1, :, 1], bm1, p.at(y=p.yp), p.opp)
    net.got(RX.at[0], u0)
    add(RX.at[0], RX.at[0], G.at[p.xm, :, 0, HB])
    net.send(RX.at[0], RY.at[0, :, 0], vp0, p.at(x=p.xm))
    net.got(RX.at[1], u1)
    add(RX.at[1], RX.at[1], G.at[p.xp, :, 1, HB])
    net.send(RX.at[1], RY.at[1, :, 1], vm1, p.at(x=p.xp))
    yield

    net.got(RB.at[0, :, 1], bp1, p.own)
    net.got(RB.at[1, :, 0], bm0, p.own)
    net.got(RB.at[0, :, 0], bp0, p.own)
    net.got(RB.at[1, :, 1], bm1, p.own)

    @pl.when(p.own)
    def _():
        add(RB.at[0], RB.at[0], RB.at[1], G.at[:, p.yh, :, HA])

    S = RB.at[0]
    net.send(S.at[p.x2, 0], RC.at[0], c0, p.at(x=p.xm), p.own)
    net.send(S.at[p.x2, 1], RC.at[1], c1, p.at(x=p.xp), p.own)
    net.send(S.at[p.xm, 1], F.at[1], g1, p.at(x=p.xm, c=1), p.own)
    net.send(S.at[p.xp, 0], F.at[2], g2, p.at(x=p.xp, c=0), p.own)
    net.send(S.at[p.x, p.o], F.at[0], g0, p.at(c=p.o), p.own)

    net.got(RY.at[0, :, 1], vp1)
    net.got(RY.at[1, :, 0], vm0)
    net.got(RY.at[0, :, 0], vp0)
    net.got(RY.at[1, :, 1], vm1)
    add(RY.at[0], RY.at[0], RY.at[1], G.at[p.x, :, :, HB])
    T = RY.at[0]
    net.send(T.at[1 - p.yh, 0], RZ.at[0], w0, p.at(y=p.ym), p.own)
    net.send(T.at[1 - p.yh, 1], RZ.at[1], w1, p.at(y=p.yp), p.own)
    net.send(T.at[p.yhm, 1], H.at[1], h1, p.at(y=p.ym, c=1), p.opp)
    net.send(T.at[p.yhp, 0], H.at[2], h2, p.at(y=p.yp, c=0), p.opp)
    net.send(T.at[p.yh, p.o], H.at[0], h0, p.at(c=p.o), p.own)
    yield

    net.got(RC.at[0], c0, p.own)
    net.got(RC.at[1], c1, p.own)
    net.got(RZ.at[0], w0, p.opp)
    net.got(RZ.at[1], w1, p.opp)

    @pl.when(p.own)
    def _():
        add(RC.at[0], RC.at[0], S.at[p.xm, 0])
        add(RC.at[1], RC.at[1], S.at[p.xp, 1])

    @pl.when(p.opp)
    def _():
        add(RZ.at[0], RZ.at[0], T.at[p.yhm, 0])
        add(RZ.at[1], RZ.at[1], T.at[p.yhp, 1])

    net.send(RC.at[0], F.at[1], g1, p.at(x=p.xm, c=0), p.own)
    net.send(RC.at[1], F.at[2], g2, p.at(x=p.xp, c=1), p.own)
    net.send(RZ.at[0], H.at[1], h1, p.at(y=p.ym, c=0), p.opp)
    net.send(RZ.at[1], H.at[2], h2, p.at(y=p.yp, c=1), p.opp)
    yield

    net.got(F.at[0], g0, p.opp)
    net.got(F.at[1], g1)
    net.got(F.at[2], g2)
    net.got(H.at[0], h0, p.opp)
    net.got(H.at[1], h1)
    net.got(H.at[2], h2)

    @pl.when(p.own)
    def _():
        F[0] = S[p.x, p.c]
        H[0] = T[p.yh, p.c]

    add(out.at[HA], F.at[0], F.at[1], F.at[2])
    add(out.at[HB], H.at[0], H.at[1], H.at[2])


def gather_ring(net, a, out):
    p = net.p
    s1, s3, s2 = net.sem(), net.sem(), net.sem()
    k = net.sem(4)
    done = net.copy(a, out.at[p.c, p.z])
    net.send(a, out.at[p.c, p.z], s1, p.at(z=p.zf))
    net.send(a, out.at[p.c, p.z], s3, p.at(z=p.zb))
    net.send(a, out.at[p.c, p.z], k + 0, p.at(c=p.o))
    yield
    net.got(out.at[p.c, p.zb], s1)
    net.send(out.at[p.c, p.zb], out.at[p.c, p.zb], s2, p.at(z=p.zf))
    net.send(out.at[p.c, p.zb], out.at[p.c, p.zb], k + (p.zb - p.z + 4) % 4, p.at(c=p.o))
    net.got(out.at[p.c, p.zf], s3)
    net.send(out.at[p.c, p.zf], out.at[p.c, p.zf], k + (p.zf - p.z + 4) % 4, p.at(c=p.o))
    yield
    net.got(out.at[p.c, p.z2], s2)
    net.send(out.at[p.c, p.z2], out.at[p.c, p.z2], k + 2, p.at(c=p.o))
    yield
    done()
    for j in range(4):
        net.got(out.at[p.o, (p.z + j) % 4], k + j)


def ring_scratch(n):
    return [pltpu.VMEM((4, ROWS, n), BF), pltpu.VMEM((2, ROWS, n), BF), pltpu.VMEM((3, ROWS, n), BF)]


def reduce_ring(net, V, out, RC, SB, RZ):
    p = net.p
    s2, sd, sr = net.sem(), net.sem(), net.sem()
    k = net.sem(4)
    for j in (2, 1, 3, 0):
        zj = (p.z + j) % 4
        net.send(V.at[p.o, zj], RC.at[j], k + j, p.at(c=p.o))
    yield
    jf, jb = (p.zf - p.z + 4) % 4, (p.zb - p.z + 4) % 4
    net.got(RC.at[2], k + 2)
    add(SB.at[0], V.at[p.c, p.z2], RC.at[2])
    net.send(SB.at[0], RZ.at[0], s2, p.at(z=p.zf))
    net.got(RC.at[jb], k + jb)
    add(SB.at[1], V.at[p.c, p.zb], RC.at[jb])
    net.send(SB.at[1], RZ.at[1], sd, p.at(z=p.zb))
    net.got(RC.at[jf], k + jf)
    add(RC.at[jf], V.at[p.c, p.zf], RC.at[jf])
    yield
    net.got(RZ.at[0], s2)
    add(RC.at[jf], RC.at[jf], RZ.at[0])
    net.send(RC.at[jf], RZ.at[2], sr, p.at(z=p.zf))
    net.got(RC.at[0], k + 0)
    add(RC.at[0], V.at[p.c, p.z], RC.at[0])
    yield
    net.got(RZ.at[1], sd)
    net.got(RZ.at[2], sr)
    add(out, RC.at[0], RZ.at[1], RZ.at[2])


def shape(s, t=BF):
    return jax.ShapeDtypeStruct(s, t)


def slots(n):
    return shape((4, 2, 2, 96, n))


def blocks(n):
    return shape((2, 4, ROWS, n))


def exchange(name, number, gathers=(), rings=(), ring_sums=(), plane_sums=()):
    ng, nz, ns, nq = len(gathers), len(rings), len(ring_sums), len(plane_sums)

    def kernel(*refs):
        refs = list(refs)

        def take(n):
            part, refs[:] = refs[:n], refs[n:]
            return part

        a, b, d, e = take(ng), take(nz), take(ns), take(nq)
        ao, bo, do, eo = take(ng), take(nz), take(ns), take(nq)
        ds = [take(3) for _ in range(ns)]
        es = [take(8) for _ in range(nq)]
        send, recv, local = refs
        p = Place()
        greet(p, bool(ng + nq), bool(nz + ns))
        net = Net(p, send, recv, local)
        jobs = [reduce_ring(net, v, o, *s) for v, o, s in zip(d, do, ds)]
        jobs += [gather_ring(net, v, o) for v, o in zip(b, bo)]
        jobs += [gather_plane(net, v, o) for v, o in zip(a, ao)]
        jobs += [reduce_plane(net, v, o, *s) for v, o, s in zip(e, eo, es)]
        together(*jobs)
        net.finish()

    any_, vm = pl.BlockSpec(memory_space=pl.ANY), pl.BlockSpec(memory_space=pltpu.VMEM)
    scratch = []
    for v in ring_sums:
        scratch += ring_scratch(v.shape[-1])
    for v in plane_sums:
        scratch += plane_scratch(v.shape[-1])
    count = 24 * (ng + nq) + 12 * (nz + ns)
    scratch += [pltpu.SemaphoreType.DMA((count,))] * 2 + [pltpu.SemaphoreType.DMA((ng + nz + 1,))]
    outs = [slots(v.shape[-1]) for v in gathers] + [blocks(v.shape[-1]) for v in rings]
    outs += [shape((ROWS, v.shape[-1]), F32) for v in ring_sums]
    outs += [shape((96, v.shape[-1]), F32) for v in plane_sums]
    return pl.pallas_call(
        kernel,
        out_shape=tuple(outs),
        in_specs=[any_] * (ng + nz) + [vm] * (ns + nq),
        out_specs=tuple([any_] * (ng + nz) + [vm] * (ns + nq)),
        scratch_shapes=scratch,
        compiler_params=pltpu.CompilerParams(
            collective_id=number, has_side_effects=True, vmem_limit_bytes=VMEM_LIMIT),
        name=name,
    )(*gathers, *rings, *ring_sums, *plane_sums)


def norm_backward_rule(gradient_of_normalized, centered_input, inverse_root, gain_widened):
    weighted_rows = gain_widened * gradient_of_normalized
    return inverse_root * (
        weighted_rows
        - centered_input * jnp.mean(weighted_rows * centered_input, axis=1, keepdims=True)
    )


SWAP = [(t, t ^ 1) for t in range(8)]


def matmul(a, b, dims, out=F32):
    return lax.dot_general(a, b, (dims, ((), ())), preferred_element_type=F32).astype(out)


def per_device(tokens, gain_mix, in_weight, conv_kernel, out_weight, gain_ffn, gate_weight, up_weight, down_weight, lengths, cotangent):
    dp, t = lax.axis_index("dp"), lax.axis_index("tensor")
    z, yl, c = t // 2, t % 2, dp % 2
    position = t * ROWS + jnp.arange(ROWS)
    live = (position < lengths[0]).astype(F32)[:, None]

    conv_pack = jnp.concatenate([in_weight.reshape(96, 3 * CH), out_weight.T], axis=1)
    wide = lambda w: jnp.pad(w, ((0, 0), (0, FP - FB)))
    gate_pack, up_pack, down_pack = wide(gate_weight), wide(up_weight), wide(down_weight.T)
    small = jnp.zeros((16, 256), BF)
    off = (96 * dp) % 128
    small = lax.dynamic_update_slice(small, jnp.stack([gain_mix, gain_ffn]), (0, off))
    small = lax.dynamic_update_slice(small, conv_kernel, (2, 0))
    small = jnp.concatenate([small] * 6, axis=0)
    grad_out = (live * cotangent.astype(F32)).astype(BF)

    wc, wg, ws, tok_all, gout_all = exchange(
        "first", 0, gathers=(conv_pack, gate_pack, small), rings=(tokens, grad_out)
    )
    pieces = ws[:, :, :, :16].reshape(16, 16, 256)
    at = [(96 * s) % 128 for s in range(16)]
    gains = jnp.concatenate([pieces[s, :2, at[s] : at[s] + 96] for s in range(16)], axis=1).astype(F32)
    g_mix, g_ffn = gains[0], gains[1]
    taps = pieces[0, 2:5, :CH].astype(F32)

    tok_f = tok_all.reshape(1024, D).astype(F32)
    inv1_all = lax.rsqrt(jnp.mean(tok_f * tok_f, axis=1, keepdims=True) + epsilon)
    normed_all = (tok_f * inv1_all * g_mix).astype(BF)
    wc = wc.reshape(D, 768)
    w_in, w_out_t = wc[:, : 3 * CH], wc[:, 3 * CH :]
    projected = matmul(normed_all, w_in, ((1,), (0,)))
    b_gate, c_gate, value = projected[:, :CH], projected[:, CH : 2 * CH], projected[:, 2 * CH :]
    bx = b_gate * value
    bx4 = bx.reshape(2, 4, ROWS, CH)
    halo = lax.ppermute(bx4[:, :, ROWS - 2 :], "tensor", SWAP)
    shifted = jnp.pad(halo, ((0, 0), (1, 0), (0, 0), (0, 0)))[:, :4]
    halo = jnp.where(yl == 1, halo, shifted)
    ext = jnp.concatenate([halo, bx4], axis=2)
    bx_one = ext[:, :, 1:-1].reshape(1024, CH)
    bx_two = ext[:, :, :-2].reshape(1024, CH)
    conv_sum = taps[0] * bx + taps[1] * bx_one + taps[2] * bx_two
    mixed = (c_gate * conv_sum).astype(BF)
    mixer_part = matmul(mixed, w_out_t, ((1,), (1,)), BF)

    wu, mixer_rows = exchange(
        "second", 1, gathers=(up_pack,), ring_sums=(mixer_part.reshape(2, 4, ROWS, D),)
    )
    tok = tokens.astype(F32)
    resid = tok + mixer_rows
    inv2 = lax.rsqrt(jnp.mean(resid * resid, axis=1, keepdims=True) + epsilon)
    xhat2 = resid * inv2
    normed2 = (xhat2 * g_ffn).astype(BF)
    wd, normed2_all = exchange("third", 2, gathers=(down_pack,), rings=(normed2,))
    normed2_all = normed2_all.reshape(1024, D)
    w_gate, w_up, w_down_t = wg.reshape(D, FP), wu.reshape(D, FP), wd.reshape(D, FP)
    gout_all = gout_all.reshape(1024, D)

    gate_pre = matmul(normed2_all, w_gate, ((1,), (0,)))
    up_pre = matmul(normed2_all, w_up, ((1,), (0,)))
    sig = jax.nn.sigmoid(gate_pre)
    silu = gate_pre * sig
    hidden = (silu * up_pre).astype(BF)
    ffn_part = matmul(hidden, w_down_t, ((1,), (1,)), BF)
    grad_act = matmul(gout_all, w_down_t, ((1,), (0,)))
    grad_gate = (grad_act * up_pre * sig * (1.0 + gate_pre * (1.0 - sig))).astype(BF)
    grad_up = (grad_act * silu).astype(BF)
    gn2 = matmul(grad_gate, w_gate, ((1,), (1,))) + matmul(grad_up, w_up, ((1,), (1,)))
    gn2 = gn2.astype(BF)
    gate_full = matmul(normed2_all, grad_gate, ((0,), (0,)), BF)
    up_full = matmul(normed2_all, grad_up, ((0,), (0,)), BF)
    down_full = matmul(gout_all, hidden, ((0,), (0,)), BF)

    as_slots = lambda v: v.reshape(4, 2, 2, 96, v.shape[-1])
    gn2_rows, gate_sum = exchange(
        "fourth", 3, ring_sums=(gn2.reshape(2, 4, ROWS, D),), plane_sums=(as_slots(gate_full),)
    )
    grad_resid = grad_out.astype(F32) + norm_backward_rule(gn2_rows, xhat2, inv2, g_ffn)
    branch_all, up_sum = exchange(
        "fifth", 4, rings=(grad_resid.astype(BF),), plane_sums=(as_slots(up_full),)
    )
    branch_all = branch_all.reshape(1024, D)
    out_full = matmul(branch_all, mixed, ((0,), (0,)), BF)
    grad_mixed = matmul(branch_all, w_out_t, ((1,), (0,)))
    grad_c = grad_mixed * conv_sum
    grad_conv = grad_mixed * c_gate
    gc4 = grad_conv.reshape(2, 4, ROWS, CH)
    ahead = lax.ppermute(gc4[:, :, :2], "tensor", SWAP)
    shifted = jnp.pad(ahead, ((0, 0), (0, 1), (0, 0), (0, 0)))[:, 1:]
    ahead = jnp.where(yl == 0, ahead, shifted)
    ext = jnp.concatenate([gc4, ahead], axis=2)
    grad_bx = (
        taps[0] * grad_conv
        + taps[1] * ext[:, :, 1:-1].reshape(1024, CH)
        + taps[2] * ext[:, :, 2:].reshape(1024, CH)
    )
    kernel_part = jnp.stack(
        [jnp.sum(grad_conv * bx, 0), jnp.sum(grad_conv * bx_one, 0), jnp.sum(grad_conv * bx_two, 0)]
    )
    grad_projected = jnp.concatenate([grad_bx * value, grad_c, grad_bx * b_gate], axis=1).astype(BF)
    in_full = matmul(normed_all, grad_projected, ((0,), (0,)), BF)
    gn1 = matmul(grad_projected, w_in, ((1,), (1,)), BF)
    conv_full = jnp.concatenate([in_full, out_full], axis=1)
    taps_at = jnp.pad(kernel_part.T.reshape(16, 12, 3), ((0, 0), (0, 84), (0, 0))).astype(BF)
    down_full = lax.dynamic_update_slice(down_full, taps_at.reshape(D, 3), (0, FB))
    gn1_rows, ffn_rows, down_sum, conv_sums = exchange(
        "sixth",
        5,
        ring_sums=(gn1.reshape(2, 4, ROWS, D), ffn_part.reshape(2, 4, ROWS, D)),
        plane_sums=(as_slots(down_full), as_slots(conv_full)),
    )
    layer_out = (live * (resid + ffn_rows)).astype(BF)
    inv1 = lax.rsqrt(jnp.mean(tok * tok, axis=1, keepdims=True) + epsilon)
    tokens_grad = (grad_resid + norm_backward_rule(gn1_rows, tok * inv1, inv1, g_mix)).astype(BF)

    in_grad = conv_sums[:, : 3 * CH].reshape(96, 3, CH)
    out_grad = conv_sums[:, 3 * CH :].T
    gate_grad, up_grad = gate_sum[:, :FB], up_sum[:, :FB]
    down_grad = down_sum[:, :FB].T
    mix_share = jnp.sum(in_grad * in_weight.astype(F32), axis=(1, 2)) / gain_mix.astype(F32)
    ffn_share = jnp.sum(
        gate_grad * gate_weight.astype(F32) + up_grad * up_weight.astype(F32), axis=1
    ) / gain_ffn.astype(F32)
    shares = lax.psum_scatter(
        jnp.stack([mix_share, ffn_share]).reshape(2, 8, 12), "tensor", scatter_dimension=1
    )
    move = [(i, (i % 8) * 16 + i // 8) for i in range(128)]
    kernel_grad = lax.ppermute(down_sum[:12, FB : FB + 3].T, ("dp", "tensor"), move)
    return (
        layer_out,
        tokens_grad,
        shares[0],
        in_grad,
        kernel_grad,
        out_grad,
        shares[1],
        gate_grad,
        up_grad,
        down_grad,
    )


def solution(mesh):
    placed = (
        P(("dp", "tensor"), None),
        P("dp"),
        P("dp", None, "tensor"),
        P(None, "tensor"),
        P("tensor", "dp"),
        P("dp"),
        P("dp", "tensor"),
        P("dp", "tensor"),
        P("tensor", "dp"),
        P("dp"),
        P(("dp", "tensor"), None),
    )
    return jax.shard_map(
        per_device,
        mesh=mesh,
        in_specs=placed,
        out_specs=(
            P(("dp", "tensor"), None),
            P(("dp", "tensor"), None),
            P(("dp", "tensor")),
            P("dp", None, "tensor"),
            P(None, ("dp", "tensor")),
            P("tensor", "dp"),
            P(("dp", "tensor")),
            P("dp", "tensor"),
            P("dp", "tensor"),
            P("tensor", "dp"),
        ),
        check_vma=False,
    )
```

```python
import functools

import jax
import jax.numpy as jnp
from jax import lax
from jax.experimental import pallas as pl
from jax.experimental.pallas import tpu as pltpu
from jax.sharding import PartitionSpec as P

epsilon = 1e-05
MESH = pl.DeviceIdType.MESH
BF = jnp.bfloat16
F32 = jnp.float32
D = 1536
ROWS = 128
CH = 192
FB = 864
FP = 896
HALF = 48
VMEM_LIMIT = 60 << 20


class Place:
    def __init__(self):
        dp = lax.axis_index("dp")
        t = lax.axis_index("tensor")
        self.x, self.yh, self.c = dp // 4, (dp // 2) % 2, dp % 2
        self.z, self.yl = t // 2, t % 2
        self.y = self.yh * 2 + self.yl
        self.o = 1 - self.c
        self.xp, self.xm, self.x2 = (self.x + 1) % 4, (self.x + 3) % 4, (self.x + 2) % 4
        self.yp, self.ym = (self.y + 1) % 4, (self.y + 3) % 4
        self.yhp, self.yhm = self.yp // 2, self.ym // 2
        self.way = 1 - 2 * self.c
        self.zf = (self.z + self.way + 4) % 4
        self.zb = (self.z - self.way + 4) % 4
        self.zp, self.zm, self.z2 = (self.z + 1) % 4, (self.z + 3) % 4, (self.z + 2) % 4
        self.own = self.c == self.yl
        self.opp = self.c != self.yl

    def at(self, x=None, y=None, z=None, c=None):
        x = self.x if x is None else x
        y = self.y if y is None else y
        z = self.z if z is None else z
        c = self.c if c is None else c
        return (x * 4 + (y // 2) * 2 + c, z * 2 + y % 2)


class Net:
    def __init__(self, place, send, recv, local=None):
        self.p, self.ss, self.rs, self.ls = place, send, recv, local
        self.ns = self.nr = self.nl = 0
        self.pending = []

    def sem(self, n=1):
        k = self.nr
        self.nr += n
        return k

    def send(self, src, dst, recv_index, target, cond=None):
        k = self.ns
        self.ns += 1
        d = pltpu.make_async_remote_copy(
            src_ref=src, dst_ref=dst, send_sem=self.ss.at[k], recv_sem=self.rs.at[recv_index],
            device_id=target, device_id_type=MESH)
        run(cond, d.start)
        self.pending.append((cond, d))

    def copy(self, src, dst, cond=None):
        k = self.nl
        self.nl += 1
        d = pltpu.make_async_copy(src, dst, self.ls.at[k])
        run(cond, d.start)
        return lambda: run(cond, d.wait)

    def got(self, dst, recv_index, cond=None):
        d = pltpu.make_async_remote_copy(
            src_ref=dst, dst_ref=dst, send_sem=self.ss.at[0], recv_sem=self.rs.at[recv_index],
            device_id=self.p.at(c=self.p.o), device_id_type=MESH)
        run(cond, d.wait_recv)

    def finish(self):
        for cond, d in self.pending:
            run(cond, d.wait_send)
        self.pending = []


def run(cond, f):
    if cond is None:
        f()
    else:
        pl.when(cond)(f)


def greet(p, plane, ring):
    bar = pltpu.get_barrier_semaphore()
    who = [p.at(c=p.o)]
    if plane:
        for c in (0, 1):
            who += [p.at(x=p.xp, c=c), p.at(x=p.xm, c=c), p.at(y=p.yp, c=c), p.at(y=p.ym, c=c)]
    if ring:
        who += [p.at(z=p.zp), p.at(z=p.zm)]
    for w in who:
        pl.semaphore_signal(bar, inc=1, device_id=w, device_id_type=MESH)
    pl.semaphore_wait(bar, len(who))


def together(*jobs):
    jobs = list(jobs)
    while jobs:
        for j in list(jobs):
            try:
                next(j)
            except StopIteration:
                jobs.remove(j)


HA, HB = pl.ds(0, HALF), pl.ds(HALF, HALF)


def add(out, *terms):
    lead = out.shape[:-2]
    count = 1
    for s in lead:
        count *= s

    def one(i):
        at = []
        for s in reversed(lead):
            at.append(i % s)
            i = i // s
        at = tuple(reversed(at))
        v = terms[0][at].astype(F32) if at else terms[0][...].astype(F32)
        for t in terms[1:]:
            v = v + (t[at] if at else t[...]).astype(F32)
        if at:
            out[at] = v.astype(out.dtype)
        else:
            out[...] = v.astype(out.dtype)

    if not lead:

        def rows(i, _):
            at = pl.ds(pl.multiple_of(i * 16, 16), 16)
            v = terms[0][at].astype(F32)
            for t in terms[1:]:
                v = v + t[at].astype(F32)
            out[at] = v.astype(out.dtype)

        lax.fori_loop(0, out.shape[0] // 16, rows, None)
    else:
        lax.fori_loop(0, count, lambda i, _: one(i), None)


def plane_scratch(n):
    return [
        pltpu.VMEM((2, 4, HALF, n), BF),
        pltpu.VMEM((2, 4, 2, HALF, n), BF),
        pltpu.VMEM((2, HALF, n), BF),
        pltpu.VMEM((3, HALF, n), BF),
        pltpu.VMEM((2, 2, HALF, n), BF),
        pltpu.VMEM((2, 2, 2, HALF, n), BF),
        pltpu.VMEM((2, HALF, n), BF),
        pltpu.VMEM((3, HALF, n), BF),
    ]


def reduce_plane(net, G, out, RA, RB, RC, F, RX, RY, RZ, H):
    p = net.p
    a0, a1, bp0, bp1, bm0, bm1, c0, c1, g0, g1, g2 = (net.sem() for _ in range(11))
    u0, u1, vp0, vp1, vm0, vm1, w0, w1, h0, h1, h2 = (net.sem() for _ in range(11))
    net.send(G.at[:, 1 - p.yh, 0, HA], RA.at[0], a0, p.at(y=p.ym), p.own)
    net.send(G.at[:, 1 - p.yh, 1, HA], RA.at[1], a1, p.at(y=p.yp), p.own)
    net.send(G.at[p.x2, :, 0, HB], RX.at[0], u0, p.at(x=p.xm))
    net.send(G.at[p.x2, :, 1, HB], RX.at[1], u1, p.at(x=p.xp))
    net.send(G.at[:, p.yhm, 1, HA], RB.at[0, :, 1], bp1, p.at(y=p.ym), p.opp)
    net.send(G.at[:, p.yhp, 0, HA], RB.at[1, :, 0], bm0, p.at(y=p.yp), p.opp)
    net.send(G.at[p.xm, :, 1, HB], RY.at[0, :, 1], vp1, p.at(x=p.xm))
    net.send(G.at[p.xp, :, 0, HB], RY.at[1, :, 0], vm0, p.at(x=p.xp))
    yield

    net.got(RA.at[0], a0, p.opp)
    net.got(RA.at[1], a1, p.opp)

    @pl.when(p.opp)
    def _():
        add(RA.at[0], RA.at[0], G.at[:, p.yhm, 0, HA])
        add(RA.at[1], RA.at[1], G.at[:, p.yhp, 1, HA])

    net.send(RA.at[0], RB.at[0, :, 0], bp0, p.at(y=p.ym), p.opp)
    net.send(RA.at[1], RB.at[1, :, 1], bm1, p.at(y=p.yp), p.opp)
    net.got(RX.at[0], u0)
    add(RX.at[0], RX.at[0], G.at[p.xm, :, 0, HB])
    net.send(RX.at[0], RY.at[0, :, 0], vp0, p.at(x=p.xm))
    net.got(RX.at[1], u1)
    add(RX.at[1], RX.at[1], G.at[p.xp, :, 1, HB])
    net.send(RX.at[1], RY.at[1, :, 1], vm1, p.at(x=p.xp))
    yield

    net.got(RB.at[0, :, 1], bp1, p.own)
    net.got(RB.at[1, :, 0], bm0, p.own)
    net.got(RB.at[0, :, 0], bp0, p.own)
    net.got(RB.at[1, :, 1], bm1, p.own)

    @pl.when(p.own)
    def _():
        add(RB.at[0], RB.at[0], RB.at[1], G.at[:, p.yh, :, HA])

    S = RB.at[0]
    net.send(S.at[p.x2, 0], RC.at[0], c0, p.at(x=p.xm), p.own)
    net.send(S.at[p.x2, 1], RC.at[1], c1, p.at(x=p.xp), p.own)
    net.send(S.at[p.xm, 1], F.at[1], g1, p.at(x=p.xm, c=1), p.own)
    net.send(S.at[p.xp, 0], F.at[2], g2, p.at(x=p.xp, c=0), p.own)
    net.send(S.at[p.x, p.o], F.at[0], g0, p.at(c=p.o), p.own)

    net.got(RY.at[0, :, 1], vp1)
    net.got(RY.at[1, :, 0], vm0)
    net.got(RY.at[0, :, 0], vp0)
    net.got(RY.at[1, :, 1], vm1)
    add(RY.at[0], RY.at[0], RY.at[1], G.at[p.x, :, :, HB])
    T = RY.at[0]
    net.send(T.at[1 - p.yh, 0], RZ.at[0], w0, p.at(y=p.ym), p.own)
    net.send(T.at[1 - p.yh, 1], RZ.at[1], w1, p.at(y=p.yp), p.own)
    net.send(T.at[p.yhm, 1], H.at[1], h1, p.at(y=p.ym, c=1), p.opp)
    net.send(T.at[p.yhp, 0], H.at[2], h2, p.at(y=p.yp, c=0), p.opp)
    net.send(T.at[p.yh, p.o], H.at[0], h0, p.at(c=p.o), p.own)
    yield

    net.got(RC.at[0], c0, p.own)
    net.got(RC.at[1], c1, p.own)
    net.got(RZ.at[0], w0, p.opp)
    net.got(RZ.at[1], w1, p.opp)

    @pl.when(p.own)
    def _():
        add(RC.at[0], RC.at[0], S.at[p.xm, 0])
        add(RC.at[1], RC.at[1], S.at[p.xp, 1])

    @pl.when(p.opp)
    def _():
        add(RZ.at[0], RZ.at[0], T.at[p.yhm, 0])
        add(RZ.at[1], RZ.at[1], T.at[p.yhp, 1])

    net.send(RC.at[0], F.at[1], g1, p.at(x=p.xm, c=0), p.own)
    net.send(RC.at[1], F.at[2], g2, p.at(x=p.xp, c=1), p.own)
    net.send(RZ.at[0], H.at[1], h1, p.at(y=p.ym, c=0), p.opp)
    net.send(RZ.at[1], H.at[2], h2, p.at(y=p.yp, c=1), p.opp)
    yield

    net.got(F.at[0], g0, p.opp)
    net.got(F.at[1], g1)
    net.got(F.at[2], g2)
    net.got(H.at[0], h0, p.opp)
    net.got(H.at[1], h1)
    net.got(H.at[2], h2)

    @pl.when(p.own)
    def _():
        F[0] = S[p.x, p.c]
        H[0] = T[p.yh, p.c]

    add(out.at[HA], F.at[0], F.at[1], F.at[2])
    add(out.at[HB], H.at[0], H.at[1], H.at[2])


def ring_scratch(n):
    return [pltpu.VMEM((4, ROWS, n), BF), pltpu.VMEM((2, ROWS, n), BF), pltpu.VMEM((3, ROWS, n), BF)]


def shape(s, t=BF):
    return jax.ShapeDtypeStruct(s, t)


def slots(n):
    return shape((4, 2, 2, 96, n))


def blocks(n):
    return shape((4, 2, ROWS, n))


def gather_plane(net, sh, W):
    p = net.p
    h = sh.shape[0] // 2
    HA, HB = pl.ds(0, h), pl.ds(h, h)
    i_own, f1, f2, f3, f4 = net.sem(), net.sem(2), net.sem(2), net.sem(2), net.sem(2)
    r1, r2, r3, r4, y1, y2, y3, y4, x1, x2, x3, x4 = (net.sem() for _ in range(12))
    q = p.yl
    done = net.copy(sh, W.at[p.x, p.yh, p.c], p.own)
    net.send(sh.at[HA], W.at[p.x, p.yh, p.c, HA], f1 + p.c, p.at(x=p.xp, c=q))
    net.send(sh.at[HA], W.at[p.x, p.yh, p.c, HA], f2 + p.c, p.at(x=p.xm, c=q))
    net.send(sh.at[HB], W.at[p.x, p.yh, p.c, HB], f3 + p.c, p.at(y=p.yp, c=q))
    net.send(sh.at[HB], W.at[p.x, p.yh, p.c, HB], f4 + p.c, p.at(y=p.ym, c=q))
    net.send(sh, W.at[p.x, p.yh, p.c], i_own, p.at(c=p.o), p.opp)
    yield
    net.got(W.at[p.xm, p.yh, 0, HA], f1 + 0, p.own)
    net.got(W.at[p.x, p.yhm, 0, HB], f3 + 0, p.opp)
    net.send(W.at[p.xm, p.yh, 0, HA], W.at[p.xm, p.yh, 0, HA], r1, p.at(x=p.xp), p.own)
    net.send(W.at[p.x, p.yhm, 0, HB], W.at[p.x, p.yhm, 0, HB], r3, p.at(y=p.yp), p.opp)
    net.got(W.at[p.xp, p.yh, 1, HA], f2 + 1, p.own)
    net.got(W.at[p.x, p.yhp, 1, HB], f4 + 1, p.opp)
    net.send(W.at[p.xp, p.yh, 1, HA], W.at[p.xp, p.yh, 1, HA], r2, p.at(x=p.xm), p.own)
    net.send(W.at[p.x, p.yhp, 1, HB], W.at[p.x, p.yhp, 1, HB], r4, p.at(y=p.ym), p.opp)
    yield
    done()
    net.got(W.at[p.x, p.yh, p.o], i_own, p.own)
    net.got(W.at[p.xm, p.yh, 1, HA], f1 + 1, p.own)
    net.got(W.at[p.xp, p.yh, 0, HA], f2 + 0, p.own)
    net.got(W.at[p.x, p.yhm, 1, HB], f3 + 1, p.opp)
    net.got(W.at[p.x, p.yhp, 0, HB], f4 + 0, p.opp)
    net.got(W.at[p.x2, p.yh, 0, HA], r1, p.own)
    net.got(W.at[p.x2, p.yh, 1, HA], r2, p.own)
    net.send(W.at[:, p.yh, :, HA], W.at[:, p.yh, :, HA], y1, p.at(y=p.yp), p.own)
    net.send(W.at[:, p.yh, :, HA], W.at[:, p.yh, :, HA], y2, p.at(y=p.ym), p.own)
    net.got(W.at[p.x, 1 - p.yh, 0, HB], r3, p.own)
    net.got(W.at[p.x, 1 - p.yh, 1, HB], r4, p.own)
    net.send(W.at[p.x, :, :, HB], W.at[p.x, :, :, HB], x1, p.at(x=p.xp))
    net.send(W.at[p.x, :, :, HB], W.at[p.x, :, :, HB], x2, p.at(x=p.xm))
    yield
    net.got(W.at[p.xm, :, :, HB], x1)
    net.send(W.at[p.xm, :, 0, HB], W.at[p.xm, :, 0, HB], x3, p.at(x=p.xp))
    net.got(W.at[p.xp, :, :, HB], x2)
    net.send(W.at[p.xp, :, 1, HB], W.at[p.xp, :, 1, HB], x4, p.at(x=p.xm))
    net.got(W.at[:, p.yhm, :, HA], y1, p.opp)
    net.send(W.at[:, p.yhm, 0, HA], W.at[:, p.yhm, 0, HA], y3, p.at(y=p.yp), p.opp)
    net.got(W.at[:, p.yhp, :, HA], y2, p.opp)
    net.send(W.at[:, p.yhp, 1, HA], W.at[:, p.yhp, 1, HA], y4, p.at(y=p.ym), p.opp)
    yield
    net.got(W.at[:, 1 - p.yh, 0, HA], y3, p.own)
    net.got(W.at[:, 1 - p.yh, 1, HA], y4, p.own)
    net.got(W.at[p.x2, :, 0, HB], x3)
    net.got(W.at[p.x2, :, 1, HB], x4)


def gather_ring(net, a, out):
    p = net.p
    s1, s3, s2 = net.sem(), net.sem(), net.sem()
    k = net.sem(4)
    net.send(a, out.at[p.z, p.c], s1, p.at(z=p.zf))
    net.send(a, out.at[p.z, p.c], s3, p.at(z=p.zb))
    net.send(a, out.at[p.z, p.c], k + 0, p.at(c=p.o))
    yield
    net.got(out.at[p.z, p.o], k + 0)
    yield
    jf, jb = (p.zf - p.z + 4) % 4, (p.zb - p.z + 4) % 4
    net.got(out.at[p.zb, p.c], s1)
    net.send(out.at[p.zb, p.c], out.at[p.zb, p.c], s2, p.at(z=p.zf))
    net.send(out.at[p.zb, p.c], out.at[p.zb, p.c], k + jb, p.at(c=p.o))
    net.got(out.at[p.zf, p.c], s3)
    net.send(out.at[p.zf, p.c], out.at[p.zf, p.c], k + jf, p.at(c=p.o))
    yield
    net.got(out.at[p.zp, p.o], k + 1)
    net.got(out.at[p.zm, p.o], k + 3)
    yield
    net.got(out.at[p.z2, p.c], s2)
    net.send(out.at[p.z2, p.c], out.at[p.z2, p.c], k + 2, p.at(c=p.o))
    net.got(out.at[p.z2, p.o], k + 2)


class ReduceRing:
    def __init__(self, net, V, out, RC, SB, RZ):
        self.net, self.V, self.out, self.RC, self.SB, self.RZ = net, V, out, RC, SB, RZ
        self.s2, self.sd, self.sr, self.k = net.sem(), net.sem(), net.sem(), net.sem(4)

    def push(self, j):
        p = self.net.p
        self.net.send(self.V.at[(p.z + j) % 4, p.o], self.RC.at[j], self.k + j, p.at(c=p.o))

    def rest(self):
        net, p, V, RC, SB, RZ, k = self.net, self.net.p, self.V, self.RC, self.SB, self.RZ, self.k
        jf, jb = (p.zf - p.z + 4) % 4, (p.zb - p.z + 4) % 4
        net.got(RC.at[2], k + 2)
        add(SB.at[0], V.at[p.z2, p.c], RC.at[2])
        net.send(SB.at[0], RZ.at[0], self.s2, p.at(z=p.zf))
        yield
        net.got(RC.at[jb], k + jb)
        add(SB.at[1], V.at[p.zb, p.c], RC.at[jb])
        net.send(SB.at[1], RZ.at[1], self.sd, p.at(z=p.zb))
        net.got(RC.at[jf], k + jf)
        add(RC.at[jf], V.at[p.zf, p.c], RC.at[jf])
        yield
        net.got(RZ.at[0], self.s2)
        add(RC.at[jf], RC.at[jf], RZ.at[0])
        net.send(RC.at[jf], RZ.at[2], self.sr, p.at(z=p.zf))
        net.got(RC.at[0], k + 0)
        add(RC.at[0], V.at[p.z, p.c], RC.at[0])
        yield
        net.got(RZ.at[1], self.sd)
        net.got(RZ.at[2], self.sr)
        add(self.out, RC.at[0], RZ.at[1], RZ.at[2])


def step(job, times=1):
    for _ in range(times):
        next(job, None)


def dot(a, b, dims):
    return lax.dot_general(a, b, (dims, ((), ())), preferred_element_type=F32)


NN, NT, TN = ((1,), (0,)), ((1,), (1,)), ((0,), (0,))


def whole(ref, columns=slice(None)):
    v = ref[:, :, :, :, columns]
    return v.reshape(D, v.shape[-1])


def row_norm(src, dst, gain, rows=32):
    def one(i, _):
        at = pl.ds(pl.multiple_of(i * rows, rows), rows)
        v = src[at].astype(F32)
        inv = lax.rsqrt(jnp.mean(v * v, axis=1, keepdims=True) + epsilon)
        dst[at] = (v * inv * gain).astype(dst.dtype)

    lax.fori_loop(0, ROWS // rows, one, None)


def forward_kernel(*refs):
    (tok, gout, conv_s, gu_s, down_s, small_s,
     n1_o, n2_o, go_o, ggu_o, hid_o, b_o, c_o, v_o, bx_o, mx_o, wc_o, pg_o, pf_o, resid, gains,
     T1, N1, GO, N2, WC, WG, WD, SM, B, C, V, BX, MX, GA, HID, GGU, PA, PB, PF, RC, SB, RZ,
     send, recv, local) = refs
    p = Place()
    BX[0, :, 0:8] = jnp.zeros((2, 8, 256), F32)
    greet(p, True, True)
    net = Net(p, send, recv, local)
    block = lambda j: (p.z + j) % 4
    halo = net.sem()

    gt = gather_ring(net, tok, T1)
    ac = gather_plane(net, conv_s, WC)
    am = gather_plane(net, small_s, SM)
    ad = gather_plane(net, down_s, WD)
    au = gather_plane(net, gu_s.at[:, 0:GA_N], WG.at[:, :, :, :, 0:GA_N])
    av = gather_plane(net, gu_s.at[:, GA_N:], WG.at[:, :, :, :, GA_N:])
    go = gather_ring(net, gout, GO)
    outs = []

    step(ac), step(am), step(gt)
    own_tok = net.copy(tok, T1.at[p.z, p.c])
    own_gout = net.copy(gout, GO.at[p.z, p.c])
    step(am), step(ac)
    step(am), step(ac)
    step(ad), step(au)
    step(am), step(ac)
    step(ad), step(au)
    step(gt, 2)
    step(go)
    step(am), step(ac)
    gains[...] = jnp.zeros(gains.shape, F32)
    for s in range(16):
        piece = SM[s // 4, (s // 2) % 2, s % 2, 0:16].astype(F32)
        at = (96 * s) // 128 * 128
        n = min(256, gains.shape[1] - at)
        gains[0:16, at : at + n] = gains[0:16, at : at + n] + piece[:, :n]
    gains[16:32, 0:256] = SM[0, 0, 0, 16:32].astype(F32)
    g_mix, g_ffn = gains[0:1, :D], gains[1:2, :D]
    taps = [gains[16 + i : 17 + i, 0:256] for i in range(3)]

    own_tok()
    lanes = lax.broadcasted_iota(jnp.int32, (256, 128), 1) < 64

    def project(j):
        zj = block(j)
        for cc in range(2):
            row_norm(T1.at[zj, cc], N1.at[zj, cc], g_mix)
        r = dot(N1[zj].reshape(256, D), whole(WC), NN)
        b1 = jnp.where(lanes, r[:, 512:640], 0.0)
        c1 = jnp.where(lanes, pltpu.roll(r[:, 512:640], 64, 1), 0.0)
        v1 = jnp.where(lanes, pltpu.roll(r[:, 640:768], 64, 1), 0.0)
        b = jnp.concatenate([r[:, 0:128], b1], axis=1)
        v = jnp.concatenate([r[:, 256:384], v1], axis=1)
        B[zj] = b.reshape(2, 128, 256)
        V[zj] = v.reshape(2, 128, 256)
        C[zj] = jnp.concatenate([r[:, 128:256], c1], axis=1).reshape(2, 128, 256)
        BX[zj, :, 8:136] = (b * v).reshape(2, 128, 256)

    project(0)
    step(ad), step(au)
    step(gt)
    project(1)
    project(3)
    step(gt)
    project(2)
    net.send(BX.at[0:4, :, 128:136], BX.at[pl.ds(p.yl, 4), :, 0:8], halo, p.at(y=p.y + 1 - 2 * p.yl))
    step(go, 2)
    step(av)
    net.got(BX.at[pl.ds(1 - p.yl, 4), :, 0:8], halo)

    r1 = ReduceRing(net, PA, resid, RC, SB, RZ)

    def mix(j):
        zj = block(j)
        for cc in range(2):
            conv = (
                taps[0] * BX[zj, cc, 8:136] + taps[1] * BX[zj, cc, 7:135] + taps[2] * BX[zj, cc, 6:134]
            )
            MX[zj, cc] = (C[zj, cc] * conv).astype(BF)
        o = jnp.concatenate([whole(WC, slice(384, 512)), whole(WC, slice(640, 768))], axis=1)
        PA[zj] = dot(MX[zj].reshape(256, 256), o, NT).astype(BF).reshape(2, 128, D)
        r1.push(j)

    for j in (2, 1, 3, 0):
        mix(j)
    r1 = r1.rest()
    step(r1)
    step(ad), step(au), step(av)
    step(r1)
    step(go, 2)
    step(ad), step(au), step(av)
    step(r1)
    step(av)
    own_gout()

    def act(j):
        zj = block(j)
        GA[zj] = dot(GO[zj].reshape(256, D), whole(WD), NN)

    act(0)
    step(r1)

    def second(i, _):
        at = pl.ds(pl.multiple_of(i * 32, 32), 32)
        v = tok[at].astype(F32) + resid[at]
        resid[at] = v
        inv = lax.rsqrt(jnp.mean(v * v, axis=1, keepdims=True) + epsilon)
        N2[p.z, p.c, at] = (v * inv * g_ffn).astype(BF)

    lax.fori_loop(0, ROWS // 32, second, None)
    g2 = gather_ring(net, N2.at[p.z, p.c], N2)
    step(g2)
    step(av)
    outs.append(net.copy(N1, n1_o))
    outs.append(net.copy(B, b_o))
    outs.append(net.copy(C, c_o))
    outs.append(net.copy(V, v_o))
    outs.append(net.copy(BX.at[0:4], bx_o))
    outs.append(net.copy(MX, mx_o))
    outs.append(net.copy(WC, wc_o))
    outs.append(net.copy(GO, go_o))
    step(g2)

    def feed(j):
        zj = block(j)
        n2 = N2[zj].reshape(256, D)
        for t in range(7):
            r = dot(n2, whole(WG, slice(256 * t, 256 * t + 256)), NN)
            g, u = r[:, :128], r[:, 128:]
            ga = GA[zj, :, 128 * t : 128 * t + 128]
            s = jax.nn.sigmoid(g)
            silu = g * s
            HID[zj, :, 128 * t : 128 * t + 128] = (silu * u).astype(BF)
            GGU[zj, :, 256 * t : 256 * t + 128] = (ga * u * s * (1.0 + g * (1.0 - s))).astype(BF)
            GGU[zj, :, 256 * t + 128 : 256 * t + 256] = (ga * silu).astype(BF)

    def back(j):
        zj = block(j)
        PB[zj] = dot(GGU[zj], whole(WG), NT).astype(BF).reshape(2, 128, D)

    def down(j):
        zj = block(j)
        PF[zj] = dot(HID[zj], whole(WD), NT).astype(BF).reshape(2, 128, D)

    feed(0)
    act(1)
    step(g2)
    back(0)
    act(3)
    act(2)
    step(g2)
    feed(1)
    back(1)
    feed(3)
    back(3)
    step(g2)
    outs.append(net.copy(N2, n2_o))
    feed(2)
    back(2)
    outs.append(net.copy(PB, pg_o))
    outs.append(net.copy(HID, hid_o))
    outs.append(net.copy(GGU, ggu_o))
    for j in range(4):
        down(j)
    outs.append(net.copy(PF, pf_o))
    for job in (gt, go, g2, ac, am, ad, au, av):
        assert next(job, "end") == "end"
    net.finish()
    for done in outs:
        done()


GA_N = 1024


def forward_call(tok, gout, conv_pack, gu_pack, down_pack, small):
    any_, vm = pl.BlockSpec(memory_space=pl.ANY), pl.BlockSpec(memory_space=pltpu.VMEM)
    ring = (4, 2, ROWS, D)
    outs = [shape(ring), shape(ring), shape(ring), shape((4, 256, 1792)), shape((4, 256, FP))]
    outs += [shape((4, 2, ROWS, 256), F32)] * 3 + [shape((4, 2, 136, 256), F32), shape((4, 2, ROWS, 256))]
    outs += [slots(768), shape(ring), shape(ring), shape((ROWS, D), F32), shape((32, D), F32)]
    vmem = lambda s, t=BF: pltpu.VMEM(s, t)
    scratch = [vmem(ring)] * 4 + [vmem((4, 2, 2, 96, n)) for n in (768, 1792, FP)]
    scratch += [vmem((4, 2, 2, 32, 256))] + [vmem((4, 2, ROWS, 256), F32)] * 3
    scratch += [vmem((5, 2, 136, 256), F32), vmem((4, 2, ROWS, 256)), vmem((4, 256, FP), F32)]
    scratch += [vmem((4, 256, FP)), vmem((4, 256, 1792)), vmem(ring), vmem(ring), vmem(ring)]
    scratch += [vmem((4, ROWS, D)), vmem((2, ROWS, D)), vmem((3, ROWS, D))]
    scratch += [pltpu.SemaphoreType.DMA((160,)), pltpu.SemaphoreType.DMA((160,)), pltpu.SemaphoreType.DMA((24,))]
    return pl.pallas_call(
        forward_kernel,
        out_shape=tuple(outs),
        in_specs=[vm] + [any_] * 5,
        out_specs=tuple([any_] * 13 + [vm] * 2),
        scratch_shapes=scratch,
        compiler_params=pltpu.CompilerParams(
            collective_id=0, has_side_effects=True, vmem_limit_bytes=VMEM_LIMIT),
        name="forward",
    )(tok, gout, conv_pack, gu_pack, down_pack, small)


def exchange(name, number, gathers=(), rings=(), ring_sums=(), plane_sums=()):
    ng, nz, ns, nq = len(gathers), len(rings), len(ring_sums), len(plane_sums)

    def kernel(*refs):
        refs = list(refs)

        def take(n):
            part, refs[:] = refs[:n], refs[n:]
            return part

        a, b, d, e = take(ng), take(nz), take(ns), take(nq)
        ao, bo, do, eo = take(ng), take(nz), take(ns), take(nq)
        ds = [take(3) for _ in range(ns)]
        es = [take(8) for _ in range(nq)]
        send, recv, local = refs
        p = Place()
        greet(p, bool(ng + nq), bool(nz + ns))
        net = Net(p, send, recv, local)
        rr = [ReduceRing(net, v, o, *s) for v, o, s in zip(d, do, ds)]
        for r in rr:
            for j in (2, 1, 3, 0):
                r.push(j)
        jobs = [r.rest() for r in rr]
        jobs += [gather_ring(net, v, o) for v, o in zip(b, bo)]
        dones = [net.copy(v, o.at[p.z, p.c]) for v, o in zip(b, bo)]
        jobs += [gather_plane(net, v, o) for v, o in zip(a, ao)]
        jobs += [reduce_plane(net, v, o, *s) for v, o, s in zip(e, eo, es)]
        together(*jobs)
        net.finish()
        for f in dones:
            f()

    any_, vm = pl.BlockSpec(memory_space=pl.ANY), pl.BlockSpec(memory_space=pltpu.VMEM)
    scratch = []
    for v in ring_sums:
        scratch += ring_scratch(v.shape[-1])
    for v in plane_sums:
        scratch += plane_scratch(v.shape[-1])
    count = 24 * (ng + nq) + 12 * (nz + ns)
    scratch += [pltpu.SemaphoreType.DMA((count,))] * 2 + [pltpu.SemaphoreType.DMA((ng + nz + 1,))]
    outs = [slots(v.shape[-1]) for v in gathers] + [blocks(v.shape[-1]) for v in rings]
    outs += [shape((ROWS, v.shape[-1]), F32) for v in ring_sums]
    outs += [shape((96, v.shape[-1]), F32) for v in plane_sums]
    return pl.pallas_call(
        kernel,
        out_shape=tuple(outs),
        in_specs=[any_] * (ng + nz) + [vm] * (ns + nq),
        out_specs=tuple([any_] * (ng + nz) + [vm] * (ns + nq)),
        scratch_shapes=scratch,
        compiler_params=pltpu.CompilerParams(
            collective_id=number, has_side_effects=True, vmem_limit_bytes=VMEM_LIMIT),
        name=name,
    )(*gathers, *rings, *ring_sums, *plane_sums)


def norm_backward_rule(gradient_of_normalized, centered_input, inverse_root, gain_widened):
    weighted_rows = gain_widened * gradient_of_normalized
    return inverse_root * (
        weighted_rows
        - centered_input * jnp.mean(weighted_rows * centered_input, axis=1, keepdims=True)
    )


SWAP = [(t, t ^ 1) for t in range(8)]


def matmul(a, b, dims, out=F32):
    return lax.dot_general(a, b, (dims, ((), ())), preferred_element_type=F32).astype(out)


def per_device(tokens, gain_mix, in_weight, conv_kernel, out_weight, gain_ffn, gate_weight, up_weight, down_weight, lengths, cotangent):
    dp, t = lax.axis_index("dp"), lax.axis_index("tensor")
    z, yl, c = t // 2, t % 2, dp % 2
    position = t * ROWS + jnp.arange(ROWS)
    live = (position < lengths[0]).astype(F32)[:, None]

    b, cg, v = in_weight[:, 0], in_weight[:, 1], in_weight[:, 2]
    o = out_weight.T
    conv_pack = jnp.concatenate(
        [b[:, :128], cg[:, :128], v[:, :128], o[:, :128], b[:, 128:], cg[:, 128:], o[:, 128:], v[:, 128:]],
        axis=1,
    )
    wide = lambda w: jnp.pad(w, ((0, 0), (0, FP - FB)))
    gu_pack = jnp.stack([wide(gate_weight).reshape(96, 7, 128), wide(up_weight).reshape(96, 7, 128)], axis=2)
    gu_pack = gu_pack.reshape(96, 1792)
    down_pack = wide(down_weight.T)
    small = jnp.zeros((32, 256), BF)
    off = (96 * dp) % 128
    small = lax.dynamic_update_slice(small, jnp.stack([gain_mix, gain_ffn]), (0, off))
    small = lax.dynamic_update_slice(small, conv_kernel, (16, 0))
    grad_out = (live * cotangent.astype(F32)).astype(BF)

    (normed_all, normed2_all, gout_all, ggu, hidden, bv, cv, vv, bxv, mixed, wc, gn2, ffn_part, resid, gains) = (
        forward_call(tokens, grad_out, conv_pack, gu_pack, down_pack, small)
    )
    g_mix, g_ffn = gains[0], gains[1]
    taps = gains[16:19, :CH]
    tok = tokens.astype(F32)
    inv2 = lax.rsqrt(jnp.mean(resid * resid, axis=1, keepdims=True) + epsilon)
    xhat2 = resid * inv2
    flat = lambda a: a.reshape(1024, -1)
    normed_all, normed2_all, gout_all = flat(normed_all), flat(normed2_all), flat(gout_all)
    ggu, hidden, mixed = flat(ggu), flat(hidden), flat(mixed)[:, :CH]
    wc = wc.reshape(D, 768)
    w_in = jnp.concatenate([wc[:, 0:128], wc[:, 512:576], wc[:, 128:256], wc[:, 576:640], wc[:, 256:384], wc[:, 704:768]], axis=1)
    w_out_t = jnp.concatenate([wc[:, 384:512], wc[:, 640:704]], axis=1)
    c_gate, value, b_gate = flat(cv)[:, :CH], flat(vv)[:, :CH], flat(bv)[:, :CH]
    bx = flat(bxv[:, :, 8:136])[:, :CH]
    bx_one = flat(bxv[:, :, 7:135])[:, :CH]
    bx_two = flat(bxv[:, :, 6:134])[:, :CH]
    conv_sum = taps[0] * bx + taps[1] * bx_one + taps[2] * bx_two
    gu_full = matmul(normed2_all, ggu, ((0,), (0,)), BF).reshape(D, 7, 2, 128)
    gate_full, up_full = gu_full[:, :, 0].reshape(D, FP), gu_full[:, :, 1].reshape(D, FP)
    down_full = matmul(gout_all, hidden, ((0,), (0,)), BF)

    as_slots = lambda v: v.reshape(4, 2, 2, 96, v.shape[-1])
    gn2_rows, gate_sum = exchange(
        "fourth", 3, ring_sums=(gn2,), plane_sums=(as_slots(gate_full),)
    )
    grad_resid = grad_out.astype(F32) + norm_backward_rule(gn2_rows, xhat2, inv2, g_ffn)
    branch_all, up_sum = exchange(
        "fifth", 4, rings=(grad_resid.astype(BF),), plane_sums=(as_slots(up_full),)
    )
    branch_all = branch_all.reshape(1024, D)
    out_full = matmul(branch_all, mixed, ((0,), (0,)), BF)
    grad_mixed = matmul(branch_all, w_out_t, ((1,), (0,)))
    grad_c = grad_mixed * conv_sum
    grad_conv = grad_mixed * c_gate
    gc4 = grad_conv.reshape(4, 2, ROWS, CH)
    ahead = lax.ppermute(gc4[:, :, :2], "tensor", SWAP)
    shifted = jnp.pad(ahead, ((0, 1), (0, 0), (0, 0), (0, 0)))[1:]
    ahead = jnp.where(yl == 0, ahead, shifted)
    ext = jnp.concatenate([gc4, ahead], axis=2)
    grad_bx = (
        taps[0] * grad_conv
        + taps[1] * ext[:, :, 1:-1].reshape(1024, CH)
        + taps[2] * ext[:, :, 2:].reshape(1024, CH)
    )
    kernel_part = jnp.stack(
        [jnp.sum(grad_conv * bx, 0), jnp.sum(grad_conv * bx_one, 0), jnp.sum(grad_conv * bx_two, 0)]
    )
    grad_projected = jnp.concatenate([grad_bx * value, grad_c, grad_bx * b_gate], axis=1).astype(BF)
    in_full = matmul(normed_all, grad_projected, ((0,), (0,)), BF)
    gn1 = matmul(grad_projected, w_in, ((1,), (1,)), BF)
    conv_full = jnp.concatenate([in_full, out_full], axis=1)
    taps_at = jnp.pad(kernel_part.T.reshape(16, 12, 3), ((0, 0), (0, 84), (0, 0))).astype(BF)
    down_full = lax.dynamic_update_slice(down_full, taps_at.reshape(D, 3), (0, FB))
    gn1_rows, ffn_rows, down_sum, conv_sums = exchange(
        "sixth",
        5,
        ring_sums=(gn1.reshape(4, 2, ROWS, D), ffn_part),
        plane_sums=(as_slots(down_full), as_slots(conv_full)),
    )
    layer_out = (live * (resid + ffn_rows)).astype(BF)
    inv1 = lax.rsqrt(jnp.mean(tok * tok, axis=1, keepdims=True) + epsilon)
    tokens_grad = (grad_resid + norm_backward_rule(gn1_rows, tok * inv1, inv1, g_mix)).astype(BF)

    in_grad = conv_sums[:, : 3 * CH].reshape(96, 3, CH)
    out_grad = conv_sums[:, 3 * CH :].T
    gate_grad, up_grad = gate_sum[:, :FB], up_sum[:, :FB]
    down_grad = down_sum[:, :FB].T
    mix_share = jnp.sum(in_grad * in_weight.astype(F32), axis=(1, 2)) / gain_mix.astype(F32)
    ffn_share = jnp.sum(
        gate_grad * gate_weight.astype(F32) + up_grad * up_weight.astype(F32), axis=1
    ) / gain_ffn.astype(F32)
    shares = lax.psum_scatter(
        jnp.stack([mix_share, ffn_share]).reshape(2, 8, 12), "tensor", scatter_dimension=1
    )
    move = [(i, (i % 8) * 16 + i // 8) for i in range(128)]
    kernel_grad = lax.ppermute(down_sum[:12, FB : FB + 3].T, ("dp", "tensor"), move)
    return (
        layer_out,
        tokens_grad,
        shares[0],
        in_grad,
        kernel_grad,
        out_grad,
        shares[1],
        gate_grad,
        up_grad,
        down_grad,
    )


def solution(mesh):
    placed = (
        P(("dp", "tensor"), None),
        P("dp"),
        P("dp", None, "tensor"),
        P(None, "tensor"),
        P("tensor", "dp"),
        P("dp"),
        P("dp", "tensor"),
        P("dp", "tensor"),
        P("tensor", "dp"),
        P("dp"),
        P(("dp", "tensor"), None),
    )
    return jax.shard_map(
        per_device,
        mesh=mesh,
        in_specs=placed,
        out_specs=(
            P(("dp", "tensor"), None),
            P(("dp", "tensor"), None),
            P(("dp", "tensor")),
            P("dp", None, "tensor"),
            P(None, ("dp", "tensor")),
            P("tensor", "dp"),
            P(("dp", "tensor")),
            P("dp", "tensor"),
            P("dp", "tensor"),
            P("tensor", "dp"),
        ),
        check_vma=False,
    )
```

```python
import functools

import jax
import jax.numpy as jnp
from jax import lax
from jax.experimental import pallas as pl
from jax.experimental.pallas import tpu as pltpu
from jax.sharding import PartitionSpec as P

epsilon = 1e-05
MESH = pl.DeviceIdType.MESH
BF = jnp.bfloat16
F32 = jnp.float32
D = 1536
ROWS = 128
CH = 192
FB = 864
FP = 896
HALF = 48
VMEM_LIMIT = 60 << 20


class Place:
    def __init__(self):
        dp = lax.axis_index("dp")
        t = lax.axis_index("tensor")
        self.x, self.yh, self.c = dp // 4, (dp // 2) % 2, dp % 2
        self.z, self.yl = t // 2, t % 2
        self.y = self.yh * 2 + self.yl
        self.o = 1 - self.c
        self.xp, self.xm, self.x2 = (self.x + 1) % 4, (self.x + 3) % 4, (self.x + 2) % 4
        self.yp, self.ym = (self.y + 1) % 4, (self.y + 3) % 4
        self.yhp, self.yhm = self.yp // 2, self.ym // 2
        self.way = 1 - 2 * self.c
        self.zf = (self.z + self.way + 4) % 4
        self.zb = (self.z - self.way + 4) % 4
        self.zp, self.zm, self.z2 = (self.z + 1) % 4, (self.z + 3) % 4, (self.z + 2) % 4
        self.own = self.c == self.yl
        self.opp = self.c != self.yl

    def at(self, x=None, y=None, z=None, c=None):
        x = self.x if x is None else x
        y = self.y if y is None else y
        z = self.z if z is None else z
        c = self.c if c is None else c
        return (x * 4 + (y // 2) * 2 + c, z * 2 + y % 2)


class Net:
    def __init__(self, place, send, recv, local=None):
        self.p, self.ss, self.rs, self.ls = place, send, recv, local
        self.ns = self.nr = self.nl = 0
        self.pending = []

    def sem(self, n=1):
        k = self.nr
        self.nr += n
        return k

    def send(self, src, dst, recv_index, target, cond=None, pending=None):
        k = self.ns
        self.ns += 1
        d = pltpu.make_async_remote_copy(
            src_ref=src, dst_ref=dst, send_sem=self.ss.at[k], recv_sem=self.rs.at[recv_index],
            device_id=target, device_id_type=MESH)
        run(cond, d.start)
        (self.pending if pending is None else pending).append((cond, d))

    def copy(self, src, dst, cond=None):
        k = self.nl
        self.nl += 1
        d = pltpu.make_async_copy(src, dst, self.ls.at[k])
        run(cond, d.start)
        return lambda: run(cond, d.wait)

    def got(self, dst, recv_index, cond=None):
        d = pltpu.make_async_remote_copy(
            src_ref=dst, dst_ref=dst, send_sem=self.ss.at[0], recv_sem=self.rs.at[recv_index],
            device_id=self.p.at(c=self.p.o), device_id_type=MESH)
        run(cond, d.wait_recv)

    def finish(self, pending=None):
        pending = self.pending if pending is None else pending
        for cond, d in pending:
            run(cond, d.wait_send)
        pending.clear()


def run(cond, f):
    if cond is None:
        f()
    else:
        pl.when(cond)(f)


def greet(p, plane, ring):
    bar = pltpu.get_barrier_semaphore()
    who = [p.at(c=p.o)]
    if plane:
        for c in (0, 1):
            who += [p.at(x=p.xp, c=c), p.at(x=p.xm, c=c), p.at(y=p.yp, c=c), p.at(y=p.ym, c=c)]
    if ring:
        who += [p.at(z=p.zp), p.at(z=p.zm)]
    for w in who:
        pl.semaphore_signal(bar, inc=1, device_id=w, device_id_type=MESH)
    pl.semaphore_wait(bar, len(who))


def add(out, *terms):
    lead = out.shape[:-2]
    count = 1
    for s in lead:
        count *= s

    def one(i):
        at = []
        for s in reversed(lead):
            at.append(i % s)
            i = i // s
        at = tuple(reversed(at))
        v = terms[0][at].astype(F32) if at else terms[0][...].astype(F32)
        for t in terms[1:]:
            v = v + (t[at] if at else t[...]).astype(F32)
        if at:
            out[at] = v.astype(out.dtype)
        else:
            out[...] = v.astype(out.dtype)

    if not lead:

        def rows(i, _):
            at = pl.ds(pl.multiple_of(i * 16, 16), 16)
            v = terms[0][at].astype(F32)
            for t in terms[1:]:
                v = v + t[at].astype(F32)
            out[at] = v.astype(out.dtype)

        lax.fori_loop(0, out.shape[0] // 16, rows, None)
    else:
        lax.fori_loop(0, count, lambda i, _: one(i), None)


def ring_scratch(n):
    return [pltpu.VMEM((4, ROWS, n), BF), pltpu.VMEM((2, ROWS, n), BF), pltpu.VMEM((3, ROWS, n), BF)]


def shape(s, t=BF):
    return jax.ShapeDtypeStruct(s, t)


def slots(n):
    return shape((4, 2, 2, 96, n))


def gather_plane(net, sh, W):
    p = net.p
    h = sh.shape[0] // 2
    HA, HB = pl.ds(0, h), pl.ds(h, h)
    i_own, f1, f2, f3, f4 = net.sem(), net.sem(2), net.sem(2), net.sem(2), net.sem(2)
    r1, r2, r3, r4, y1, y2, y3, y4, x1, x2, x3, x4 = (net.sem() for _ in range(12))
    q = p.yl
    done = net.copy(sh, W.at[p.x, p.yh, p.c], p.own)
    net.send(sh.at[HA], W.at[p.x, p.yh, p.c, HA], f1 + p.c, p.at(x=p.xp, c=q))
    net.send(sh.at[HA], W.at[p.x, p.yh, p.c, HA], f2 + p.c, p.at(x=p.xm, c=q))
    net.send(sh.at[HB], W.at[p.x, p.yh, p.c, HB], f3 + p.c, p.at(y=p.yp, c=q))
    net.send(sh.at[HB], W.at[p.x, p.yh, p.c, HB], f4 + p.c, p.at(y=p.ym, c=q))
    net.send(sh, W.at[p.x, p.yh, p.c], i_own, p.at(c=p.o), p.opp)
    yield
    net.got(W.at[p.xm, p.yh, 0, HA], f1 + 0, p.own)
    net.got(W.at[p.x, p.yhm, 0, HB], f3 + 0, p.opp)
    net.send(W.at[p.xm, p.yh, 0, HA], W.at[p.xm, p.yh, 0, HA], r1, p.at(x=p.xp), p.own)
    net.send(W.at[p.x, p.yhm, 0, HB], W.at[p.x, p.yhm, 0, HB], r3, p.at(y=p.yp), p.opp)
    net.got(W.at[p.xp, p.yh, 1, HA], f2 + 1, p.own)
    net.got(W.at[p.x, p.yhp, 1, HB], f4 + 1, p.opp)
    net.send(W.at[p.xp, p.yh, 1, HA], W.at[p.xp, p.yh, 1, HA], r2, p.at(x=p.xm), p.own)
    net.send(W.at[p.x, p.yhp, 1, HB], W.at[p.x, p.yhp, 1, HB], r4, p.at(y=p.ym), p.opp)
    yield
    done()
    net.got(W.at[p.x, p.yh, p.o], i_own, p.own)
    net.got(W.at[p.xm, p.yh, 1, HA], f1 + 1, p.own)
    net.got(W.at[p.xp, p.yh, 0, HA], f2 + 0, p.own)
    net.got(W.at[p.x, p.yhm, 1, HB], f3 + 1, p.opp)
    net.got(W.at[p.x, p.yhp, 0, HB], f4 + 0, p.opp)
    net.got(W.at[p.x2, p.yh, 0, HA], r1, p.own)
    net.got(W.at[p.x2, p.yh, 1, HA], r2, p.own)
    net.send(W.at[:, p.yh, :, HA], W.at[:, p.yh, :, HA], y1, p.at(y=p.yp), p.own)
    net.send(W.at[:, p.yh, :, HA], W.at[:, p.yh, :, HA], y2, p.at(y=p.ym), p.own)
    net.got(W.at[p.x, 1 - p.yh, 0, HB], r3, p.own)
    net.got(W.at[p.x, 1 - p.yh, 1, HB], r4, p.own)
    net.send(W.at[p.x, :, :, HB], W.at[p.x, :, :, HB], x1, p.at(x=p.xp))
    net.send(W.at[p.x, :, :, HB], W.at[p.x, :, :, HB], x2, p.at(x=p.xm))
    yield
    net.got(W.at[p.xm, :, :, HB], x1)
    net.send(W.at[p.xm, :, 0, HB], W.at[p.xm, :, 0, HB], x3, p.at(x=p.xp))
    net.got(W.at[p.xp, :, :, HB], x2)
    net.send(W.at[p.xp, :, 1, HB], W.at[p.xp, :, 1, HB], x4, p.at(x=p.xm))
    net.got(W.at[:, p.yhm, :, HA], y1, p.opp)
    net.send(W.at[:, p.yhm, 0, HA], W.at[:, p.yhm, 0, HA], y3, p.at(y=p.yp), p.opp)
    net.got(W.at[:, p.yhp, :, HA], y2, p.opp)
    net.send(W.at[:, p.yhp, 1, HA], W.at[:, p.yhp, 1, HA], y4, p.at(y=p.ym), p.opp)
    yield
    net.got(W.at[:, 1 - p.yh, 0, HA], y3, p.own)
    net.got(W.at[:, 1 - p.yh, 1, HA], y4, p.own)
    net.got(W.at[p.x2, :, 0, HB], x3)
    net.got(W.at[p.x2, :, 1, HB], x4)


def gather_ring(net, a, out):
    p = net.p
    s1, s3, s2 = net.sem(), net.sem(), net.sem()
    k = net.sem(4)
    net.send(a, out.at[p.z, p.c], s1, p.at(z=p.zf))
    net.send(a, out.at[p.z, p.c], s3, p.at(z=p.zb))
    net.send(a, out.at[p.z, p.c], k + 0, p.at(c=p.o))
    yield
    net.got(out.at[p.z, p.o], k + 0)
    yield
    jf, jb = (p.zf - p.z + 4) % 4, (p.zb - p.z + 4) % 4
    net.got(out.at[p.zb, p.c], s1)
    net.send(out.at[p.zb, p.c], out.at[p.zb, p.c], s2, p.at(z=p.zf))
    net.send(out.at[p.zb, p.c], out.at[p.zb, p.c], k + jb, p.at(c=p.o))
    net.got(out.at[p.zf, p.c], s3)
    net.send(out.at[p.zf, p.c], out.at[p.zf, p.c], k + jf, p.at(c=p.o))
    yield
    net.got(out.at[p.zp, p.o], k + 1)
    net.got(out.at[p.zm, p.o], k + 3)
    yield
    net.got(out.at[p.z2, p.c], s2)
    net.send(out.at[p.z2, p.c], out.at[p.z2, p.c], k + 2, p.at(c=p.o))
    net.got(out.at[p.z2, p.o], k + 2)


class ReduceRing:
    def __init__(self, net, V, out, RC, SB, RZ):
        self.net, self.V, self.out, self.RC, self.SB, self.RZ = net, V, out, RC, SB, RZ
        self.s2, self.sd, self.sr, self.k = net.sem(), net.sem(), net.sem(), net.sem(4)
        self.mine = []
        self.send = functools.partial(net.send, pending=self.mine)

    def push(self, j):
        p = self.net.p
        self.send(self.V.at[(p.z + j) % 4, p.o], self.RC.at[j], self.k + j, p.at(c=p.o))

    def rest(self):
        net, p, V, RC, SB, RZ, k = self.net, self.net.p, self.V, self.RC, self.SB, self.RZ, self.k
        jf, jb = (p.zf - p.z + 4) % 4, (p.zb - p.z + 4) % 4
        net.got(RC.at[2], k + 2)
        add(SB.at[0], V.at[p.z2, p.c], RC.at[2])
        self.send(SB.at[0], RZ.at[0], self.s2, p.at(z=p.zf))
        yield
        net.got(RC.at[jb], k + jb)
        add(SB.at[1], V.at[p.zb, p.c], RC.at[jb])
        self.send(SB.at[1], RZ.at[1], self.sd, p.at(z=p.zb))
        net.got(RC.at[jf], k + jf)
        add(RC.at[jf], V.at[p.zf, p.c], RC.at[jf])
        yield
        net.got(RZ.at[0], self.s2)
        add(RC.at[jf], RC.at[jf], RZ.at[0])
        self.send(RC.at[jf], RZ.at[2], self.sr, p.at(z=p.zf))
        net.got(RC.at[0], k + 0)
        add(RC.at[0], V.at[p.z, p.c], RC.at[0])
        yield
        net.got(RZ.at[1], self.sd)
        net.got(RZ.at[2], self.sr)
        add(self.out, RC.at[0], RZ.at[1], RZ.at[2])


def step(job, times=1):
    for _ in range(times):
        next(job, None)


def dot(a, b, dims):
    return lax.dot_general(a, b, (dims, ((), ())), preferred_element_type=F32)


NN, NT, TN = ((1,), (0,)), ((1,), (1,)), ((0,), (0,))


def whole(ref, columns=slice(None)):
    v = ref[:, :, :, :, columns]
    return v.reshape(D, v.shape[-1])


def row_norm(src, dst, gain, rows=32):
    def one(i, _):
        at = pl.ds(pl.multiple_of(i * rows, rows), rows)
        v = src[at].astype(F32)
        inv = lax.rsqrt(jnp.mean(v * v, axis=1, keepdims=True) + epsilon)
        dst[at] = (v * inv * gain).astype(dst.dtype)

    lax.fori_loop(0, ROWS // rows, one, None)


def forward_kernel(*refs):
    (tok, gout, conv_s, gu_s, down_s, small_s,
     n1_o, n2_o, go_o, ggu_o, hid_o, b_o, c_o, v_o, bx_o, mx_o, wc_o, pg_o, pf_o, resid, gains,
     T1, N1, GO, N2, WC, WG, WD, SM, B, C, V, BX, MX, GA, HID, GGU, PA, PB, PF, RC, SB, RZ,
     send, recv, local) = refs
    p = Place()
    BX[0, :, 0:8] = jnp.zeros((2, 8, 256), F32)
    greet(p, True, True)
    net = Net(p, send, recv, local)
    block = lambda j: (p.z + j) % 4
    halo = net.sem()

    gt = gather_ring(net, tok, T1)
    ac = gather_plane(net, conv_s, WC)
    am = gather_plane(net, small_s, SM)
    ad = gather_plane(net, down_s, WD)
    au = gather_plane(net, gu_s.at[:, 0:GA_N], WG.at[:, :, :, :, 0:GA_N])
    av = gather_plane(net, gu_s.at[:, GA_N:], WG.at[:, :, :, :, GA_N:])
    go = gather_ring(net, gout, GO)
    outs = []

    step(ac), step(am), step(gt)
    own_tok = net.copy(tok, T1.at[p.z, p.c])
    own_gout = net.copy(gout, GO.at[p.z, p.c])
    step(am), step(ac)
    step(am), step(ac)
    step(ad), step(au)
    step(am), step(ac)
    step(ad), step(au)
    step(gt, 2)
    step(go)
    step(am), step(ac)
    gains[...] = jnp.zeros(gains.shape, F32)
    for s in range(16):
        piece = SM[s // 4, (s // 2) % 2, s % 2, 0:16].astype(F32)
        at = (96 * s) // 128 * 128
        n = min(256, gains.shape[1] - at)
        gains[0:16, at : at + n] = gains[0:16, at : at + n] + piece[:, :n]
    gains[16:32, 0:256] = SM[0, 0, 0, 16:32].astype(F32)
    g_mix, g_ffn = gains[0:1, :D], gains[1:2, :D]
    taps = [gains[16 + i : 17 + i, 0:256] for i in range(3)]

    own_tok()
    lanes = lax.broadcasted_iota(jnp.int32, (256, 128), 1) < 64

    def project(j):
        zj = block(j)
        for cc in range(2):
            row_norm(T1.at[zj, cc], N1.at[zj, cc], g_mix)
        r = dot(N1[zj].reshape(256, D), whole(WC), NN)
        b1 = jnp.where(lanes, r[:, 512:640], 0.0)
        c1 = jnp.where(lanes, pltpu.roll(r[:, 512:640], 64, 1), 0.0)
        v1 = jnp.where(lanes, pltpu.roll(r[:, 640:768], 64, 1), 0.0)
        b = jnp.concatenate([r[:, 0:128], b1], axis=1)
        v = jnp.concatenate([r[:, 256:384], v1], axis=1)
        B[zj] = b.reshape(2, 128, 256)
        V[zj] = v.reshape(2, 128, 256)
        C[zj] = jnp.concatenate([r[:, 128:256], c1], axis=1).reshape(2, 128, 256)
        BX[zj, :, 8:136] = (b * v).reshape(2, 128, 256)

    project(0)
    step(ad), step(au)
    step(gt)
    project(1)
    project(3)
    step(gt)
    project(2)
    net.send(BX.at[0:4, :, 128:136], BX.at[pl.ds(p.yl, 4), :, 0:8], halo, p.at(y=p.y + 1 - 2 * p.yl))
    step(go, 2)
    step(av)
    net.got(BX.at[pl.ds(1 - p.yl, 4), :, 0:8], halo)

    r1 = ReduceRing(net, PA, resid, RC, SB, RZ)

    def mix(j):
        zj = block(j)
        for cc in range(2):
            conv = (
                taps[0] * BX[zj, cc, 8:136] + taps[1] * BX[zj, cc, 7:135] + taps[2] * BX[zj, cc, 6:134]
            )
            MX[zj, cc] = (C[zj, cc] * conv).astype(BF)
        o = jnp.concatenate([whole(WC, slice(384, 512)), whole(WC, slice(640, 768))], axis=1)
        PA[zj] = dot(MX[zj].reshape(256, 256), o, NT).astype(BF).reshape(2, 128, D)
        r1.push(j)

    for j in (2, 1, 3, 0):
        mix(j)
    mixed_sends, r1 = r1.mine, r1.rest()
    step(r1)
    step(ad), step(au), step(av)
    step(r1)
    step(go, 2)
    step(ad), step(au), step(av)
    step(r1)
    step(av)
    own_gout()

    def act(j):
        zj = block(j)
        GA[zj] = dot(GO[zj].reshape(256, D), whole(WD), NN)

    act(0)
    step(r1)

    def second(i, _):
        at = pl.ds(pl.multiple_of(i * 32, 32), 32)
        v = tok[at].astype(F32) + resid[at]
        resid[at] = v
        inv = lax.rsqrt(jnp.mean(v * v, axis=1, keepdims=True) + epsilon)
        N2[p.z, p.c, at] = (v * inv * g_ffn).astype(BF)

    lax.fori_loop(0, ROWS // 32, second, None)
    g2 = gather_ring(net, N2.at[p.z, p.c], N2)
    step(g2)
    step(av)
    outs.append(net.copy(N1, n1_o))
    outs.append(net.copy(B, b_o))
    outs.append(net.copy(C, c_o))
    outs.append(net.copy(V, v_o))
    outs.append(net.copy(BX.at[0:4], bx_o))
    outs.append(net.copy(MX, mx_o))
    outs.append(net.copy(WC, wc_o))
    outs.append(net.copy(GO, go_o))
    step(g2)

    def feed(j):
        zj = block(j)
        n2 = N2[zj].reshape(256, D)
        for t in range(7):
            r = dot(n2, whole(WG, slice(256 * t, 256 * t + 256)), NN)
            g, u = r[:, :128], r[:, 128:]
            ga = GA[zj, :, 128 * t : 128 * t + 128]
            s = jax.nn.sigmoid(g)
            silu = g * s
            HID[zj, :, 128 * t : 128 * t + 128] = (silu * u).astype(BF)
            GGU[zj, :, 256 * t : 256 * t + 128] = (ga * u * s * (1.0 + g * (1.0 - s))).astype(BF)
            GGU[zj, :, 256 * t + 128 : 256 * t + 256] = (ga * silu).astype(BF)

    def back(j):
        zj = block(j)
        PB[zj] = dot(GGU[zj], whole(WG), NT).astype(BF).reshape(2, 128, D)

    def down(j):
        zj = block(j)
        PF[zj] = dot(HID[zj], whole(WD), NT).astype(BF).reshape(2, 128, D)

    feed(0)
    act(1)
    step(g2)
    back(0)
    act(3)
    act(2)
    step(g2)
    feed(1)
    back(1)
    feed(3)
    back(3)
    step(g2)
    outs.append(net.copy(N2, n2_o))
    feed(2)
    back(2)
    outs.append(net.copy(PB, pg_o))
    outs.append(net.copy(HID, hid_o))
    outs.append(net.copy(GGU, ggu_o))
    for j in range(4):
        down(j)
    outs.append(net.copy(PF, pf_o))
    for job in (gt, go, g2, ac, am, ad, au, av):
        assert next(job, "end") == "end"
    net.finish(mixed_sends)
    net.finish()
    for done in outs:
        done()


GA_N = 1024


def forward_call(tok, gout, conv_pack, gu_pack, down_pack, small):
    any_, vm = pl.BlockSpec(memory_space=pl.ANY), pl.BlockSpec(memory_space=pltpu.VMEM)
    ring = (4, 2, ROWS, D)
    outs = [shape(ring), shape(ring), shape(ring), shape((4, 256, 1792)), shape((4, 256, FP))]
    outs += [shape((4, 2, ROWS, 256), F32)] * 3 + [shape((4, 2, 136, 256), F32), shape((4, 2, ROWS, 256))]
    outs += [slots(768), shape(ring), shape(ring), shape((ROWS, D), F32), shape((32, D), F32)]
    vmem = lambda s, t=BF: pltpu.VMEM(s, t)
    scratch = [vmem(ring)] * 4 + [vmem((4, 2, 2, 96, n)) for n in (768, 1792, FP)]
    scratch += [vmem((4, 2, 2, 32, 256))] + [vmem((4, 2, ROWS, 256), F32)] * 3
    scratch += [vmem((5, 2, 136, 256), F32), vmem((4, 2, ROWS, 256)), vmem((4, 256, FP), F32)]
    scratch += [vmem((4, 256, FP)), vmem((4, 256, 1792)), vmem(ring), vmem(ring), vmem(ring)]
    scratch += [vmem((4, ROWS, D)), vmem((2, ROWS, D)), vmem((3, ROWS, D))]
    scratch += [pltpu.SemaphoreType.DMA((160,)), pltpu.SemaphoreType.DMA((160,)), pltpu.SemaphoreType.DMA((24,))]
    return pl.pallas_call(
        forward_kernel,
        out_shape=tuple(outs),
        in_specs=[vm] + [any_] * 5,
        out_specs=tuple([any_] * 13 + [vm] * 2),
        scratch_shapes=scratch,
        compiler_params=pltpu.CompilerParams(
            collective_id=0, has_side_effects=True, vmem_limit_bytes=VMEM_LIMIT),
        name="forward",
    )(tok, gout, conv_pack, gu_pack, down_pack, small)


def plane_scratch(n, h=HALF):
    return [
        pltpu.VMEM((2, 4, h, n), BF),
        pltpu.VMEM((2, 4, 2, h, n), BF),
        pltpu.VMEM((2, h, n), BF),
        pltpu.VMEM((3, h, n), BF),
        pltpu.VMEM((2, 2, h, n), BF),
        pltpu.VMEM((2, 2, 2, h, n), BF),
        pltpu.VMEM((2, h, n), BF),
        pltpu.VMEM((3, h, n), BF),
    ]


def reduce_plane(net, G, out, RA, RB, RC, F, RX, RY, RZ, H):
    p = net.p
    h = out.shape[0] // 2
    HA, HB = pl.ds(0, h), pl.ds(h, h)
    mine = []
    send = functools.partial(net.send, pending=mine)
    a0, a1, bp0, bp1, bm0, bm1, c0, c1, g0, g1, g2 = (net.sem() for _ in range(11))
    u0, u1, vp0, vp1, vm0, vm1, w0, w1, h0, h1, h2 = (net.sem() for _ in range(11))
    send(G.at[:, 1 - p.yh, 0, HA], RA.at[0], a0, p.at(y=p.ym), p.own)
    send(G.at[:, 1 - p.yh, 1, HA], RA.at[1], a1, p.at(y=p.yp), p.own)
    send(G.at[p.x2, :, 0, HB], RX.at[0], u0, p.at(x=p.xm))
    send(G.at[p.x2, :, 1, HB], RX.at[1], u1, p.at(x=p.xp))
    send(G.at[:, p.yhm, 1, HA], RB.at[0, :, 1], bp1, p.at(y=p.ym), p.opp)
    send(G.at[:, p.yhp, 0, HA], RB.at[1, :, 0], bm0, p.at(y=p.yp), p.opp)
    send(G.at[p.xm, :, 1, HB], RY.at[0, :, 1], vp1, p.at(x=p.xm))
    send(G.at[p.xp, :, 0, HB], RY.at[1, :, 0], vm0, p.at(x=p.xp))
    yield

    net.got(RX.at[0], u0)
    add(RX.at[0], RX.at[0], G.at[p.xm, :, 0, HB])
    send(RX.at[0], RY.at[0, :, 0], vp0, p.at(x=p.xm))
    net.got(RX.at[1], u1)
    add(RX.at[1], RX.at[1], G.at[p.xp, :, 1, HB])
    send(RX.at[1], RY.at[1, :, 1], vm1, p.at(x=p.xp))
    net.got(RA.at[0], a0, p.opp)
    net.got(RA.at[1], a1, p.opp)

    @pl.when(p.opp)
    def _():
        add(RA.at[0], RA.at[0], G.at[:, p.yhm, 0, HA])
        add(RA.at[1], RA.at[1], G.at[:, p.yhp, 1, HA])

    send(RA.at[0], RB.at[0, :, 0], bp0, p.at(y=p.ym), p.opp)
    send(RA.at[1], RB.at[1, :, 1], bm1, p.at(y=p.yp), p.opp)
    yield

    net.got(RY.at[0, :, 1], vp1)
    net.got(RY.at[1, :, 0], vm0)
    net.got(RY.at[0, :, 0], vp0)
    net.got(RY.at[1, :, 1], vm1)
    add(RY.at[0], RY.at[0], RY.at[1], G.at[p.x, :, :, HB])
    T = RY.at[0]
    send(T.at[1 - p.yh, 0], RZ.at[0], w0, p.at(y=p.ym), p.own)
    send(T.at[1 - p.yh, 1], RZ.at[1], w1, p.at(y=p.yp), p.own)
    send(T.at[p.yhm, 1], H.at[1], h1, p.at(y=p.ym, c=1), p.opp)
    send(T.at[p.yhp, 0], H.at[2], h2, p.at(y=p.yp, c=0), p.opp)
    send(T.at[p.yh, p.o], H.at[0], h0, p.at(c=p.o), p.own)

    net.got(RB.at[0, :, 1], bp1, p.own)
    net.got(RB.at[1, :, 0], bm0, p.own)
    net.got(RB.at[0, :, 0], bp0, p.own)
    net.got(RB.at[1, :, 1], bm1, p.own)

    @pl.when(p.own)
    def _():
        add(RB.at[0], RB.at[0], RB.at[1], G.at[:, p.yh, :, HA])

    S = RB.at[0]
    send(S.at[p.x2, 0], RC.at[0], c0, p.at(x=p.xm), p.own)
    send(S.at[p.x2, 1], RC.at[1], c1, p.at(x=p.xp), p.own)
    send(S.at[p.xm, 1], F.at[1], g1, p.at(x=p.xm, c=1), p.own)
    send(S.at[p.xp, 0], F.at[2], g2, p.at(x=p.xp, c=0), p.own)
    send(S.at[p.x, p.o], F.at[0], g0, p.at(c=p.o), p.own)
    yield

    net.got(RC.at[0], c0, p.own)
    net.got(RC.at[1], c1, p.own)
    net.got(RZ.at[0], w0, p.opp)
    net.got(RZ.at[1], w1, p.opp)

    @pl.when(p.own)
    def _():
        add(RC.at[0], RC.at[0], S.at[p.xm, 0])
        add(RC.at[1], RC.at[1], S.at[p.xp, 1])

    @pl.when(p.opp)
    def _():
        add(RZ.at[0], RZ.at[0], T.at[p.yhm, 0])
        add(RZ.at[1], RZ.at[1], T.at[p.yhp, 1])

    send(RC.at[0], F.at[1], g1, p.at(x=p.xm, c=0), p.own)
    send(RC.at[1], F.at[2], g2, p.at(x=p.xp, c=1), p.own)
    send(RZ.at[0], H.at[1], h1, p.at(y=p.ym, c=0), p.opp)
    send(RZ.at[1], H.at[2], h2, p.at(y=p.yp, c=1), p.opp)
    yield

    net.got(F.at[0], g0, p.opp)
    net.got(F.at[1], g1)
    net.got(F.at[2], g2)
    net.got(H.at[0], h0, p.opp)
    net.got(H.at[1], h1)
    net.got(H.at[2], h2)
    net.finish(mine)

    @pl.when(p.own)
    def _():
        F[0] = S[p.x, p.c]
        H[0] = T[p.yh, p.c]

    add(out.at[HA], F.at[0], F.at[1], F.at[2])
    add(out.at[HB], H.at[0], H.at[1], H.at[2])


def backward_kernel(*refs):
    (tok, gout, live, resid, gains, conv_s, gu_s, gcol,
     pg_i, n2_i, ggu_i, go_i, hid_i, pf_i, n1_i, b_i, c_i, v_i, bx_i, mx_i, wc_i,
     layer_out, tokens_grad, in3, out_t, gate, up, down_t, shares, taps_out,
     PV, N, GGU, GO, HID, B, C, V, BX, MX, WC, BR, GC, DA, DB, DD, KP,
     *more) = refs
    sa, sb, sd, sk, ring_a, ring_b = [more[8 * i : 8 * i + 8] for i in range(4)] + [more[32:35], more[35:38]]
    KG, GR, MR, R1, SA, SB_, SD, SC, SK, free, send, recv, local = more[38:]
    p = Place()
    GC[4, :, 128:136] = jnp.zeros((2, 8, 256), F32)
    greet(p, True, True)
    net = Net(p, send, recv, local)
    block = lambda j: (p.z + j) % 4
    halo = net.sem()
    g_mix, g_ffn = gains[0:1, :D], gains[1:2, :D]
    taps = [gains[16 + i : 17 + i, 0:256] for i in range(3)]
    partners = [p.at(c=p.o)]
    for cc in (0, 1):
        partners += [p.at(x=p.xp, c=cc), p.at(x=p.xm, c=cc), p.at(y=p.yp, c=cc), p.at(y=p.ym, c=cc)]

    pg_in = net.copy(pg_i, PV)
    n2_in = net.copy(n2_i, N)
    ggu_in = net.copy(ggu_i, GGU)
    pg_in()
    r2 = ReduceRing(net, PV, MR, *ring_a)
    for j in (2, 1, 3, 0):
        r2.push(j)
    r2_mine, r2 = r2.mine, r2.rest()

    def weight_grad(out, lhs, rhs, x0, n):
        a = lhs[:, :, :, 384 * x0 : 384 * x0 + 384].reshape(1024, 384)
        out[x0] = dot(a, rhs.reshape(1024, n), TN).astype(BF).reshape(2, 2, 96, n)

    ja = reduce_plane(net, DA, SA, *sa)
    jb = reduce_plane(net, DB, SB_, *sb)
    jd = reduce_plane(net, DD, SD, *sd)
    n2_in(), ggu_in()
    go_in, hid_in = net.copy(go_i, GO), net.copy(hid_i, HID)
    pairs = ((b_i, B), (c_i, C), (v_i, V), (bx_i, BX), (mx_i, MX), (wc_i, WC))
    later = [net.copy(a, b) for a, b in pairs]
    weight_grad(DA, N, GGU[:, :, 0:1024], 0, 1024)
    step(r2)
    weight_grad(DA, N, GGU[:, :, 0:1024], 1, 1024)
    step(r2)
    weight_grad(DA, N, GGU[:, :, 0:1024], 2, 1024)
    weight_grad(DA, N, GGU[:, :, 0:1024], 3, 1024)
    step(ja)
    weight_grad(DB, N, GGU[:, :, 1024:1792], 0, 768)
    weight_grad(DB, N, GGU[:, :, 1024:1792], 1, 768)
    weight_grad(DB, N, GGU[:, :, 1024:1792], 2, 768)
    weight_grad(DB, N, GGU[:, :, 1024:1792], 3, 768)
    step(r2)
    step(jb)
    step(ja)
    go_in(), hid_in()
    n1_in = net.copy(n1_i, N)
    for x0 in range(4):
        weight_grad(DD, GO, HID[...], x0, FP)
    step(r2)
    net.finish(r2_mine)

    def second(i, _):
        at = pl.ds(pl.multiple_of(i * 32, 32), 32)
        v = resid[at]
        inv = lax.rsqrt(jnp.mean(v * v, axis=1, keepdims=True) + epsilon)
        x = v * inv
        w = g_ffn * MR[at]
        g = gout[at].astype(F32) + inv * (w - x * jnp.mean(w * x, axis=1, keepdims=True))
        GR[at] = g
        BR[p.z, p.c, at] = g.astype(BF)

    lax.fori_loop(0, ROWS // 32, second, None)
    g3 = gather_ring(net, BR.at[p.z, p.c], BR)
    step(g3)
    pf_in = net.copy(pf_i, PV)
    step(jd)
    step(ja)
    step(jb)
    for f in later:
        f()
    KP[...] = jnp.zeros(KP.shape, F32)
    lanes = lax.broadcasted_iota(jnp.int32, (256, 128), 1) < 64
    o = jnp.concatenate([whole(WC, slice(384, 512)), whole(WC, slice(640, 768))], axis=1)

    def unmix(j):
        zj = block(j)
        gm = dot(BR[zj].reshape(256, D), o, NN)
        gm = jnp.concatenate([gm[:, :128], jnp.where(lanes, gm[:, 128:], 0.0)], axis=1).reshape(2, 128, 256)
        for cc in range(2):
            b0, b1, b2 = BX[zj, cc, 8:136], BX[zj, cc, 7:135], BX[zj, cc, 6:134]
            gc = gm[cc] * (taps[0] * b0 + taps[1] * b1 + taps[2] * b2)
            at = slice(128 * cc, 128 * cc + 128)
            GGU[zj, at, 128:256] = gc[:, :128].astype(BF)
            GGU[zj, at, 512:640] = pltpu.roll(gc[:, 128:], 64, 1).astype(BF)
            gv = gm[cc] * C[zj, cc]
            GC[zj + 1, cc, 0:128] = gv
            for i, b in enumerate((b0, b1, b2)):
                KP[i : i + 1] = KP[i : i + 1] + jnp.sum(gv * b, axis=0, keepdims=True)

    step(g3)
    unmix(0)
    step(g3)
    step(ja)
    step(jd)
    step(jb)
    step(g3)
    unmix(1)
    unmix(3)
    step(g3)
    unmix(2)
    net.send(GC.at[1:5, :, 0:8], GC.at[pl.ds(p.yl, 4), :, 128:136], halo, p.at(y=p.y + 1 - 2 * p.yl))
    pf_in()
    r4 = ReduceRing(net, PV, MR, *ring_a)
    for j in (2, 1, 3, 0):
        r4.push(j)
    r4_mine, r4 = r4.mine, r4.rest()
    step(ja)
    for who in partners:
        pl.semaphore_signal(free, inc=1, device_id=who, device_id_type=MESH)
    step(r4)
    step(jd)
    net.got(GC.at[pl.ds(1 - p.yl, 4), :, 128:136], halo)

    P1 = GO
    r3 = ReduceRing(net, P1, R1, *ring_b)

    def unproject(j):
        zj = block(j)
        for cc in range(2):
            at = slice(128 * cc, 128 * cc + 128)
            gb = taps[0] * GC[zj + 1, cc, 0:128] + taps[1] * GC[zj + 1, cc, 1:129] + taps[2] * GC[zj + 1, cc, 2:130]
            bb, vv = gb * V[zj, cc], gb * B[zj, cc]
            GGU[zj, at, 0:128] = bb[:, :128].astype(BF)
            GGU[zj, at, 256:384] = vv[:, :128].astype(BF)
            GGU[zj, at, 384:512] = jnp.zeros((128, 128), BF)
            GGU[zj, at, 512:640] = (GGU[zj, at, 512:640].astype(F32) + bb[:, 128:]).astype(BF)
            GGU[zj, at, 640:768] = pltpu.roll(vv[:, 128:], 64, 1).astype(BF)
        P1[zj] = dot(GGU[zj, :, 0:768], whole(WC), NT).astype(BF).reshape(2, 128, D)
        r3.push(j)

    unproject(2)
    step(r4)
    unproject(1)
    unproject(3)
    unproject(0)
    r3_mine, r3 = r3.mine, r3.rest()
    step(r3)
    step(jb)
    n1_in()
    DC = DA.at[:, :, :, :, 0:768]
    for x0 in range(4):
        at = slice(384 * x0, 384 * x0 + 384)
        w = dot(N[:, :, :, at].reshape(1024, 384), GGU[:, :, 0:768].reshape(1024, 768), TN)
        m = dot(BR[:, :, :, at].reshape(1024, 384), MX[...].reshape(1024, 256), TN)
        w = jnp.concatenate([w[:, :384], m[:, :128], w[:, 512:640], w[:, 640:] + m[:, 128:]], axis=1)
        DC[x0] = w.astype(BF).reshape(2, 2, 96, 768)
        if x0 == 1:
            step(r3)
    tile = jnp.concatenate([KP[...], jnp.zeros((24, 256), F32)], axis=0).astype(BF)
    for s in range(16):
        KG[s // 4, (s // 2) % 2, s % 2] = tile
    pl.semaphore_wait(free, len(partners))
    jc = reduce_plane(net, DC, SC, *[r.at[(slice(None),) * (len(r.shape) - 1) + (slice(0, 768),)] for r in sa])
    jk = reduce_plane(net, KG, SK, *sk)
    step(jc), step(jk)
    step(r4)
    step(r3)
    step(jd)
    step(jc), step(jk)
    step(r4)
    step(r3)
    step(jc), step(jk)

    def last(i, _):
        at = pl.ds(pl.multiple_of(i * 32, 32), 32)
        layer_out[at] = (live[at, 0:1] * (resid[at] + MR[at])).astype(BF)
        v = tok[at].astype(F32)
        inv = lax.rsqrt(jnp.mean(v * v, axis=1, keepdims=True) + epsilon)
        x = v * inv
        w = g_mix * R1[at]
        g = GR[at] + inv * (w - x * jnp.mean(w * x, axis=1, keepdims=True))
        tokens_grad[at] = g.astype(BF)

    lax.fori_loop(0, ROWS // 32, last, None)
    step(jd), step(jb), step(ja)
    ffn_share = jnp.sum(SA[...] * gu_s[:, 0:1024].astype(F32), axis=1, keepdims=True)
    ffn_share += jnp.sum(SB_[...] * gu_s[:, 1024:1792].astype(F32), axis=1, keepdims=True)
    for t in range(7):
        n = 96 if t == 6 else 128
        src, at = (SA, 256 * t) if t < 4 else (SB_, 256 * t - 1024)
        gate[:, 128 * t : 128 * t + n] = src[:, at : at + n]
        up[:, 128 * t : 128 * t + n] = src[:, at + 128 : at + 128 + n]
    down_t[...] = SD[:, :FB]
    step(jc), step(jk)
    step(jc), step(jk)
    half = lax.broadcasted_iota(jnp.int32, (96, 128), 1) < 64
    for i in range(3):
        in3[i, :, 0:128] = SC[:, 128 * i : 128 * i + 128]
    in3[0, :, 128:192] = SC[:, 512:576]
    in3[1, :, 128:192] = pltpu.roll(SC[:, 512:640], 64, 1)[:, :64]
    in3[2, :, 128:192] = pltpu.roll(SC[:, 640:768], 64, 1)[:, :64]
    out_t[:, 0:128] = SC[:, 384:512]
    out_t[:, 128:192] = SC[:, 640:704]
    mix = SC[...] * conv_s[...].astype(F32)
    mix_share = jnp.sum(mix[:, :384], axis=1, keepdims=True) + jnp.sum(
        mix[:, 512:640] + jnp.where(half, 0.0, mix[:, 640:]), axis=1, keepdims=True
    )
    lane = lax.broadcasted_iota(jnp.int32, (96, 128), 1)
    shares[...] = jnp.where(lane == 0, mix_share / gcol[:, 0:1], ffn_share / gcol[:, 1:2])
    taps_out[...] = SK[0:8]
    for job in (r2, r3, r4, g3, ja, jb, jd, jc, jk):
        assert next(job, "end") == "end"
    net.finish(r3_mine + r4_mine)
    net.finish()


def backward_call(*args):
    any_, vm = pl.BlockSpec(memory_space=pl.ANY), pl.BlockSpec(memory_space=pltpu.VMEM)
    ring = (4, 2, ROWS, D)
    outs = [shape((ROWS, D)), shape((ROWS, D)), shape((3, 96, CH), F32), shape((96, CH), F32)]
    outs += [shape((96, FB), F32)] * 3 + [shape((96, 128), F32), shape((8, 256), F32)]
    v = lambda s, t=BF: pltpu.VMEM(s, t)
    wide = (4, 2, ROWS, 256)
    scratch = [v(ring), v(ring), v((4, 256, 1792)), v(ring), v((4, 256, FP))]
    scratch += [v(wide, F32)] * 3 + [v((4, 2, 136, 256), F32), v(wide), v((4, 2, 2, 96, 768)), v(ring)]
    scratch += [v((5, 2, 136, 256), F32)] + [v((4, 2, 2, 96, n)) for n in (1024, 768, FP)] + [v((8, 256), F32)]
    scratch += plane_scratch(1024) + plane_scratch(768) + plane_scratch(FP) + plane_scratch(256, 16)
    scratch += ring_scratch(D) * 2 + [v((4, 2, 2, 32, 256))]
    scratch += [v((ROWS, D), F32)] * 3 + [v((96, n), F32) for n in (1024, 768, FP, 768)] + [v((32, 256), F32)]
    scratch += [pltpu.SemaphoreType.REGULAR]
    scratch += [pltpu.SemaphoreType.DMA((200,)), pltpu.SemaphoreType.DMA((200,)), pltpu.SemaphoreType.DMA((24,))]
    return pl.pallas_call(
        backward_kernel,
        out_shape=tuple(outs),
        in_specs=[vm] * 8 + [any_] * 13,
        out_specs=tuple([vm] * 9),
        scratch_shapes=scratch,
        compiler_params=pltpu.CompilerParams(
            collective_id=1, has_side_effects=True, vmem_limit_bytes=64 << 20),
        name="backward",
    )(*args)


def per_device(tokens, gain_mix, in_weight, conv_kernel, out_weight, gain_ffn, gate_weight, up_weight, down_weight, lengths, cotangent):
    dp, t = lax.axis_index("dp"), lax.axis_index("tensor")
    position = t * ROWS + jnp.arange(ROWS)
    live = (position < lengths[0]).astype(F32)[:, None]
    b, cg, v = in_weight[:, 0], in_weight[:, 1], in_weight[:, 2]
    o = out_weight.T
    conv_pack = jnp.concatenate(
        [b[:, :128], cg[:, :128], v[:, :128], o[:, :128], b[:, 128:], cg[:, 128:], o[:, 128:], v[:, 128:]],
        axis=1,
    )
    wide = lambda w: jnp.pad(w, ((0, 0), (0, FP - FB)))
    gu_pack = jnp.stack([wide(gate_weight).reshape(96, 7, 128), wide(up_weight).reshape(96, 7, 128)], axis=2)
    gu_pack = gu_pack.reshape(96, 1792)
    down_pack = wide(down_weight.T)
    small = jnp.zeros((32, 256), BF)
    off = (96 * dp) % 128
    small = lax.dynamic_update_slice(small, jnp.stack([gain_mix, gain_ffn]), (0, off))
    small = lax.dynamic_update_slice(small, conv_kernel, (16, 0))
    grad_out = (live * cotangent.astype(F32)).astype(BF)
    gcol = jnp.pad(jnp.stack([gain_mix, gain_ffn], axis=1).astype(F32), ((0, 0), (0, 126)), constant_values=1.0)
    live_wide = jnp.broadcast_to(live, (ROWS, 128))

    (n1, n2, go, ggu, hid, bv, cv, vv, bxv, mx, wc, pg, pf, resid, gains) = (
        forward_call(tokens, grad_out, conv_pack, gu_pack, down_pack, small)
    )
    layer_out, tokens_grad, in3, out_t, gate_grad, up_grad, down_t, shares, taps = backward_call(
        tokens, grad_out, live_wide, resid, gains, conv_pack, gu_pack, gcol,
        pg, n2, ggu, go, hid, pf, n1, bv, cv, vv, bxv, mx, wc)
    sums = lax.psum_scatter(shares[:, :2].T.reshape(2, 8, 12), "tensor", scatter_dimension=1)
    mine = lax.dynamic_slice(taps[:3, :CH].reshape(3, 16, 12), (0, dp, 0), (3, 1, 12)).reshape(3, 12)
    move = [(i, (i % 8) * 16 + i // 8) for i in range(128)]
    kernel_grad = lax.ppermute(mine, ("dp", "tensor"), move)
    return (
        layer_out,
        tokens_grad,
        sums[0],
        in3.transpose(1, 0, 2),
        kernel_grad,
        out_t.T,
        sums[1],
        gate_grad,
        up_grad,
        down_t.T,
    )


def solution(mesh):
    placed = (
        P(("dp", "tensor"), None),
        P("dp"),
        P("dp", None, "tensor"),
        P(None, "tensor"),
        P("tensor", "dp"),
        P("dp"),
        P("dp", "tensor"),
        P("dp", "tensor"),
        P("tensor", "dp"),
        P("dp"),
        P(("dp", "tensor"), None),
    )
    return jax.shard_map(
        per_device,
        mesh=mesh,
        in_specs=placed,
        out_specs=(
            P(("dp", "tensor"), None),
            P(("dp", "tensor"), None),
            P(("dp", "tensor")),
            P("dp", None, "tensor"),
            P(None, ("dp", "tensor")),
            P("tensor", "dp"),
            P(("dp", "tensor")),
            P("dp", "tensor"),
            P("dp", "tensor"),
            P("tensor", "dp"),
        ),
        check_vma=False,
    )
```

```python
import functools

import jax
import jax.numpy as jnp
from jax import lax
from jax.experimental import pallas as pl
from jax.experimental.pallas import tpu as pltpu
from jax.sharding import PartitionSpec as P

epsilon = 1e-05
MESH = pl.DeviceIdType.MESH
BF = jnp.bfloat16
F32 = jnp.float32
D = 1536
ROWS = 128
CH = 192
FB = 864
FP = 896
HALF = 48
VMEM_LIMIT = 60 << 20


class Place:
    def __init__(self):
        dp = lax.axis_index("dp")
        t = lax.axis_index("tensor")
        self.x, self.yh, self.c = dp // 4, (dp // 2) % 2, dp % 2
        self.z, self.yl = t // 2, t % 2
        self.y = self.yh * 2 + self.yl
        self.o = 1 - self.c
        self.xp, self.xm, self.x2 = (self.x + 1) % 4, (self.x + 3) % 4, (self.x + 2) % 4
        self.yp, self.ym = (self.y + 1) % 4, (self.y + 3) % 4
        self.yhp, self.yhm = self.yp // 2, self.ym // 2
        self.way = 1 - 2 * self.c
        self.zf = (self.z + self.way + 4) % 4
        self.zb = (self.z - self.way + 4) % 4
        self.zp, self.zm, self.z2 = (self.z + 1) % 4, (self.z + 3) % 4, (self.z + 2) % 4
        self.own = self.c == self.yl
        self.opp = self.c != self.yl

    def at(self, x=None, y=None, z=None, c=None):
        x = self.x if x is None else x
        y = self.y if y is None else y
        z = self.z if z is None else z
        c = self.c if c is None else c
        return (x * 4 + (y // 2) * 2 + c, z * 2 + y % 2)


class Net:
    def __init__(self, place, send, recv, local=None):
        self.p, self.ss, self.rs, self.ls = place, send, recv, local
        self.ns = self.nr = self.nl = 0
        self.pending = []

    def sem(self, n=1):
        k = self.nr
        self.nr += n
        return k

    def send(self, src, dst, recv_index, target, cond=None, pending=None):
        k = self.ns
        self.ns += 1
        d = pltpu.make_async_remote_copy(
            src_ref=src, dst_ref=dst, send_sem=self.ss.at[k], recv_sem=self.rs.at[recv_index],
            device_id=target, device_id_type=MESH)
        run(cond, d.start)
        (self.pending if pending is None else pending).append((cond, d))

    def copy(self, src, dst, cond=None):
        k = self.nl
        self.nl += 1
        d = pltpu.make_async_copy(src, dst, self.ls.at[k])
        run(cond, d.start)
        return lambda: run(cond, d.wait)

    def got(self, dst, recv_index, cond=None):
        d = pltpu.make_async_remote_copy(
            src_ref=dst, dst_ref=dst, send_sem=self.ss.at[0], recv_sem=self.rs.at[recv_index],
            device_id=self.p.at(c=self.p.o), device_id_type=MESH)
        run(cond, d.wait_recv)

    def finish(self, pending=None):
        pending = self.pending if pending is None else pending
        for cond, d in pending:
            run(cond, d.wait_send)
        pending.clear()


def run(cond, f):
    if cond is None:
        f()
    else:
        pl.when(cond)(f)


def greet(p, plane, ring, group=False):
    bar = pltpu.get_barrier_semaphore()
    who = [p.at(c=p.o)]
    if plane:
        for c in (0, 1):
            who += [p.at(x=p.xp, c=c), p.at(x=p.xm, c=c), p.at(y=p.yp, c=c), p.at(y=p.ym, c=c)]
    if group:
        me = lax.axis_index("tensor")
        who += [(lax.axis_index("dp"), (me + i) % 8) for i in range(1, 8)]
    elif ring:
        who += [p.at(z=p.zp), p.at(z=p.zm)]
    for w in who:
        pl.semaphore_signal(bar, inc=1, device_id=w, device_id_type=MESH)
    return lambda: pl.semaphore_wait(bar, len(who))


def add(out, *terms):
    lead = out.shape[:-2]
    count = 1
    for s in lead:
        count *= s

    def one(i):
        at = []
        for s in reversed(lead):
            at.append(i % s)
            i = i // s
        at = tuple(reversed(at))
        v = terms[0][at].astype(F32) if at else terms[0][...].astype(F32)
        for t in terms[1:]:
            v = v + (t[at] if at else t[...]).astype(F32)
        if at:
            out[at] = v.astype(out.dtype)
        else:
            out[...] = v.astype(out.dtype)

    if not lead:

        def rows(i, _):
            at = pl.ds(pl.multiple_of(i * 16, 16), 16)
            v = terms[0][at].astype(F32)
            for t in terms[1:]:
                v = v + t[at].astype(F32)
            out[at] = v.astype(out.dtype)

        lax.fori_loop(0, out.shape[0] // 16, rows, None)
    else:
        lax.fori_loop(0, count, lambda i, _: one(i), None)


def ring_scratch(n):
    return [pltpu.VMEM((4, ROWS, n), BF), pltpu.VMEM((2, ROWS, n), BF), pltpu.VMEM((3, ROWS, n), BF)]


def shape(s, t=BF):
    return jax.ShapeDtypeStruct(s, t)


def slots(n):
    return shape((4, 2, 2, 96, n))


def gather_plane(net, sh, W, mine):
    p = net.p
    send = functools.partial(net.send, pending=mine)
    h = sh.shape[0] // 2
    HA, HB = pl.ds(0, h), pl.ds(h, h)
    i_own, f1, f2, f3, f4 = net.sem(), net.sem(2), net.sem(2), net.sem(2), net.sem(2)
    r1, r2, r3, r4, y1, y2, y3, y4, x1, x2, x3, x4 = (net.sem() for _ in range(12))
    q = p.yl
    done = net.copy(sh, W.at[p.x, p.yh, p.c], p.own)
    send(sh.at[HA], W.at[p.x, p.yh, p.c, HA], f1 + p.c, p.at(x=p.xp, c=q))
    send(sh.at[HA], W.at[p.x, p.yh, p.c, HA], f2 + p.c, p.at(x=p.xm, c=q))
    send(sh.at[HB], W.at[p.x, p.yh, p.c, HB], f3 + p.c, p.at(y=p.yp, c=q))
    send(sh.at[HB], W.at[p.x, p.yh, p.c, HB], f4 + p.c, p.at(y=p.ym, c=q))
    send(sh, W.at[p.x, p.yh, p.c], i_own, p.at(c=p.o), p.opp)
    yield
    net.got(W.at[p.xm, p.yh, 0, HA], f1 + 0, p.own)
    net.got(W.at[p.x, p.yhm, 0, HB], f3 + 0, p.opp)
    send(W.at[p.xm, p.yh, 0, HA], W.at[p.xm, p.yh, 0, HA], r1, p.at(x=p.xp), p.own)
    send(W.at[p.x, p.yhm, 0, HB], W.at[p.x, p.yhm, 0, HB], r3, p.at(y=p.yp), p.opp)
    net.got(W.at[p.xp, p.yh, 1, HA], f2 + 1, p.own)
    net.got(W.at[p.x, p.yhp, 1, HB], f4 + 1, p.opp)
    send(W.at[p.xp, p.yh, 1, HA], W.at[p.xp, p.yh, 1, HA], r2, p.at(x=p.xm), p.own)
    send(W.at[p.x, p.yhp, 1, HB], W.at[p.x, p.yhp, 1, HB], r4, p.at(y=p.ym), p.opp)
    yield
    done()
    net.got(W.at[p.x, p.yh, p.o], i_own, p.own)
    net.got(W.at[p.xm, p.yh, 1, HA], f1 + 1, p.own)
    net.got(W.at[p.xp, p.yh, 0, HA], f2 + 0, p.own)
    net.got(W.at[p.x, p.yhm, 1, HB], f3 + 1, p.opp)
    net.got(W.at[p.x, p.yhp, 0, HB], f4 + 0, p.opp)
    net.got(W.at[p.x2, p.yh, 0, HA], r1, p.own)
    net.got(W.at[p.x2, p.yh, 1, HA], r2, p.own)
    send(W.at[:, p.yh, :, HA], W.at[:, p.yh, :, HA], y1, p.at(y=p.yp), p.own)
    send(W.at[:, p.yh, :, HA], W.at[:, p.yh, :, HA], y2, p.at(y=p.ym), p.own)
    net.got(W.at[p.x, 1 - p.yh, 0, HB], r3, p.own)
    net.got(W.at[p.x, 1 - p.yh, 1, HB], r4, p.own)
    send(W.at[p.x, :, :, HB], W.at[p.x, :, :, HB], x1, p.at(x=p.xp))
    send(W.at[p.x, :, :, HB], W.at[p.x, :, :, HB], x2, p.at(x=p.xm))
    yield
    net.got(W.at[p.xm, :, :, HB], x1)
    send(W.at[p.xm, :, 0, HB], W.at[p.xm, :, 0, HB], x3, p.at(x=p.xp))
    net.got(W.at[p.xp, :, :, HB], x2)
    send(W.at[p.xp, :, 1, HB], W.at[p.xp, :, 1, HB], x4, p.at(x=p.xm))
    net.got(W.at[:, p.yhm, :, HA], y1, p.opp)
    send(W.at[:, p.yhm, 0, HA], W.at[:, p.yhm, 0, HA], y3, p.at(y=p.yp), p.opp)
    net.got(W.at[:, p.yhp, :, HA], y2, p.opp)
    send(W.at[:, p.yhp, 1, HA], W.at[:, p.yhp, 1, HA], y4, p.at(y=p.ym), p.opp)
    yield
    net.got(W.at[:, 1 - p.yh, 0, HA], y3, p.own)
    net.got(W.at[:, 1 - p.yh, 1, HA], y4, p.own)
    net.got(W.at[p.x2, :, 0, HB], x3)
    net.got(W.at[p.x2, :, 1, HB], x4)


PARTS = [pl.ds(0, 64), pl.ds(64, 64)]


def gather_ring(net, a, out, mine, late=False):
    p = net.p
    send = functools.partial(net.send, pending=mine)
    s1, s3, s2 = net.sem(2), net.sem(2), net.sem(2)
    k = net.sem(8)
    jf, jb = (p.zf - p.z + 4) % 4, (p.zb - p.z + 4) % 4
    for i, r in enumerate(PARTS):
        send(a.at[r], out.at[p.z, p.c, r], s1 + i, p.at(z=p.zf))
        send(a.at[r], out.at[p.z, p.c, r], s3 + i, p.at(z=p.zb))
    for i, r in enumerate(PARTS):
        send(a.at[r], out.at[p.z, p.c, r], k + 4 * i, p.at(c=p.o))
    yield
    for i, r in enumerate(PARTS):
        net.got(out.at[p.z, p.o, r], k + 4 * i)
    yield
    for i, r in enumerate(PARTS):
        net.got(out.at[p.zb, p.c, r], s1 + i)
        if not late:
            send(out.at[p.zb, p.c, r], out.at[p.zb, p.c, r], s2 + i, p.at(z=p.zf))
        send(out.at[p.zb, p.c, r], out.at[p.zb, p.c, r], k + 4 * i + jb, p.at(c=p.o))
        net.got(out.at[p.zf, p.c, r], s3 + i)
        send(out.at[p.zf, p.c, r], out.at[p.zf, p.c, r], k + 4 * i + jf, p.at(c=p.o))
    yield
    for i, r in enumerate(PARTS):
        net.got(out.at[p.zp, p.o, r], k + 4 * i + 1)
        net.got(out.at[p.zm, p.o, r], k + 4 * i + 3)
    yield
    if late:
        for i, r in enumerate(PARTS):
            send(out.at[p.zb, p.c, r], out.at[p.zb, p.c, r], s2 + i, p.at(z=p.zf))
        yield
    for i, r in enumerate(PARTS):
        net.got(out.at[p.z2, p.c, r], s2 + i)
        send(out.at[p.z2, p.c, r], out.at[p.z2, p.c, r], k + 4 * i + 2, p.at(c=p.o))
    for i, r in enumerate(PARTS):
        net.got(out.at[p.z2, p.o, r], k + 4 * i + 2)


class ReduceRing:
    def __init__(self, net, V, out, RC, SB, RZ):
        self.net, self.V, self.out, self.RC, self.SB, self.RZ = net, V, out, RC, SB, RZ
        self.s2, self.sd, self.sr, self.k = net.sem(2), net.sem(2), net.sem(2), net.sem(8)
        self.mine = []
        self.send = functools.partial(net.send, pending=self.mine)

    def push(self, j):
        p = self.net.p
        for i, r in enumerate(PARTS):
            self.send(self.V.at[(p.z + j) % 4, p.o, r], self.RC.at[j, r], self.k + 4 * i + j, p.at(c=p.o))

    def rest(self):
        net, p, V, RC, SB, RZ, k = self.net, self.net.p, self.V, self.RC, self.SB, self.RZ, self.k
        jf, jb = (p.zf - p.z + 4) % 4, (p.zb - p.z + 4) % 4
        for i, r in enumerate(PARTS):
            net.got(RC.at[2, r], k + 4 * i + 2)
            add(SB.at[0, r], V.at[p.z2, p.c, r], RC.at[2, r])
            self.send(SB.at[0, r], RZ.at[0, r], self.s2 + i, p.at(z=p.zf))
        yield
        for i, r in enumerate(PARTS):
            net.got(RC.at[jb, r], k + 4 * i + jb)
            add(SB.at[1, r], V.at[p.zb, p.c, r], RC.at[jb, r])
            self.send(SB.at[1, r], RZ.at[1, r], self.sd + i, p.at(z=p.zb))
        for i, r in enumerate(PARTS):
            net.got(RC.at[jf, r], k + 4 * i + jf)
            add(RC.at[jf, r], V.at[p.zf, p.c, r], RC.at[jf, r])
        yield
        for i, r in enumerate(PARTS):
            net.got(RZ.at[0, r], self.s2 + i)
            add(RC.at[jf, r], RC.at[jf, r], RZ.at[0, r])
            self.send(RC.at[jf, r], RZ.at[2, r], self.sr + i, p.at(z=p.zf))
        for i, r in enumerate(PARTS):
            net.got(RC.at[0, r], k + 4 * i)
            add(RC.at[0, r], V.at[p.z, p.c, r], RC.at[0, r])
        yield
        for i, r in enumerate(PARTS):
            net.got(RZ.at[1, r], self.sd + i)
            net.got(RZ.at[2, r], self.sr + i)
            add(self.out.at[r], RC.at[0, r], RZ.at[1, r], RZ.at[2, r])


def step(job, times=1):
    for _ in range(times):
        next(job, None)


def dot(a, b, dims):
    return lax.dot_general(a, b, (dims, ((), ())), preferred_element_type=F32)


NN, NT, TN = ((1,), (0,)), ((1,), (1,)), ((0,), (0,))


def whole(ref, columns=slice(None)):
    v = ref[:, :, :, :, columns]
    return v.reshape(D, v.shape[-1])


def row_norm(src, dst, gain, rows=32):
    def one(i, _):
        at = pl.ds(pl.multiple_of(i * rows, rows), rows)
        v = src[at].astype(F32)
        inv = lax.rsqrt(jnp.mean(v * v, axis=1, keepdims=True) + epsilon)
        dst[at] = (v * inv * gain).astype(dst.dtype)

    lax.fori_loop(0, ROWS // rows, one, None)


def live_rows(lens):
    at = lax.axis_index("tensor") * ROWS + lax.broadcasted_iota(jnp.int32, (ROWS, 1), 0)
    return jnp.where(at < lens[...], 1.0, 0.0).astype(F32)


def plane_scratch(n, h=HALF):
    return [
        pltpu.VMEM((2, 4, h, n), BF),
        pltpu.VMEM((2, 4, 2, h, n), BF),
        pltpu.VMEM((2, h, n), BF),
        pltpu.VMEM((3, h, n), BF),
        pltpu.VMEM((2, 2, h, n), BF),
        pltpu.VMEM((2, 2, 2, h, n), BF),
        pltpu.VMEM((2, h, n), BF),
        pltpu.VMEM((3, h, n), BF),
    ]


def reduce_plane(net, G, out, RA, RB, RC, F, RX, RY, RZ, H):
    p = net.p
    h = out.shape[0] // 2
    HA, HB = pl.ds(0, h), pl.ds(h, h)
    mine = []
    send = functools.partial(net.send, pending=mine)
    a0, a1, bp0, bp1, bm0, bm1, c0, c1, g0, g1, g2 = (net.sem() for _ in range(11))
    u0, u1, vp0, vp1, vm0, vm1, w0, w1, h0, h1, h2 = (net.sem() for _ in range(11))
    send(G.at[:, 1 - p.yh, 0, HA], RA.at[0], a0, p.at(y=p.ym), p.own)
    send(G.at[:, 1 - p.yh, 1, HA], RA.at[1], a1, p.at(y=p.yp), p.own)
    send(G.at[p.x2, :, 0, HB], RX.at[0], u0, p.at(x=p.xm))
    send(G.at[p.x2, :, 1, HB], RX.at[1], u1, p.at(x=p.xp))
    send(G.at[:, p.yhm, 1, HA], RB.at[0, :, 1], bp1, p.at(y=p.ym), p.opp)
    send(G.at[:, p.yhp, 0, HA], RB.at[1, :, 0], bm0, p.at(y=p.yp), p.opp)
    send(G.at[p.xm, :, 1, HB], RY.at[0, :, 1], vp1, p.at(x=p.xm))
    send(G.at[p.xp, :, 0, HB], RY.at[1, :, 0], vm0, p.at(x=p.xp))
    yield

    net.got(RX.at[0], u0)
    add(RX.at[0], RX.at[0], G.at[p.xm, :, 0, HB])
    send(RX.at[0], RY.at[0, :, 0], vp0, p.at(x=p.xm))
    net.got(RX.at[1], u1)
    add(RX.at[1], RX.at[1], G.at[p.xp, :, 1, HB])
    send(RX.at[1], RY.at[1, :, 1], vm1, p.at(x=p.xp))
    net.got(RA.at[0], a0, p.opp)
    net.got(RA.at[1], a1, p.opp)

    @pl.when(p.opp)
    def _():
        add(RA.at[0], RA.at[0], G.at[:, p.yhm, 0, HA])
        add(RA.at[1], RA.at[1], G.at[:, p.yhp, 1, HA])

    send(RA.at[0], RB.at[0, :, 0], bp0, p.at(y=p.ym), p.opp)
    send(RA.at[1], RB.at[1, :, 1], bm1, p.at(y=p.yp), p.opp)
    yield

    net.got(RY.at[0, :, 1], vp1)
    net.got(RY.at[1, :, 0], vm0)
    net.got(RY.at[0, :, 0], vp0)
    net.got(RY.at[1, :, 1], vm1)
    add(RY.at[0], RY.at[0], RY.at[1], G.at[p.x, :, :, HB])
    T = RY.at[0]
    send(T.at[1 - p.yh, 0], RZ.at[0], w0, p.at(y=p.ym), p.own)
    send(T.at[1 - p.yh, 1], RZ.at[1], w1, p.at(y=p.yp), p.own)
    send(T.at[p.yhm, 1], H.at[1], h1, p.at(y=p.ym, c=1), p.opp)
    send(T.at[p.yhp, 0], H.at[2], h2, p.at(y=p.yp, c=0), p.opp)
    send(T.at[p.yh, p.o], H.at[0], h0, p.at(c=p.o), p.own)

    net.got(RB.at[0, :, 1], bp1, p.own)
    net.got(RB.at[1, :, 0], bm0, p.own)
    net.got(RB.at[0, :, 0], bp0, p.own)
    net.got(RB.at[1, :, 1], bm1, p.own)

    @pl.when(p.own)
    def _():
        add(RB.at[0], RB.at[0], RB.at[1], G.at[:, p.yh, :, HA])

    S = RB.at[0]
    send(S.at[p.x2, 0], RC.at[0], c0, p.at(x=p.xm), p.own)
    send(S.at[p.x2, 1], RC.at[1], c1, p.at(x=p.xp), p.own)
    send(S.at[p.xm, 1], F.at[1], g1, p.at(x=p.xm, c=1), p.own)
    send(S.at[p.xp, 0], F.at[2], g2, p.at(x=p.xp, c=0), p.own)
    send(S.at[p.x, p.o], F.at[0], g0, p.at(c=p.o), p.own)
    yield

    net.got(RC.at[0], c0, p.own)
    net.got(RC.at[1], c1, p.own)
    net.got(RZ.at[0], w0, p.opp)
    net.got(RZ.at[1], w1, p.opp)

    @pl.when(p.own)
    def _():
        add(RC.at[0], RC.at[0], S.at[p.xm, 0])
        add(RC.at[1], RC.at[1], S.at[p.xp, 1])

    @pl.when(p.opp)
    def _():
        add(RZ.at[0], RZ.at[0], T.at[p.yhm, 0])
        add(RZ.at[1], RZ.at[1], T.at[p.yhp, 1])

    send(RC.at[0], F.at[1], g1, p.at(x=p.xm, c=0), p.own)
    send(RC.at[1], F.at[2], g2, p.at(x=p.xp, c=1), p.own)
    send(RZ.at[0], H.at[1], h1, p.at(y=p.ym, c=0), p.opp)
    send(RZ.at[1], H.at[2], h2, p.at(y=p.yp, c=1), p.opp)
    yield

    net.got(F.at[0], g0, p.opp)
    net.got(F.at[1], g1)
    net.got(F.at[2], g2)
    net.got(H.at[0], h0, p.opp)
    net.got(H.at[1], h1)
    net.got(H.at[2], h2)
    net.finish(mine)

    @pl.when(p.own)
    def _():
        F[0] = S[p.x, p.c]
        H[0] = T[p.yh, p.c]

    add(out.at[HA], F.at[0], F.at[1], F.at[2])
    add(out.at[HB], H.at[0], H.at[1], H.at[2])


def train_kernel(*refs):
    (tok, cot, lens, in_w, out_w, gate_w, up_w, down_w, gm_w, gf_w, taps_w,
     resid, gains, GR, MR, R1, SA, SB_, SD, SC, XR, spill,
     gout, conv_s, gu_s, down_s, small_s, flip, T, N, GO, WC, WG, WD, SM, B, C, V, BX, MX, GC, HID, GGU, PA, DD, KP,
     *more) = refs
    sa, sb, sd, sk, ring_a, ring_b = [more[8 * i : 8 * i + 8] for i in range(4)] + [more[32:35], more[35:38]]
    KG, X, SK, free, send, recv, local = more[38:]
    p = Place()
    BX[0, :, 0:8] = jnp.zeros((2, 8, 256), F32)
    GC[4, :, 128:136] = jnp.zeros((2, 8, 256), F32)
    greeted = greet(p, True, True, True)
    net = Net(p, send, recv, local)
    block = lambda j: (p.z + j) % 4
    halo, halo_back = net.sem(), net.sem()
    partners = [p.at(c=p.o)]
    for cc in (0, 1):
        partners += [p.at(x=p.xp, c=cc), p.at(x=p.xm, c=cc), p.at(y=p.yp, c=cc), p.at(y=p.ym, c=cc)]

    WA, WB = WG.at[:, :, :, :, 0:GA_N], WG.at[:, :, :, :, GA_N:]
    gt_sent, go_sent, g2_sent, g3_sent, gu_sent, w_sent = [], [], [], [], [], []
    gt = gather_ring(net, tok, T, gt_sent)
    go = gather_ring(net, gout, GO, go_sent, True)
    am = gather_plane(net, small_s, SM, w_sent)
    ac = gather_plane(net, conv_s.at[:, 0:384], WC.at[:, :, :, :, 0:384], w_sent)
    ae = gather_plane(net, conv_s.at[:, 384:768], WC.at[:, :, :, :, 384:768], w_sent)
    ad = gather_plane(net, down_s, WD, w_sent)
    au = gather_plane(net, gu_s.at[:, 0:GA_N], WA, gu_sent)
    av = gather_plane(net, gu_s.at[:, GA_N:], WB, gu_sent)

    flip[0:256] = jnp.zeros((256, 128), F32)
    flip[0:CH, 0:96] = out_w[...].astype(F32)
    o = flip[0:256].T[0:96]
    side = jnp.zeros((96, 64), F32)
    w = [jnp.concatenate([in_w[i].astype(F32), side], axis=1) for i in range(3)]
    parts = [
        w[0][:, 0:128],
        w[1][:, 0:128],
        w[2][:, 0:128],
        o[:, 0:128],
        w[0][:, 128:256] + pltpu.roll(w[1][:, 128:256], 64, 1),
        o[:, 128:256] + pltpu.roll(w[2][:, 128:256], 64, 1),
    ]
    conv_s[...] = jnp.concatenate(parts, axis=1).astype(BF)
    wide_row = lambda g: jnp.concatenate([g[...].astype(F32), jnp.zeros((1, 160), F32)], axis=1)
    gain = jnp.concatenate([wide_row(gm_w), wide_row(gf_w), jnp.zeros((6, 256), F32)], axis=0)
    small_s[0:16] = jnp.concatenate(
        [pltpu.roll(gain, lax.rem(96 * lax.axis_index("dp"), 128), 1), jnp.zeros((8, 256), F32)], axis=0
    ).astype(BF)
    taps_row = jnp.concatenate([taps_w[...].astype(F32), jnp.zeros((3, 64), F32)], axis=1)
    small_s[16:32] = jnp.concatenate([taps_row, jnp.zeros((13, 256), F32)], axis=0).astype(BF)
    greeted()
    step(gt)
    step(am), step(ac), step(ae)
    live = live_rows(lens)
    gout[...] = (live * cot[...].astype(F32)).astype(BF)
    down_s[:, 768:FP] = jnp.zeros((96, 128), BF)
    down_s[:, 0:FB] = down_w[...]
    for t in range(7):
        n = 96 if t == 6 else 128
        if t == 6:
            gu_s[:, 1536:1792] = jnp.zeros((96, 256), BF)
        gu_s[:, 256 * t : 256 * t + n] = gate_w[:, 128 * t : 128 * t + n]
        gu_s[:, 256 * t + 128 : 256 * t + 128 + n] = up_w[:, 128 * t : 128 * t + n]
    own_tok = net.copy(tok, T.at[p.z, p.c])
    own_gout = net.copy(gout, GO.at[p.z, p.c])
    step(am), step(ac), step(ae)
    step(au)
    step(am), step(ac), step(ae)
    step(av), step(ad)
    step(gt, 2)
    step(au), step(av), step(ad)
    step(am), step(ac), step(ae)
    step(go)
    step(gt)
    step(au)
    step(am)
    gains[...] = jnp.zeros(gains.shape, F32)
    for s in range(16):
        piece = SM[s // 4, (s // 2) % 2, s % 2, 0:16].astype(F32)
        at = (96 * s) // 128 * 128
        n = min(256, gains.shape[1] - at)
        gains[0:16, at : at + n] = gains[0:16, at : at + n] + piece[:, :n]
    gains[16:32, 0:256] = SM[0, 0, 0, 16:32].astype(F32)
    g_mix, g_ffn = gains[0:1, :D], gains[1:2, :D]
    taps = [gains[16 + i : 17 + i, 0:256] for i in range(3)]
    own_tok()
    step(ac), step(ae)
    lanes = lax.broadcasted_iota(jnp.int32, (256, 128), 1) < 64

    def project(j):
        zj = block(j)
        for cc in range(2):
            row_norm(T.at[zj, cc], N.at[zj, cc], g_mix)
        r = dot(N[zj].reshape(256, D), whole(WC), NN)
        b1 = jnp.where(lanes, r[:, 512:640], 0.0)
        c1 = jnp.where(lanes, pltpu.roll(r[:, 512:640], 64, 1), 0.0)
        v1 = jnp.where(lanes, pltpu.roll(r[:, 640:768], 64, 1), 0.0)
        b = jnp.concatenate([r[:, 0:128], b1], axis=1)
        v = jnp.concatenate([r[:, 256:384], v1], axis=1)
        BX[zj, :, 8:136] = (b * v).reshape(2, 128, 256)
        B[zj] = b.astype(BF).reshape(2, 128, 256)
        V[zj] = v.astype(BF).reshape(2, 128, 256)
        C[zj] = jnp.concatenate([r[:, 128:256], c1], axis=1).astype(BF).reshape(2, 128, 256)

    project(0)
    project(1)
    project(3)
    step(gt)
    project(2)
    spilled = net.copy(N, spill)
    net.send(BX.at[0:4, :, 128:136], BX.at[pl.ds(p.yl, 4), :, 0:8], halo, p.at(y=p.y + 1 - 2 * p.yl))
    step(av)
    net.finish(gt_sent)
    spilled()
    net.got(BX.at[pl.ds(1 - p.yl, 4), :, 0:8], halo)

    r1 = ReduceRing(net, PA, resid, *ring_a)

    def conv(zj, cc):
        return taps[0] * BX[zj, cc, 8:136] + taps[1] * BX[zj, cc, 7:135] + taps[2] * BX[zj, cc, 6:134]

    def mix(j):
        zj = block(j)
        for cc in range(2):
            MX[zj, cc] = (C[zj, cc].astype(F32) * conv(zj, cc)).astype(BF)
        o = jnp.concatenate([whole(WC, slice(384, 512)), whole(WC, slice(640, 768))], axis=1)
        PA[zj] = dot(MX[zj].reshape(256, 256), o, NT).astype(BF).reshape(2, 128, D)
        r1.push(j)

    for j in (2, 1, 3, 0):
        mix(j)
    r1_sent, r1 = r1.mine, r1.rest()
    step(r1, 2)
    step(au)
    step(go, 2)
    step(r1)
    step(ad), step(av)
    step(r1)
    net.finish(r1_sent)
    own_gout()

    def second(i, _):
        at = pl.ds(pl.multiple_of(i * 16, 16), 16)
        v = tok[at].astype(F32) + resid[at]
        resid[at] = v
        inv = lax.rsqrt(jnp.mean(v * v, axis=1, keepdims=True) + epsilon)
        N[p.z, p.c, at] = (v * inv * g_ffn).astype(BF)

    lax.fori_loop(0, ROWS // 16, second, None)
    g2 = gather_ring(net, N.at[p.z, p.c], N, g2_sent)
    step(g2)
    step(go)
    step(au)
    step(g2)
    step(av)

    def ahead(j):
        zj = block(j)
        n2 = N[zj].reshape(256, D)
        for t in range(7):
            r = dot(n2, whole(WG, slice(256 * t, 256 * t + 256)), NN)
            g, u = r[:, :128], r[:, 128:]
            HID[zj, :, 128 * t : 128 * t + 128] = (g * jax.nn.sigmoid(g) * u).astype(BF)
            GGU[zj, :, 256 * t : 256 * t + 256] = r.astype(BF)

    def act(j):
        zj = block(j)
        for t in range(0, 7, 2):
            n = min(2, 7 - t)
            a = dot(GO[zj].reshape(256, D), whole(WD, slice(128 * t, 128 * (t + n))), NN)
            for i in range(n):
                ga = a[:, 128 * i : 128 * i + 128]
                at = 256 * (t + i)
                g, u = GGU[zj, :, at : at + 128].astype(F32), GGU[zj, :, at + 128 : at + 256].astype(F32)
                s = jax.nn.sigmoid(g)
                GGU[zj, :, at : at + 128] = (ga * u * s * (1.0 + g * (1.0 - s))).astype(BF)
                GGU[zj, :, at + 128 : at + 256] = (ga * g * s).astype(BF)

    def back(j):
        zj = block(j)
        PA[zj] = dot(GGU[zj], whole(WG), NT).astype(BF).reshape(2, 128, D)

    def down(j):
        zj = block(j)
        N[zj] = dot(HID[zj], whole(WD), NT).astype(BF).reshape(2, 128, D)

    ahead(0)
    step(g2)
    step(ad)
    step(g2)
    ahead(1)
    ahead(3)
    step(g2)
    step(go)
    ahead(2)
    step(ad)
    step(go)
    net.finish(go_sent)
    r2 = ReduceRing(net, PA, GR, *ring_a)
    r2_sent, r2_rest = r2.mine, r2.rest()
    act(2)
    back(2)
    r2.push(2)
    act(1)
    step(r2_rest)
    back(1)
    r2.push(1)
    act(3)
    back(3)
    r2.push(3)
    act(0)
    step(r2_rest)
    back(0)
    r2.push(0)
    net.finish(gu_sent)

    def weight_grad(out, lhs, rhs, x0, n):
        a = lhs[:, :, :, 384 * x0 : 384 * x0 + 384].reshape(1024, 384)
        out[x0] = dot(a, rhs.reshape(1024, n), TN).astype(BF).reshape(2, 2, 96, n)

    def grad_down(x0):
        weight_grad(DD, GO, HID[...], x0, FP)

    def grad_a(x0):
        weight_grad(WA, N, GGU[:, :, 0:GA_N], x0, GA_N)

    def grad_b(x0):
        weight_grad(WB, N, GGU[:, :, GA_N:], x0, 1792 - GA_N)

    jd = reduce_plane(net, DD, SD, *sd)
    ja = reduce_plane(net, WA, SA, *sa)
    jb = reduce_plane(net, WB, SB_, *sb)
    grad_down(0)
    step(r2_rest)
    grad_down(1)
    grad_down(2)
    grad_down(3)
    step(jd)
    grad_a(0)
    grad_a(1)
    grad_a(2)
    step(jd)
    step(r2_rest)
    net.finish(r2_sent)

    def third(i, _):
        at = pl.ds(pl.multiple_of(i * 16, 16), 16)
        v = resid[at]
        inv = lax.rsqrt(jnp.mean(v * v, axis=1, keepdims=True) + epsilon)
        x = v * inv
        w = g_ffn * GR[at]
        g = gout[at].astype(F32) + inv * (w - x * jnp.mean(w * x, axis=1, keepdims=True))
        GR[at] = g
        T[p.z, p.c, at] = g.astype(BF)

    lax.fori_loop(0, ROWS // 16, third, None)
    g3 = gather_ring(net, T.at[p.z, p.c], T, g3_sent)
    step(g3)
    reloaded = net.copy(spill, PA)
    grad_a(3)
    step(ja)
    grad_b(0)
    grad_b(1)
    grad_b(2)
    grad_b(3)
    step(jb)
    step(jd)
    KP[...] = jnp.zeros(KP.shape, F32)

    def unmix(j):
        zj = block(j)
        o = jnp.concatenate([whole(WC, slice(384, 512)), whole(WC, slice(640, 768))], axis=1)
        gm = dot(T[zj].reshape(256, D), o, NN)
        gm = jnp.concatenate([gm[:, :128], jnp.where(lanes, gm[:, 128:], 0.0)], axis=1).reshape(2, 128, 256)
        for cc in range(2):
            gc = gm[cc] * conv(zj, cc)
            at = slice(128 * cc, 128 * cc + 128)
            GGU[zj, at, 128:256] = gc[:, :128].astype(BF)
            GGU[zj, at, 512:640] = pltpu.roll(gc[:, 128:], 64, 1).astype(BF)
            gv = gm[cc] * C[zj, cc].astype(F32)
            GC[zj + 1, cc, 0:128] = gv
            for i in range(3):
                KP[i : i + 1] = KP[i : i + 1] + jnp.sum(gv * BX[zj, cc, 8 - i : 136 - i], axis=0, keepdims=True)

    step(g3)
    unmix(0)
    step(g3)
    step(ja)
    net.finish(g2_sent)
    down(0)
    down(1)
    step(jb)
    step(jd)
    step(g3)
    unmix(1)
    unmix(3)
    step(ja)
    down(2)
    step(g3)
    unmix(2)
    net.send(GC.at[1:5, :, 0:8], GC.at[pl.ds(p.yl, 4), :, 128:136], halo_back, p.at(y=p.y + 1 - 2 * p.yl))
    down(3)
    r4 = ReduceRing(net, N, MR, *ring_a)
    r4_sent, r4_rest = r4.mine, r4.rest()
    for j in (2, 1, 3, 0):
        r4.push(j)
    step(jb)
    step(jd)
    for who in partners:
        pl.semaphore_signal(free, inc=1, device_id=who, device_id_type=MESH)
    step(r4_rest)
    net.got(GC.at[pl.ds(1 - p.yl, 4), :, 128:136], halo_back)
    r3 = ReduceRing(net, GO, R1, *ring_b)
    r3_sent, r3_rest = r3.mine, r3.rest()

    def unproject(j):
        zj = block(j)
        for cc in range(2):
            at = slice(128 * cc, 128 * cc + 128)
            gb = taps[0] * GC[zj + 1, cc, 0:128] + taps[1] * GC[zj + 1, cc, 1:129] + taps[2] * GC[zj + 1, cc, 2:130]
            bb, vv = gb * V[zj, cc].astype(F32), gb * B[zj, cc].astype(F32)
            GGU[zj, at, 0:128] = bb[:, :128].astype(BF)
            GGU[zj, at, 256:384] = vv[:, :128].astype(BF)
            GGU[zj, at, 384:512] = jnp.zeros((128, 128), BF)
            GGU[zj, at, 512:640] = (GGU[zj, at, 512:640].astype(F32) + bb[:, 128:]).astype(BF)
            GGU[zj, at, 640:768] = pltpu.roll(vv[:, 128:], 64, 1).astype(BF)
        GO[zj] = dot(GGU[zj, :, 0:768], whole(WC), NT).astype(BF).reshape(2, 128, D)
        r3.push(j)

    unproject(2)
    step(r4_rest)
    unproject(1)
    unproject(3)
    unproject(0)
    step(r3_rest)
    step(ja)
    reloaded()
    DC = DD.at[:, :, :, :, 0:768]
    for x0 in range(4):
        at = slice(384 * x0, 384 * x0 + 384)
        w = dot(PA[:, :, :, at].reshape(1024, 384), GGU[:, :, 0:768].reshape(1024, 768), TN)
        m = dot(T[:, :, :, at].reshape(1024, 384), MX[...].reshape(1024, 256), TN)
        w = jnp.concatenate([w[:, :384], m[:, :128], w[:, 512:640], w[:, 640:] + m[:, 128:]], axis=1)
        DC[x0] = w.astype(BF).reshape(2, 2, 96, 768)
        if x0 == 1:
            step(r3_rest)
    tile = jnp.concatenate([KP[...], jnp.zeros((24, 256), F32)], axis=0).astype(BF)
    for s in range(16):
        KG[s // 4, (s // 2) % 2, s % 2] = tile
    pl.semaphore_wait(free, len(partners))
    jc = reduce_plane(net, DC, SC, *[r.at[(slice(None),) * (len(r.shape) - 1) + (slice(0, 768),)] for r in sd])
    jk = reduce_plane(net, KG, SK, *sk)
    step(jc), step(jk)
    step(r4_rest)
    step(r3_rest)
    step(jb)
    step(jc), step(jk)
    step(r4_rest)
    step(r3_rest)
    step(jc), step(jk)
    step(ja), step(jb)
    ffn_share = jnp.sum(SA[...] * gu_s[:, 0:GA_N].astype(F32), axis=1, keepdims=True)
    ffn_share += jnp.sum(SB_[...] * gu_s[:, GA_N:].astype(F32), axis=1, keepdims=True)
    step(jc), step(jk)
    step(jc), step(jk)
    half = lax.broadcasted_iota(jnp.int32, (96, 128), 1) < 64
    mix_ = SC[...] * conv_s[...].astype(F32)
    mix_share = jnp.sum(mix_[:, :384], axis=1, keepdims=True) + jnp.sum(
        mix_[:, 512:640] + jnp.where(half, 0.0, mix_[:, 640:]), axis=1, keepdims=True
    )
    lane = lax.broadcasted_iota(jnp.int32, (96, 128), 1)
    both = jnp.where(lane == 0, mix_share, ffn_share)
    both = jnp.concatenate([both, jnp.zeros((32, 128), F32)], axis=0).T
    X[0:8] = SK[0:8]
    X[8:16] = jnp.zeros((8, 256), F32)
    X[8:9, 0:96] = both[0:1, 0:96] / gm_w[...].astype(F32)
    X[9:10, 0:96] = both[1:2, 0:96] / gf_w[...].astype(F32)
    me = lax.axis_index("tensor")
    done = net.copy(X, XR.at[me])
    base = net.sem(8)
    for i in range(1, 8):
        net.send(X, XR.at[me], base + i, (lax.axis_index("dp"), (me + i) % 8))
    for i in range(1, 8):
        net.got(XR.at[(me + 8 - i) % 8], base + i)
    done()
    for job in (gt, go, g2, g3, am, ac, ae, ad, au, av, r1, r2_rest, r3_rest, r4_rest, ja, jb, jd, jc, jk):
        assert next(job, "end") == "end"
    net.finish(r3_sent + r4_sent + g3_sent + w_sent)
    net.finish()


GA_N = 1024


def train_call(*args):
    any_, vm = pl.BlockSpec(memory_space=pl.ANY), pl.BlockSpec(memory_space=pltpu.VMEM)
    ring, wide = (4, 2, ROWS, D), (4, 2, ROWS, 256)
    outs = [shape((ROWS, D), F32), shape((32, D), F32)] + [shape((ROWS, D), F32)] * 3
    outs += [shape((96, n), F32) for n in (GA_N, 1792 - GA_N, FP, 768)] + [shape((8, 16, 256), F32), shape(ring)]
    v = lambda s, t=BF: pltpu.VMEM(s, t)
    scratch = [v((ROWS, D)), v((96, 768)), v((96, 1792)), v((96, FP)), v((32, 256)), v((256, 128), F32)]
    scratch += [v(ring)] * 3 + [v((4, 2, 2, 96, n)) for n in (768, 1792, FP)] + [v((4, 2, 2, 32, 256))]
    scratch += [v(wide)] * 3 + [v((5, 2, 136, 256), F32), v(wide), v((5, 2, 136, 256), F32)]
    scratch += [v((4, 256, FP)), v((4, 256, 1792)), v(ring), v((4, 2, 2, 96, FP)), v((8, 256), F32)]
    scratch += plane_scratch(GA_N) + plane_scratch(1792 - GA_N) + plane_scratch(FP) + plane_scratch(256, 16)
    scratch += ring_scratch(D) * 2 + [v((4, 2, 2, 32, 256)), v((16, 256), F32), v((32, 256), F32)]
    scratch += [pltpu.SemaphoreType.REGULAR]
    scratch += [pltpu.SemaphoreType.DMA((400,)), pltpu.SemaphoreType.DMA((400,)), pltpu.SemaphoreType.DMA((24,))]
    *sums, _ = pl.pallas_call(
        train_kernel,
        out_shape=tuple(outs),
        in_specs=[vm] * 11,
        out_specs=tuple([vm] * 10 + [any_]),
        scratch_shapes=scratch,
        compiler_params=pltpu.CompilerParams(
            collective_id=0, has_side_effects=True, vmem_limit_bytes=64 << 20),
        name="train",
    )(*args)
    return sums


def finish_kernel(tok, lens, resid, gains, GR, MR, R1, SA, SB, SD, SC, XR,
                  layer_out, tokens_grad, mix, in_grad, taps, out_grad, ffn, gate, up, down, flip, live):
    g_mix = gains[0:1, :D]
    live[...] = jnp.broadcast_to(live_rows(lens), (ROWS, 128))

    def last(i, _):
        at = pl.ds(pl.multiple_of(i * 16, 16), 16)
        layer_out[at] = (live[at, 0:1] * (resid[at] + MR[at])).astype(BF)
        v = tok[at].astype(F32)
        inv = lax.rsqrt(jnp.mean(v * v, axis=1, keepdims=True) + epsilon)
        x = v * inv
        w = g_mix * R1[at]
        g = GR[at] + inv * (w - x * jnp.mean(w * x, axis=1, keepdims=True))
        tokens_grad[at] = g.astype(BF)

    lax.fori_loop(0, ROWS // 16, last, None)
    for t in range(7):
        n = 96 if t == 6 else 128
        src, at = (SA, 256 * t) if t < 4 else (SB, 256 * t - 1024)
        gate[:, 128 * t : 128 * t + n] = src[:, at : at + n]
        up[:, 128 * t : 128 * t + n] = src[:, at + 128 : at + 128 + n]
    down[...] = SD[:, 0:FB]
    flip[96:128] = jnp.zeros((32, 256), F32)
    flip[0:96, 0:128] = SC[:, 384:512]
    flip[0:96, 128:256] = SC[:, 640:768]
    out_grad[...] = flip[...].T[0:CH, 0:96]
    for i in range(3):
        in_grad[i, :, 0:128] = SC[:, 128 * i : 128 * i + 128]
    in_grad[0, :, 128:192] = SC[:, 512:576]
    in_grad[1, :, 128:192] = pltpu.roll(SC[:, 512:640], 64, 1)[:, :64]
    in_grad[2, :, 128:192] = pltpu.roll(SC[:, 640:768], 64, 1)[:, :64]
    dp, t = lax.axis_index("dp"), lax.axis_index("tensor")
    shares = XR[0, 8:16]
    for i in range(1, 8):
        shares = shares + XR[i, 8:16]
    shares = pltpu.roll(shares, 256 - 12 * t, 1)
    mix[...] = shares[0:1, 0:12]
    ffn[...] = shares[1:2, 0:12]
    k = pltpu.roll(XR[dp // 2, 0:8], lax.rem(256 - 12 * ((dp * 8 + t) % 16), 256), 1)
    taps[...] = k[0:3, 0:12]


def finish_call(*args):
    vm = pl.BlockSpec(memory_space=pltpu.VMEM)
    outs = [shape((ROWS, D)), shape((ROWS, D)), shape((1, 12), F32), shape((3, 96, CH), F32), shape((3, 12), F32)]
    outs += [shape((CH, 96), F32), shape((1, 12), F32), shape((96, FB), F32), shape((96, FB), F32), shape((96, FB), F32)]
    return pl.pallas_call(
        finish_kernel,
        out_shape=tuple(outs),
        in_specs=[vm] * 12,
        out_specs=tuple([vm] * 10),
        scratch_shapes=[pltpu.VMEM((128, 256), F32), pltpu.VMEM((ROWS, 128), F32)],
        compiler_params=pltpu.CompilerParams(vmem_limit_bytes=VMEM_LIMIT),
        name="finish",
    )(*args)


def per_device(tokens, gain_mix, in_weight, conv_kernel, out_weight, gain_ffn, gate_weight, up_weight, down_weight, lengths, cotangent):
    gm, gf, lens = gain_mix.reshape(1, 96), gain_ffn.reshape(1, 96), lengths.reshape(1, 1)
    resid, gains, *sums = train_call(
        tokens, cotangent, lens, in_weight.transpose(1, 0, 2), out_weight, gate_weight, up_weight,
        down_weight.T, gm, gf, conv_kernel)
    layer_out, tokens_grad, mix, in_grad, taps_grad, out_grad, ffn, gate, up, down = finish_call(
        tokens, lens, resid, gains, *sums
    )
    return layer_out, tokens_grad, mix[0], in_grad.transpose(1, 0, 2), taps_grad, out_grad, ffn[0], gate, up, down.T


def solution(mesh):
    placed = (
        P(("dp", "tensor"), None),
        P("dp"),
        P("dp", None, "tensor"),
        P(None, "tensor"),
        P("tensor", "dp"),
        P("dp"),
        P("dp", "tensor"),
        P("dp", "tensor"),
        P("tensor", "dp"),
        P("dp"),
        P(("dp", "tensor"), None),
    )
    return jax.shard_map(
        per_device,
        mesh=mesh,
        in_specs=placed,
        out_specs=(
            P(("dp", "tensor"), None),
            P(("dp", "tensor"), None),
            P(("dp", "tensor")),
            P("dp", None, "tensor"),
            P(None, ("dp", "tensor")),
            P("tensor", "dp"),
            P(("dp", "tensor")),
            P("dp", "tensor"),
            P("dp", "tensor"),
            P("tensor", "dp"),
        ),
        check_vma=False,
    )
```

```python
import functools

import jax
import jax.numpy as jnp
from jax import lax
from jax.experimental import pallas as pl
from jax.experimental.pallas import tpu as pltpu
from jax.sharding import PartitionSpec as P

epsilon = 1e-05
MESH = pl.DeviceIdType.MESH
BF = jnp.bfloat16
F32 = jnp.float32
D = 1536
ROWS = 128
CH = 192
FB = 864
FP = 896
HALF = 48
VMEM_LIMIT = 60 << 20


class Place:
    def __init__(self):
        dp = lax.axis_index("dp")
        t = lax.axis_index("tensor")
        self.x, self.yh, self.c = dp // 4, (dp // 2) % 2, dp % 2
        self.z, self.yl = t // 2, t % 2
        self.y = self.yh * 2 + self.yl
        self.o = 1 - self.c
        self.xp, self.xm, self.x2 = (self.x + 1) % 4, (self.x + 3) % 4, (self.x + 2) % 4
        self.yp, self.ym = (self.y + 1) % 4, (self.y + 3) % 4
        self.y2 = (self.y + 2) % 4
        self.yhp, self.yhm = self.yp // 2, self.ym // 2
        self.way = 1 - 2 * self.c
        self.zf = (self.z + self.way + 4) % 4
        self.zb = (self.z - self.way + 4) % 4
        self.zp, self.zm, self.z2 = (self.z + 1) % 4, (self.z + 3) % 4, (self.z + 2) % 4
        self.own = self.c == self.yl
        self.opp = self.c != self.yl

    def at(self, x=None, y=None, z=None, c=None):
        x = self.x if x is None else x
        y = self.y if y is None else y
        z = self.z if z is None else z
        c = self.c if c is None else c
        return (x * 4 + (y // 2) * 2 + c, z * 2 + y % 2)


class Net:
    def __init__(self, place, send, recv, local=None):
        self.p, self.ss, self.rs, self.ls = place, send, recv, local
        self.ns = self.nr = self.nl = 0
        self.pending = []

    def sem(self, n=1):
        k = self.nr
        self.nr += n
        return k

    def send(self, src, dst, recv_index, target, cond=None, pending=None):
        k = self.ns
        self.ns += 1
        d = pltpu.make_async_remote_copy(
            src_ref=src, dst_ref=dst, send_sem=self.ss.at[k], recv_sem=self.rs.at[recv_index],
            device_id=target, device_id_type=MESH)
        run(cond, d.start)
        (self.pending if pending is None else pending).append((cond, d))

    def copy(self, src, dst, cond=None):
        k = self.nl
        self.nl += 1
        d = pltpu.make_async_copy(src, dst, self.ls.at[k])
        run(cond, d.start)
        return lambda: run(cond, d.wait)

    def got(self, dst, recv_index, cond=None):
        d = pltpu.make_async_remote_copy(
            src_ref=dst, dst_ref=dst, send_sem=self.ss.at[0], recv_sem=self.rs.at[recv_index],
            device_id=self.p.at(c=self.p.o), device_id_type=MESH)
        run(cond, d.wait_recv)

    def finish(self, pending=None):
        pending = self.pending if pending is None else pending
        for cond, d in pending:
            run(cond, d.wait_send)
        pending.clear()


def run(cond, f):
    if cond is None:
        f()
    else:
        pl.when(cond)(f)


def greet(p, plane, ring, group=False):
    bar = pltpu.get_barrier_semaphore()
    who = [p.at(c=p.o)]
    if plane:
        for c in (0, 1):
            who += [p.at(x=p.xp, c=c), p.at(x=p.xm, c=c), p.at(y=p.yp, c=c), p.at(y=p.ym, c=c)]
            who += [p.at(x=p.x2, c=c), p.at(y=p.y2, c=c)]
    if group:
        me = lax.axis_index("tensor")
        who += [(lax.axis_index("dp"), (me + i) % 8) for i in range(1, 8)]
    elif ring:
        who += [p.at(z=p.zp), p.at(z=p.zm)]
    for w in who:
        pl.semaphore_signal(bar, inc=1, device_id=w, device_id_type=MESH)
    return lambda: pl.semaphore_wait(bar, len(who))


def add(out, *terms):
    lead = out.shape[:-2]
    count = 1
    for s in lead:
        count *= s

    def one(i):
        at = []
        for s in reversed(lead):
            at.append(i % s)
            i = i // s
        at = tuple(reversed(at))
        v = terms[0][at].astype(F32) if at else terms[0][...].astype(F32)
        for t in terms[1:]:
            v = v + (t[at] if at else t[...]).astype(F32)
        if at:
            out[at] = v.astype(out.dtype)
        else:
            out[...] = v.astype(out.dtype)

    if not lead:

        def rows(i, _):
            at = pl.ds(pl.multiple_of(i * 16, 16), 16)
            v = terms[0][at].astype(F32)
            for t in terms[1:]:
                v = v + t[at].astype(F32)
            out[at] = v.astype(out.dtype)

        lax.fori_loop(0, out.shape[0] // 16, rows, None)
    else:
        lax.fori_loop(0, count, lambda i, _: one(i), None)


def ring_scratch(n):
    return [pltpu.VMEM((4, ROWS, n), BF), pltpu.VMEM((3, ROWS, n), BF)]


def shape(s, t=BF):
    return jax.ShapeDtypeStruct(s, t)


def slots(n):
    return shape((4, 2, 2, 96, n))


def gather_plane(net, sh, W, mine, far=False):
    p = net.p
    send = functools.partial(net.send, pending=mine)
    h = sh.shape[0] // 2
    HA, HB = pl.ds(0, h), pl.ds(h, h)
    i_own, f1, f2, f3, f4 = net.sem(), net.sem(2), net.sem(2), net.sem(2), net.sem(2)
    r1, r2, r3, r4, y1, y2, y3, y4, x1, x2, x3, x4 = (net.sem() for _ in range(12))
    f5, f6 = net.sem(2), net.sem(2)
    q = p.yl

    def pass_near():
        net.got(W.at[p.xm, p.yh, 0, HA], f1 + 0, p.own)
        net.got(W.at[p.x, p.yhm, 0, HB], f3 + 0, p.opp)
        send(W.at[p.xm, p.yh, 0, HA], W.at[p.xm, p.yh, 0, HA], r1, p.at(x=p.xp), p.own)
        send(W.at[p.x, p.yhm, 0, HB], W.at[p.x, p.yhm, 0, HB], r3, p.at(y=p.yp), p.opp)
        net.got(W.at[p.xp, p.yh, 1, HA], f2 + 1, p.own)
        net.got(W.at[p.x, p.yhp, 1, HB], f4 + 1, p.opp)
        send(W.at[p.xp, p.yh, 1, HA], W.at[p.xp, p.yh, 1, HA], r2, p.at(x=p.xm), p.own)
        send(W.at[p.x, p.yhp, 1, HB], W.at[p.x, p.yhp, 1, HB], r4, p.at(y=p.ym), p.opp)
        yield

    done = net.copy(sh, W.at[p.x, p.yh, p.c], p.own)
    send(sh.at[HA], W.at[p.x, p.yh, p.c, HA], f1 + p.c, p.at(x=p.xp, c=q))
    send(sh.at[HA], W.at[p.x, p.yh, p.c, HA], f2 + p.c, p.at(x=p.xm, c=q))
    send(sh.at[HB], W.at[p.x, p.yh, p.c, HB], f3 + p.c, p.at(y=p.yp, c=q))
    send(sh.at[HB], W.at[p.x, p.yh, p.c, HB], f4 + p.c, p.at(y=p.ym, c=q))
    send(sh, W.at[p.x, p.yh, p.c], i_own, p.at(c=p.o), p.opp)
    if far:
        send(sh.at[HA], W.at[p.x, p.yh, p.c, HA], f5 + p.c, p.at(x=p.x2, c=q))
        send(sh.at[HB], W.at[p.x, p.yh, p.c, HB], f6 + p.c, p.at(y=p.y2, c=q))
    yield
    if not far:
        yield from pass_near()
    done()
    net.got(W.at[p.x, p.yh, p.o], i_own, p.own)
    net.got(W.at[p.xm, p.yh, 1, HA], f1 + 1, p.own)
    net.got(W.at[p.xp, p.yh, 0, HA], f2 + 0, p.own)
    net.got(W.at[p.x, p.yhm, 1, HB], f3 + 1, p.opp)
    net.got(W.at[p.x, p.yhp, 0, HB], f4 + 0, p.opp)
    if far:
        net.got(W.at[p.xm, p.yh, 0, HA], f1 + 0, p.own)
        net.got(W.at[p.xp, p.yh, 1, HA], f2 + 1, p.own)
        net.got(W.at[p.x, p.yhm, 0, HB], f3 + 0, p.opp)
        net.got(W.at[p.x, p.yhp, 1, HB], f4 + 1, p.opp)
    for cc in range(2):
        net.got(W.at[p.x2, p.yh, cc, HA], f5 + cc if far else (r1, r2)[cc], p.own)
    send(W.at[:, p.yh, :, HA], W.at[:, p.yh, :, HA], y1, p.at(y=p.yp), p.own)
    send(W.at[:, p.yh, :, HA], W.at[:, p.yh, :, HA], y2, p.at(y=p.ym), p.own)
    for cc in range(2):
        net.got(W.at[p.x, 1 - p.yh, cc, HB], f6 + cc if far else (r3, r4)[cc], p.own)
    send(W.at[p.x, :, :, HB], W.at[p.x, :, :, HB], x1, p.at(x=p.xp))
    send(W.at[p.x, :, :, HB], W.at[p.x, :, :, HB], x2, p.at(x=p.xm))
    yield
    net.got(W.at[p.xm, :, :, HB], x1)
    send(W.at[p.xm, :, 0, HB], W.at[p.xm, :, 0, HB], x3, p.at(x=p.xp))
    net.got(W.at[p.xp, :, :, HB], x2)
    send(W.at[p.xp, :, 1, HB], W.at[p.xp, :, 1, HB], x4, p.at(x=p.xm))
    net.got(W.at[:, p.yhm, :, HA], y1, p.opp)
    send(W.at[:, p.yhm, 0, HA], W.at[:, p.yhm, 0, HA], y3, p.at(y=p.yp), p.opp)
    net.got(W.at[:, p.yhp, :, HA], y2, p.opp)
    send(W.at[:, p.yhp, 1, HA], W.at[:, p.yhp, 1, HA], y4, p.at(y=p.ym), p.opp)
    yield
    net.got(W.at[:, 1 - p.yh, 0, HA], y3, p.own)
    net.got(W.at[:, 1 - p.yh, 1, HA], y4, p.own)
    net.got(W.at[p.x2, :, 0, HB], x3)
    net.got(W.at[p.x2, :, 1, HB], x4)


PARTS = [pl.ds(0, 64), pl.ds(64, 64)]


def gather_ring(net, a, out, mine, late=False):
    p = net.p
    send = functools.partial(net.send, pending=mine)
    s1, s3, s2 = net.sem(2), net.sem(2), net.sem(2)
    k = net.sem(8)
    jf, jb = (p.zf - p.z + 4) % 4, (p.zb - p.z + 4) % 4
    for i, r in enumerate(PARTS):
        send(a.at[r], out.at[p.z, p.c, r], s1 + i, p.at(z=p.zf))
        send(a.at[r], out.at[p.z, p.c, r], s3 + i, p.at(z=p.zb))
    for i, r in enumerate(PARTS):
        send(a.at[r], out.at[p.z, p.c, r], k + 4 * i, p.at(c=p.o))
    yield
    for i, r in enumerate(PARTS):
        net.got(out.at[p.z, p.o, r], k + 4 * i)
    yield
    for i, r in enumerate(PARTS):
        net.got(out.at[p.zb, p.c, r], s1 + i)
        if not late:
            send(out.at[p.zb, p.c, r], out.at[p.zb, p.c, r], s2 + i, p.at(z=p.zf))
        send(out.at[p.zb, p.c, r], out.at[p.zb, p.c, r], k + 4 * i + jb, p.at(c=p.o))
        net.got(out.at[p.zf, p.c, r], s3 + i)
        send(out.at[p.zf, p.c, r], out.at[p.zf, p.c, r], k + 4 * i + jf, p.at(c=p.o))
    yield
    for i, r in enumerate(PARTS):
        net.got(out.at[p.zp, p.o, r], k + 4 * i + 1)
        net.got(out.at[p.zm, p.o, r], k + 4 * i + 3)
    yield
    if late:
        for i, r in enumerate(PARTS):
            send(out.at[p.zb, p.c, r], out.at[p.zb, p.c, r], s2 + i, p.at(z=p.zf))
        yield
    for i, r in enumerate(PARTS):
        net.got(out.at[p.z2, p.c, r], s2 + i)
        send(out.at[p.z2, p.c, r], out.at[p.z2, p.c, r], k + 4 * i + 2, p.at(c=p.o))
    yield
    for i, r in enumerate(PARTS):
        net.got(out.at[p.z2, p.o, r], k + 4 * i + 2)


class ReduceRing:
    def __init__(self, net, V, out, RC, RZ):
        self.net, self.V, self.out, self.RC, self.RZ = net, V, out, RC, RZ
        self.s2, self.sd, self.sr, self.k = net.sem(2), net.sem(2), net.sem(2), net.sem(8)
        self.mine = []
        self.send = functools.partial(net.send, pending=self.mine)

    def push(self, j):
        p = self.net.p
        for i, r in enumerate(PARTS):
            self.send(self.V.at[(p.z + j) % 4, p.o, r], self.RC.at[j, r], self.k + 4 * i + j, p.at(c=p.o))

    def rest(self):
        net, p, V, RC, RZ, k = self.net, self.net.p, self.V, self.RC, self.RZ, self.k
        jf, jb = (p.zf - p.z + 4) % 4, (p.zb - p.z + 4) % 4
        for i, r in enumerate(PARTS):
            net.got(RC.at[2, r], k + 4 * i + 2)
            add(RC.at[2, r], V.at[p.z2, p.c, r], RC.at[2, r])
            self.send(RC.at[2, r], RZ.at[0, r], self.s2 + i, p.at(z=p.zf))
        yield
        for i, r in enumerate(PARTS):
            net.got(RC.at[jb, r], k + 4 * i + jb)
            add(RC.at[jb, r], V.at[p.zb, p.c, r], RC.at[jb, r])
            self.send(RC.at[jb, r], RZ.at[1, r], self.sd + i, p.at(z=p.zb))
        for i, r in enumerate(PARTS):
            net.got(RC.at[jf, r], k + 4 * i + jf)
            add(RC.at[jf, r], V.at[p.zf, p.c, r], RC.at[jf, r])
        yield
        for i, r in enumerate(PARTS):
            net.got(RZ.at[0, r], self.s2 + i)
            add(RC.at[jf, r], RC.at[jf, r], RZ.at[0, r])
            self.send(RC.at[jf, r], RZ.at[2, r], self.sr + i, p.at(z=p.zf))
        yield
        for i, r in enumerate(PARTS):
            net.got(RC.at[0, r], k + 4 * i)
            add(RC.at[0, r], V.at[p.z, p.c, r], RC.at[0, r])
        yield
        for i, r in enumerate(PARTS):
            net.got(RZ.at[1, r], self.sd + i)
            net.got(RZ.at[2, r], self.sr + i)
            add(self.out.at[r], RC.at[0, r], RZ.at[1, r], RZ.at[2, r])


def step(job, times=1):
    for _ in range(times):
        next(job, None)


def dot(a, b, dims):
    return lax.dot_general(a, b, (dims, ((), ())), preferred_element_type=F32)


NN, NT, TN = ((1,), (0,)), ((1,), (1,)), ((0,), (0,))


def whole(ref, columns=slice(None)):
    v = ref[:, :, :, :, columns]
    return v.reshape(D, v.shape[-1])


def row_norm(src, dst, gain, rows=32):
    def one(i, _):
        at = pl.ds(pl.multiple_of(i * rows, rows), rows)
        v = src[at].astype(F32)
        inv = lax.rsqrt(jnp.mean(v * v, axis=1, keepdims=True) + epsilon)
        dst[at] = (v * inv * gain).astype(dst.dtype)

    lax.fori_loop(0, ROWS // rows, one, None, unroll=2)


def live_rows(lens, first=0, rows=ROWS):
    at = lax.axis_index("tensor") * ROWS + first + lax.broadcasted_iota(jnp.int32, (rows, 1), 0)
    return jnp.where(at < lens[...], 1.0, 0.0).astype(F32)


def plane_scratch(n, h=HALF):
    return [
        pltpu.VMEM((2, 4, h, n), BF),
        pltpu.VMEM((2, 4, 2, h, n), BF),
        pltpu.VMEM((2, h, n), BF),
        pltpu.VMEM((3, h, n), BF),
        pltpu.VMEM((2, 2, h, n), BF),
        pltpu.VMEM((2, 2, 2, h, n), BF),
        pltpu.VMEM((2, h, n), BF),
        pltpu.VMEM((3, h, n), BF),
    ]


def reduce_plane(net, G, out, RA, RB, RC, F, RX, RY, RZ, H):
    p = net.p
    h = out.shape[0] // 2
    HA, HB = pl.ds(0, h), pl.ds(h, h)
    mine = []
    send = functools.partial(net.send, pending=mine)
    a0, a1, bp0, bp1, bm0, bm1, c0, c1, g0, g1, g2 = (net.sem() for _ in range(11))
    u0, u1, vp0, vp1, vm0, vm1, w0, w1, h0, h1, h2 = (net.sem() for _ in range(11))
    send(G.at[:, 1 - p.yh, 0, HA], RA.at[0], a0, p.at(y=p.ym), p.own)
    send(G.at[:, 1 - p.yh, 1, HA], RA.at[1], a1, p.at(y=p.yp), p.own)
    send(G.at[p.x2, :, 0, HB], RX.at[0], u0, p.at(x=p.xm))
    send(G.at[p.x2, :, 1, HB], RX.at[1], u1, p.at(x=p.xp))
    yield
    send(G.at[:, p.yhm, 1, HA], RB.at[0, :, 1], bp1, p.at(y=p.ym), p.opp)
    send(G.at[:, p.yhp, 0, HA], RB.at[1, :, 0], bm0, p.at(y=p.yp), p.opp)
    send(G.at[p.xm, :, 1, HB], RY.at[0, :, 1], vp1, p.at(x=p.xm))
    send(G.at[p.xp, :, 0, HB], RY.at[1, :, 0], vm0, p.at(x=p.xp))
    yield

    net.got(RX.at[0], u0)
    add(RX.at[0], RX.at[0], G.at[p.xm, :, 0, HB])
    send(RX.at[0], RY.at[0, :, 0], vp0, p.at(x=p.xm))
    net.got(RX.at[1], u1)
    add(RX.at[1], RX.at[1], G.at[p.xp, :, 1, HB])
    send(RX.at[1], RY.at[1, :, 1], vm1, p.at(x=p.xp))
    net.got(RA.at[0], a0, p.opp)
    net.got(RA.at[1], a1, p.opp)

    @pl.when(p.opp)
    def _():
        add(RA.at[0], RA.at[0], G.at[:, p.yhm, 0, HA])
        add(RA.at[1], RA.at[1], G.at[:, p.yhp, 1, HA])

    send(RA.at[0], RB.at[0, :, 0], bp0, p.at(y=p.ym), p.opp)
    send(RA.at[1], RB.at[1, :, 1], bm1, p.at(y=p.yp), p.opp)
    yield

    net.got(RY.at[0, :, 1], vp1)
    net.got(RY.at[1, :, 0], vm0)
    net.got(RY.at[0, :, 0], vp0)
    net.got(RY.at[1, :, 1], vm1)
    add(RY.at[0], RY.at[0], RY.at[1], G.at[p.x, :, :, HB])
    T = RY.at[0]
    send(T.at[1 - p.yh, 0], RZ.at[0], w0, p.at(y=p.ym), p.own)
    send(T.at[1 - p.yh, 1], RZ.at[1], w1, p.at(y=p.yp), p.own)
    send(T.at[p.yhm, 1], H.at[1], h1, p.at(y=p.ym, c=1), p.opp)
    send(T.at[p.yhp, 0], H.at[2], h2, p.at(y=p.yp, c=0), p.opp)
    send(T.at[p.yh, p.o], H.at[0], h0, p.at(c=p.o), p.own)

    net.got(RB.at[0, :, 1], bp1, p.own)
    net.got(RB.at[1, :, 0], bm0, p.own)
    net.got(RB.at[0, :, 0], bp0, p.own)
    net.got(RB.at[1, :, 1], bm1, p.own)

    @pl.when(p.own)
    def _():
        add(RB.at[0], RB.at[0], RB.at[1], G.at[:, p.yh, :, HA])

    S = RB.at[0]
    send(S.at[p.x2, 0], RC.at[0], c0, p.at(x=p.xm), p.own)
    send(S.at[p.x2, 1], RC.at[1], c1, p.at(x=p.xp), p.own)
    send(S.at[p.xm, 1], F.at[1], g1, p.at(x=p.xm, c=1), p.own)
    send(S.at[p.xp, 0], F.at[2], g2, p.at(x=p.xp, c=0), p.own)
    send(S.at[p.x, p.o], F.at[0], g0, p.at(c=p.o), p.own)
    yield

    net.got(RC.at[0], c0, p.own)
    net.got(RC.at[1], c1, p.own)
    net.got(RZ.at[0], w0, p.opp)
    net.got(RZ.at[1], w1, p.opp)

    @pl.when(p.own)
    def _():
        add(RC.at[0], RC.at[0], S.at[p.xm, 0])
        add(RC.at[1], RC.at[1], S.at[p.xp, 1])

    @pl.when(p.opp)
    def _():
        add(RZ.at[0], RZ.at[0], T.at[p.yhm, 0])
        add(RZ.at[1], RZ.at[1], T.at[p.yhp, 1])

    send(RC.at[0], F.at[1], g1, p.at(x=p.xm, c=0), p.own)
    send(RC.at[1], F.at[2], g2, p.at(x=p.xp, c=1), p.own)
    send(RZ.at[0], H.at[1], h1, p.at(y=p.ym, c=0), p.opp)
    send(RZ.at[1], H.at[2], h2, p.at(y=p.yp, c=1), p.opp)
    yield

    net.got(F.at[0], g0, p.opp)
    net.got(F.at[1], g1)
    net.got(F.at[2], g2)
    net.got(H.at[0], h0, p.opp)
    net.got(H.at[1], h1)
    net.got(H.at[2], h2)
    net.finish(mine)

    @pl.when(p.own)
    def _():
        F[0] = S[p.x, p.c]
        H[0] = T[p.yh, p.c]

    add(out.at[HA], F.at[0], F.at[1], F.at[2])
    add(out.at[HB], H.at[0], H.at[1], H.at[2])


def train_kernel(*refs):
    (tok, cot, lens, in_w, out_w, gate_w, up_w, down_w, gm_w, gf_w, taps_w,
     layer_out, tokens_grad, SA, SB_, SD, SC, XR, spill,
     resid, gains, GR, MR, R1, conv_s, gu_s, down_s, small_s, flip, T, N, GO, WC, WG, WD, SM, B, C, V, BX, MX, GC, HID, GGU, PA, DD, KP,
     *more) = refs
    sa, sb, sd, sk, se = [more[8 * i : 8 * i + 8] for i in range(5)]
    ring_a, ring_b = more[40:42], more[42:44]
    KG, X, SK, free, send, recv, local = more[44:]
    p = Place()
    BX[0, :, 0:8] = jnp.zeros((2, 8, 256), F32)
    GC[4, :, 128:136] = jnp.zeros((2, 8, 256), F32)
    greeted = greet(p, True, True, True)
    net = Net(p, send, recv, local)
    block = lambda j: (p.z + j) % 4
    halo, halo_back = net.sem(), net.sem(4)
    partners = [p.at(c=p.o)]
    for cc in (0, 1):
        partners += [p.at(x=p.xp, c=cc), p.at(x=p.xm, c=cc), p.at(y=p.yp, c=cc), p.at(y=p.ym, c=cc)]

    WA, WB = WG.at[:, :, :, :, 0:GA_N], WG.at[:, :, :, :, GA_N:]
    gt_sent, go_sent, g2_sent, g3_sent, gu_sent, w_sent = [], [], [], [], [], []
    gt = gather_ring(net, tok, T, gt_sent)
    go = gather_ring(net, GO.at[p.z, p.c], GO, go_sent)
    am = gather_plane(net, small_s, SM, w_sent, True)
    ac = gather_plane(net, conv_s.at[:, 0:384], WC.at[:, :, :, :, 0:384], w_sent, True)
    ae = gather_plane(net, conv_s.at[:, 384:768], WC.at[:, :, :, :, 384:768], w_sent, True)
    ad = gather_plane(net, down_s, WD, w_sent)
    au = gather_plane(net, gu_s.at[:, 0:GA_N], WA, gu_sent)
    av = gather_plane(net, gu_s.at[:, GA_N:], WB, gu_sent)

    flip[0:256] = jnp.zeros((256, 128), F32)
    flip[0:CH, 0:96] = out_w[...].astype(F32)
    o = flip[0:256].T[0:96]
    side = jnp.zeros((96, 64), F32)
    w = [jnp.concatenate([in_w[i].astype(F32), side], axis=1) for i in range(3)]
    parts = [
        w[1][:, 0:128],
        o[:, 0:128],
        o[:, 128:256] + pltpu.roll(w[1][:, 128:256], 64, 1),
        w[0][:, 0:128],
        w[2][:, 0:128],
        w[0][:, 128:256] + pltpu.roll(w[2][:, 128:256], 64, 1),
    ]
    conv_s[...] = jnp.concatenate(parts, axis=1).astype(BF)
    wide_row = lambda g: jnp.concatenate([g[...].astype(F32), jnp.zeros((1, 160), F32)], axis=1)
    gain = jnp.concatenate([wide_row(gm_w), wide_row(gf_w), jnp.zeros((6, 256), F32)], axis=0)
    small_s[0:16] = jnp.concatenate(
        [pltpu.roll(gain, lax.rem(96 * lax.axis_index("dp"), 128), 1), jnp.zeros((8, 256), F32)], axis=0
    ).astype(BF)
    taps_row = jnp.concatenate([taps_w[...].astype(F32), jnp.zeros((3, 64), F32)], axis=1)
    small_s[16:32] = jnp.concatenate([taps_row, jnp.zeros((13, 256), F32)], axis=0).astype(BF)
    greeted()
    step(gt)
    step(am), step(ac), step(ae)
    live = live_rows(lens)
    GO[p.z, p.c] = (live * cot[...].astype(F32)).astype(BF)
    down_s[:, 768:FP] = jnp.zeros((96, 128), BF)
    down_s[:, 0:FB] = down_w[...]
    for t in range(7):
        n = 96 if t == 6 else 128
        if t == 6:
            gu_s[:, 1536:1792] = jnp.zeros((96, 256), BF)
        gu_s[:, 256 * t : 256 * t + n] = gate_w[:, 128 * t : 128 * t + n]
        gu_s[:, 256 * t + 128 : 256 * t + 128 + n] = up_w[:, 128 * t : 128 * t + n]
    own_tok = net.copy(tok, T.at[p.z, p.c])
    step(am)
    step(au), step(av), step(ad)
    step(ac), step(ae)
    step(gt, 2)
    step(am), step(ac), step(ae)
    step(go)
    step(au), step(av), step(ad)
    step(gt, 2)
    step(am)
    gains[...] = jnp.zeros(gains.shape, F32)
    for s in range(16):
        piece = SM[s // 4, (s // 2) % 2, s % 2, 0:16].astype(F32)
        at = (96 * s) // 128 * 128
        n = min(256, gains.shape[1] - at)
        gains[0:16, at : at + n] = gains[0:16, at : at + n] + piece[:, :n]
    gains[16:32, 0:256] = SM[0, 0, 0, 16:32].astype(F32)
    g_mix, g_ffn = gains[0:1, :D], gains[1:2, :D]
    taps = [gains[16 + i : 17 + i, 0:256] for i in range(3)]
    own_tok()

    def norm(j):
        zj = block(j)
        for cc in range(2):
            row_norm(T.at[zj, cc], N.at[zj, cc], g_mix)

    norm(0)
    norm(1)
    norm(3)
    step(gt)
    norm(2)
    step(ac), step(ae)
    lanes = lax.broadcasted_iota(jnp.int32, (256, 128), 1) < 64

    def project(j):
        zj = block(j)
        r = dot(N[zj].reshape(256, D), whole(WC), NN)
        b1 = jnp.where(lanes, r[:, 640:768], 0.0)
        c1 = jnp.where(lanes, pltpu.roll(r[:, 256:384], 64, 1), 0.0)
        v1 = jnp.where(lanes, pltpu.roll(r[:, 640:768], 64, 1), 0.0)
        b = jnp.concatenate([r[:, 384:512], b1], axis=1)
        v = jnp.concatenate([r[:, 512:640], v1], axis=1)
        BX[zj, :, 8:136] = (b * v).reshape(2, 128, 256)
        B[zj] = b.astype(BF).reshape(2, 128, 256)
        V[zj] = v.astype(BF).reshape(2, 128, 256)
        C[zj] = jnp.concatenate([r[:, 0:128], c1], axis=1).astype(BF).reshape(2, 128, 256)

    for j in range(4):
        project(j)
    spilled = net.copy(N, spill)
    net.send(BX.at[0:4, :, 128:136], BX.at[pl.ds(p.yl, 4), :, 0:8], halo, p.at(y=p.y + 1 - 2 * p.yl))
    step(au), step(av), step(ad)
    step(go, 2)
    net.finish(gt_sent)
    spilled()
    net.got(BX.at[pl.ds(1 - p.yl, 4), :, 0:8], halo)

    r1 = ReduceRing(net, PA, resid, *ring_a)

    def conv(zj, cc):
        return taps[0] * BX[zj, cc, 8:136] + taps[1] * BX[zj, cc, 7:135] + taps[2] * BX[zj, cc, 6:134]

    def mix(j):
        zj = block(j)
        for cc in range(2):
            MX[zj, cc] = (C[zj, cc].astype(F32) * conv(zj, cc)).astype(BF)
        o = whole(WC, slice(128, 384))
        PA[zj] = dot(MX[zj].reshape(256, 256), o, NT).astype(BF).reshape(2, 128, D)
        r1.push(j)

    r1_sent, r1_rest = r1.mine, r1.rest()
    mix(2)
    mix(1)
    step(r1_rest)
    mix(3)
    mix(0)
    step(r1_rest)
    step(r1_rest, 2)
    step(go, 2)
    step(au)
    step(r1_rest)
    net.finish(r1_sent)

    def second(i, _):
        at = pl.ds(pl.multiple_of(i * 16, 16), 16)
        v = tok[at].astype(F32) + resid[at]
        resid[at] = v
        inv = lax.rsqrt(jnp.mean(v * v, axis=1, keepdims=True) + epsilon)
        N[p.z, p.c, at] = (v * inv * g_ffn).astype(BF)

    lax.fori_loop(0, ROWS // 16, second, None, unroll=2)
    g2 = gather_ring(net, N.at[p.z, p.c], N, g2_sent)
    step(g2)
    step(go)
    step(av)
    step(g2)
    step(ad)
    step(au)

    def ahead(j):
        zj = block(j)
        n2 = N[zj].reshape(256, D)
        for t in range(7):
            r = dot(n2, whole(WG, slice(256 * t, 256 * t + 256)), NN)
            g, u = r[:, :128], r[:, 128:]
            HID[zj, :, 128 * t : 128 * t + 128] = (g * jax.nn.sigmoid(g) * u).astype(BF)
            GGU[zj, :, 256 * t : 256 * t + 256] = r.astype(BF)

    def act(j):
        zj = block(j)
        for t in range(0, 7, 2):
            n = min(2, 7 - t)
            a = dot(GO[zj].reshape(256, D), whole(WD, slice(128 * t, 128 * (t + n))), NN)
            for i in range(n):
                ga = a[:, 128 * i : 128 * i + 128]
                at = 256 * (t + i)
                g, u = GGU[zj, :, at : at + 128].astype(F32), GGU[zj, :, at + 128 : at + 256].astype(F32)
                s = jax.nn.sigmoid(g)
                GGU[zj, :, at : at + 128] = (ga * u * s * (1.0 + g * (1.0 - s))).astype(BF)
                GGU[zj, :, at + 128 : at + 256] = (ga * g * s).astype(BF)

    def back(j):
        zj = block(j)
        PA[zj] = dot(GGU[zj], whole(WG), NT).astype(BF).reshape(2, 128, D)

    def down(j):
        zj = block(j)
        N[zj] = dot(HID[zj], whole(WD), NT).astype(BF).reshape(2, 128, D)

    step(g2)
    step(av)
    ahead(0)
    step(g2)
    ahead(1)
    ahead(3)
    step(g2, 2)
    ahead(2)
    step(ad)
    net.finish(go_sent)
    r2 = ReduceRing(net, PA, GR, *ring_a)
    r2_sent, r2_rest = r2.mine, r2.rest()
    def weight_grad(out, lhs, rhs, x0, n):
        a = lhs[:, :, :, 384 * x0 : 384 * x0 + 384].reshape(1024, 384)
        out[x0] = dot(a, rhs.reshape(1024, n), TN).astype(BF).reshape(2, 2, 96, n)

    def grad_down(x0):
        weight_grad(DD, GO, HID[...], x0, FP)

    def grad_a(x0):
        weight_grad(WA, N, GGU[:, :, 0:GA_N], x0, GA_N)

    def grad_b(x0):
        weight_grad(WB, N, GGU[:, :, GA_N:], x0, 1792 - GA_N)

    jd = reduce_plane(net, DD, SD, *sd)
    ja = reduce_plane(net, WA, SA, *sa)
    jb = reduce_plane(net, WB, SB_, *sb)
    for x0 in range(4):
        grad_down(x0)
    step(jd)
    act(2)
    back(2)
    r2.push(2)
    step(jd)
    act(1)
    step(r2_rest)
    back(1)
    r2.push(1)
    act(3)
    back(3)
    r2.push(3)
    act(0)
    step(r2_rest, 2)
    back(0)
    r2.push(0)
    step(jd)
    net.finish(gu_sent)
    for x0 in range(4):
        grad_a(x0)
    step(ja)
    step(r2_rest, 2)
    net.finish(r2_sent)

    def third(i, _):
        at = pl.ds(pl.multiple_of(i * 16, 16), 16)
        v = resid[at]
        inv = lax.rsqrt(jnp.mean(v * v, axis=1, keepdims=True) + epsilon)
        x = v * inv
        w = g_ffn * GR[at]
        g = GO[p.z, p.c, at].astype(F32) + inv * (w - x * jnp.mean(w * x, axis=1, keepdims=True))
        GR[at] = g
        T[p.z, p.c, at] = g.astype(BF)

    lax.fori_loop(0, ROWS // 16, third, None, unroll=2)
    g3 = gather_ring(net, T.at[p.z, p.c], T, g3_sent)
    step(g3)
    reloaded = net.copy(spill, PA)
    step(ja)
    for x0 in range(4):
        grad_b(x0)
    step(jb)
    KP[...] = jnp.zeros(KP.shape, F32)

    def unmix(j):
        zj = block(j)
        o = whole(WC, slice(128, 384))
        gm = dot(T[zj].reshape(256, D), o, NN)
        gm = jnp.concatenate([gm[:, :128], jnp.where(lanes, gm[:, 128:], 0.0)], axis=1).reshape(2, 128, 256)
        for cc in range(2):
            gc = gm[cc] * conv(zj, cc)
            at = slice(128 * cc, 128 * cc + 128)
            GGU[zj, at, 0:128] = gc[:, :128].astype(BF)
            GGU[zj, at, 128:256] = jnp.zeros((128, 128), BF)
            GGU[zj, at, 256:384] = pltpu.roll(gc[:, 128:], 64, 1).astype(BF)
            gv = gm[cc] * C[zj, cc].astype(F32)
            GC[zj + 1, cc, 0:128] = gv
            for i in range(3):
                KP[i : i + 1] = KP[i : i + 1] + jnp.sum(gv * BX[zj, cc, 8 - i : 136 - i], axis=0, keepdims=True)
        net.send(GC.at[zj + 1, :, 0:8], GC.at[zj + p.yl, :, 128:136], halo_back + j, p.at(y=p.y + 1 - 2 * p.yl))

    step(g3)
    unmix(0)
    net.finish(g2_sent)
    down(0)
    down(1)
    step(jb)
    down(2)
    down(3)
    step(jd)
    step(g3)
    step(g3)
    unmix(1)
    unmix(3)
    step(g3, 2)
    unmix(2)
    r4 = ReduceRing(net, N, MR, *ring_a)
    r4_sent, r4_rest = r4.mine, r4.rest()
    for j in (2, 1, 3, 0):
        r4.push(j)
    step(ja)
    reloaded()
    net.finish(w_sent)
    DE = WD.at[:, :, :, :, 0:384]
    for x0 in range(4):
        at = slice(384 * x0, 384 * x0 + 384)
        w = dot(PA[:, :, :, at].reshape(1024, 384), GGU[:, :, 0:384].reshape(1024, 384), TN)
        m = dot(T[:, :, :, at].reshape(1024, 384), MX[...].reshape(1024, 256), TN)
        w = jnp.concatenate([w[:, :128], m[:, :128], w[:, 256:] + m[:, 128:]], axis=1)
        DE[x0] = w.astype(BF).reshape(2, 2, 96, 384)
        if x0 == 1:
            step(r4_rest)
    je = reduce_plane(net, DE, SC.at[:, 0:384], *se)
    for j in range(4):
        net.got(GC.at[block(j) + 1 - p.yl, :, 128:136], halo_back + j)
    r3 = ReduceRing(net, GO, R1, *ring_b)
    r3_sent, r3_rest = r3.mine, r3.rest()

    def unproject(j):
        zj = block(j)
        for cc in range(2):
            at = slice(128 * cc, 128 * cc + 128)
            gb = taps[0] * GC[zj + 1, cc, 0:128] + taps[1] * GC[zj + 1, cc, 1:129] + taps[2] * GC[zj + 1, cc, 2:130]
            bb, vv = gb * V[zj, cc].astype(F32), gb * B[zj, cc].astype(F32)
            GGU[zj, at, 384:512] = bb[:, :128].astype(BF)
            GGU[zj, at, 512:640] = vv[:, :128].astype(BF)
            GGU[zj, at, 640:768] = (bb[:, 128:] + pltpu.roll(vv[:, 128:], 64, 1)).astype(BF)
        GO[zj] = dot(GGU[zj, :, 0:768], whole(WC), NT).astype(BF).reshape(2, 128, D)
        r3.push(j)

    step(jd)
    unproject(2)
    step(je, 2)
    unproject(1)
    step(r3_rest)
    step(r4_rest)
    unproject(3)
    unproject(0)
    step(r3_rest)
    step(jd)
    for who in partners:
        pl.semaphore_signal(free, inc=1, device_id=who, device_id_type=MESH)
    step(jb)
    step(r4_rest)
    DC = DD.at[:, :, :, :, 0:384]
    for x0 in range(4):
        at = slice(384 * x0, 384 * x0 + 384)
        w = dot(PA[:, :, :, at].reshape(1024, 384), GGU[:, :, 384:768].reshape(1024, 384), TN)
        DC[x0] = w.astype(BF).reshape(2, 2, 96, 384)
    step(je)
    step(ja)
    pl.semaphore_wait(free, len(partners))
    jc = reduce_plane(net, DC, SC.at[:, 384:768], *[r.at[(slice(None),) * (len(r.shape) - 1) + (slice(0, 384),)] for r in sd])
    jk = reduce_plane(net, KG, SK, *sk)
    step(jc, 2)

    def gain_rows(i, v):
        zj = i // 8
        at = pl.ds(pl.multiple_of(i % 4 * 32, 32), 32)
        cc = i // 4 % 2
        g = GO[zj, cc, at].astype(F32) * PA[zj, cc, at].astype(F32)
        return v + (g[0:8] + g[8:16]) + (g[16:24] + g[24:32])

    mix_row = jnp.sum(lax.fori_loop(0, 32, gain_rows, jnp.zeros((8, D), F32)), axis=0, keepdims=True)
    mix_row = jnp.concatenate([mix_row / g_mix, jnp.zeros((1, 128), F32)], axis=1)
    low = lax.broadcasted_iota(jnp.int32, (1, 256), 1) < 96
    for s in range(16):
        at = (96 * s) // 128 * 128
        row = mix_row[:, at : at + 256]
        row = row if 96 * s == at else pltpu.roll(row, 256 - (96 * s - at), 1)
        tile = jnp.concatenate([KP[...], jnp.where(low, row, 0.0), jnp.zeros((23, 256), F32)], axis=0)
        KG[s // 4, (s // 2) % 2, s % 2] = tile.astype(BF)
    step(jk, 2)
    step(jb)
    step(ja)
    step(r3_rest)
    step(je)
    step(jk)
    step(jc)
    step(r4_rest)
    step(ja)
    step(jb)
    step(jk)
    step(r3_rest)
    step(jb)
    step(je)
    ffn_share = jnp.sum(SA[...] * gu_s[:, 0:GA_N].astype(F32), axis=1, keepdims=True)
    ffn_share += jnp.sum(SB_[...] * gu_s[:, GA_N:].astype(F32), axis=1, keepdims=True)
    both = jnp.concatenate([jnp.broadcast_to(ffn_share, (96, 128)), jnp.zeros((32, 128), F32)], axis=0).T
    step(jk)
    step(jc)
    step(r4_rest)
    step(jk)
    X[0:16] = SK[0:16]
    X[9:10, 0:96] = both[0:1, 0:96] / gf_w[...].astype(F32)
    me = lax.axis_index("tensor")
    done = net.copy(X, XR.at[me])
    base = net.sem(8)
    for i in range(1, 8):
        net.send(X, XR.at[me], base + i, (lax.axis_index("dp"), (me + i) % 8))
    step(je)
    step(jc)
    step(r3_rest)

    def last(i, _):
        at = pl.ds(pl.multiple_of(i * 16, 16), 16)
        lv = live_rows(lens, i * 16, 16)
        layer_out[at] = (lv * (resid[at] + MR[at])).astype(BF)
        v = tok[at].astype(F32)
        inv = lax.rsqrt(jnp.mean(v * v, axis=1, keepdims=True) + epsilon)
        x = v * inv
        w = g_mix * R1[at]
        g = GR[at] + inv * (w - x * jnp.mean(w * x, axis=1, keepdims=True))
        tokens_grad[at] = g.astype(BF)

    lax.fori_loop(0, ROWS // 16, last, None, unroll=2)
    step(jc)
    for i in range(1, 8):
        net.got(XR.at[(me + 8 - i) % 8], base + i)
    done()
    for job in (gt, go, g2, g3, am, ac, ae, ad, au, av, r1_rest, r2_rest, r3_rest, r4_rest, ja, jb, jd, jc, je, jk):
        assert next(job, "end") == "end"
    assert max(net.ns, net.nr) <= SEMS and net.nl <= 24
    net.finish(r3_sent + r4_sent + g3_sent + w_sent)
    net.finish()


GA_N = 1024
SEMS = 480


def train_call(*args):
    any_, vm = pl.BlockSpec(memory_space=pl.ANY), pl.BlockSpec(memory_space=pltpu.VMEM)
    ring, wide = (4, 2, ROWS, D), (4, 2, ROWS, 256)
    outs = [shape((ROWS, D)), shape((ROWS, D))]
    outs += [shape((96, n), F32) for n in (GA_N, 1792 - GA_N, FP, 768)] + [shape((8, 16, 256), F32), shape(ring)]
    v = lambda s, t=BF: pltpu.VMEM(s, t)
    scratch = [v((ROWS, D), F32), v((32, D), F32)] + [v((ROWS, D), F32)] * 3
    scratch += [v((96, 768)), v((96, 1792)), v((96, FP)), v((32, 256)), v((256, 128), F32)]
    scratch += [v(ring)] * 3 + [v((4, 2, 2, 96, n)) for n in (768, 1792, FP)] + [v((4, 2, 2, 32, 256))]
    scratch += [v(wide)] * 3 + [v((5, 2, 136, 256), F32), v(wide), v((5, 2, 136, 256), F32)]
    scratch += [v((4, 256, FP)), v((4, 256, 1792)), v(ring), v((4, 2, 2, 96, FP)), v((8, 256), F32)]
    scratch += plane_scratch(GA_N) + plane_scratch(1792 - GA_N) + plane_scratch(FP) + plane_scratch(256, 16) + plane_scratch(384)
    scratch += ring_scratch(D) * 2 + [v((4, 2, 2, 32, 256)), v((16, 256), F32), v((32, 256), F32)]
    scratch += [pltpu.SemaphoreType.REGULAR]
    scratch += [pltpu.SemaphoreType.DMA((SEMS,)), pltpu.SemaphoreType.DMA((SEMS,)), pltpu.SemaphoreType.DMA((24,))]
    *sums, _ = pl.pallas_call(
        train_kernel,
        out_shape=tuple(outs),
        in_specs=[vm] * 11,
        out_specs=tuple([vm] * 7 + [any_]),
        scratch_shapes=scratch,
        compiler_params=pltpu.CompilerParams(
            collective_id=0, has_side_effects=True, vmem_limit_bytes=64 << 20),
        name="train",
    )(*args)
    return sums


def finish_kernel(lo, tg, SA, SB, SD, SC, XR,
                  layer_out, tokens_grad, mix, in_grad, taps, out_grad, ffn, gate, up, down, flip):
    layer_out[...] = lo[...]
    tokens_grad[...] = tg[...]
    for t in range(7):
        n = 96 if t == 6 else 128
        src, at = (SA, 256 * t) if t < 4 else (SB, 256 * t - 1024)
        gate[:, 128 * t : 128 * t + n] = src[:, at : at + n]
        up[:, 128 * t : 128 * t + n] = src[:, at + 128 : at + 128 + n]
    down[...] = SD[:, 0:FB]
    flip[96:128] = jnp.zeros((32, 256), F32)
    flip[0:96] = SC[:, 128:384]
    out_grad[...] = flip[...].T[0:CH, 0:96]
    for i in range(3):
        at = (384, 0, 512)[i]
        in_grad[i, :, 0:128] = SC[:, at : at + 128]
    in_grad[0, :, 128:192] = SC[:, 640:704]
    in_grad[1, :, 128:192] = pltpu.roll(SC[:, 256:384], 64, 1)[:, :64]
    in_grad[2, :, 128:192] = pltpu.roll(SC[:, 640:768], 64, 1)[:, :64]
    dp, t = lax.axis_index("dp"), lax.axis_index("tensor")
    shares = XR[0, 8:16]
    for i in range(1, 8):
        shares = shares + XR[i, 8:16]
    shares = pltpu.roll(shares, 256 - 12 * t, 1)
    mix[...] = shares[0:1, 0:12]
    ffn[...] = shares[1:2, 0:12]
    k = pltpu.roll(XR[dp // 2, 0:8], lax.rem(256 - 12 * ((dp * 8 + t) % 16), 256), 1)
    taps[...] = k[0:3, 0:12]


def finish_call(*args):
    vm = pl.BlockSpec(memory_space=pltpu.VMEM)
    outs = [shape((ROWS, D)), shape((ROWS, D)), shape((1, 12), F32), shape((3, 96, CH), F32), shape((3, 12), F32)]
    outs += [shape((CH, 96), F32), shape((1, 12), F32), shape((96, FB), F32), shape((96, FB), F32), shape((96, FB), F32)]
    return pl.pallas_call(
        finish_kernel,
        out_shape=tuple(outs),
        in_specs=[vm] * 7,
        out_specs=tuple([vm] * 10),
        scratch_shapes=[pltpu.VMEM((128, 256), F32)],
        compiler_params=pltpu.CompilerParams(vmem_limit_bytes=VMEM_LIMIT),
        name="finish",
    )(*args)


def per_device(tokens, gain_mix, in_weight, conv_kernel, out_weight, gain_ffn, gate_weight, up_weight, down_weight, lengths, cotangent):
    gm, gf, lens = gain_mix.reshape(1, 96), gain_ffn.reshape(1, 96), lengths.reshape(1, 1)
    sums = train_call(
        tokens, cotangent, lens, in_weight.transpose(1, 0, 2), out_weight, gate_weight, up_weight,
        down_weight.T, gm, gf, conv_kernel)
    layer_out, tokens_grad, mix, in_grad, taps_grad, out_grad, ffn, gate, up, down = finish_call(*sums)
    return layer_out, tokens_grad, mix[0], in_grad.transpose(1, 0, 2), taps_grad, out_grad, ffn[0], gate, up, down.T


def solution(mesh):
    placed = (
        P(("dp", "tensor"), None),
        P("dp"),
        P("dp", None, "tensor"),
        P(None, "tensor"),
        P("tensor", "dp"),
        P("dp"),
        P("dp", "tensor"),
        P("dp", "tensor"),
        P("tensor", "dp"),
        P("dp"),
        P(("dp", "tensor"), None),
    )
    return jax.shard_map(
        per_device,
        mesh=mesh,
        in_specs=placed,
        out_specs=(
            P(("dp", "tensor"), None),
            P(("dp", "tensor"), None),
            P(("dp", "tensor")),
            P("dp", None, "tensor"),
            P(None, ("dp", "tensor")),
            P("tensor", "dp"),
            P(("dp", "tensor")),
            P("dp", "tensor"),
            P("dp", "tensor"),
            P("tensor", "dp"),
        ),
        check_vma=False,
    )
```

```python
import functools

import jax
import jax.numpy as jnp
from jax import lax
from jax.experimental import pallas as pl
from jax.experimental.pallas import tpu as pltpu
from jax.sharding import PartitionSpec as P

epsilon = 1e-05
MESH = pl.DeviceIdType.MESH
BF = jnp.bfloat16
F32 = jnp.float32
D = 1536
ROWS = 128
CH = 192
FB = 864
FP = 896
HALF = 48
VMEM_LIMIT = 60 << 20


class Place:
    def __init__(self):
        dp = lax.axis_index("dp")
        t = lax.axis_index("tensor")
        self.x, self.yh, self.c = dp // 4, (dp // 2) % 2, dp % 2
        self.z, self.yl = t // 2, t % 2
        self.y = self.yh * 2 + self.yl
        self.o = 1 - self.c
        self.xp, self.xm, self.x2 = (self.x + 1) % 4, (self.x + 3) % 4, (self.x + 2) % 4
        self.yp, self.ym = (self.y + 1) % 4, (self.y + 3) % 4
        self.y2 = (self.y + 2) % 4
        self.yhp, self.yhm = self.yp // 2, self.ym // 2
        self.way = 1 - 2 * self.c
        self.zf = (self.z + self.way + 4) % 4
        self.zb = (self.z - self.way + 4) % 4
        self.zp, self.zm, self.z2 = (self.z + 1) % 4, (self.z + 3) % 4, (self.z + 2) % 4
        self.own = self.c == self.yl
        self.opp = self.c != self.yl

    def at(self, x=None, y=None, z=None, c=None):
        x = self.x if x is None else x
        y = self.y if y is None else y
        z = self.z if z is None else z
        c = self.c if c is None else c
        return (x * 4 + (y // 2) * 2 + c, z * 2 + y % 2)


class Net:
    def __init__(self, place, send, recv, local=None):
        self.p, self.ss, self.rs, self.ls = place, send, recv, local
        self.ns = self.nr = self.nl = 0
        self.pending = []

    def sem(self, n=1):
        k = self.nr
        self.nr += n
        return k

    def send(self, src, dst, recv_index, target, cond=None, pending=None):
        k = self.ns
        self.ns += 1
        d = pltpu.make_async_remote_copy(
            src_ref=src, dst_ref=dst, send_sem=self.ss.at[k], recv_sem=self.rs.at[recv_index],
            device_id=target, device_id_type=MESH)
        run(cond, d.start)
        (self.pending if pending is None else pending).append((cond, d))

    def copy(self, src, dst, cond=None):
        k = self.nl
        self.nl += 1
        d = pltpu.make_async_copy(src, dst, self.ls.at[k])
        run(cond, d.start)
        return lambda: run(cond, d.wait)

    def got(self, dst, recv_index, cond=None):
        d = pltpu.make_async_remote_copy(
            src_ref=dst, dst_ref=dst, send_sem=self.ss.at[0], recv_sem=self.rs.at[recv_index],
            device_id=self.p.at(c=self.p.o), device_id_type=MESH)
        run(cond, d.wait_recv)

    def finish(self, pending=None):
        pending = self.pending if pending is None else pending
        for cond, d in pending:
            run(cond, d.wait_send)
        pending.clear()


def run(cond, f):
    if cond is None:
        f()
    else:
        pl.when(cond)(f)


def greet(p, plane, ring, group=False):
    bar = pltpu.get_barrier_semaphore()
    who = [p.at(c=p.o)]
    if plane:
        for c in (0, 1):
            who += [p.at(x=p.xp, c=c), p.at(x=p.xm, c=c), p.at(y=p.yp, c=c), p.at(y=p.ym, c=c)]
            who += [p.at(x=p.x2, c=c), p.at(y=p.y2, c=c)]
    if group:
        me = lax.axis_index("tensor")
        who += [(lax.axis_index("dp"), (me + i) % 8) for i in range(1, 8)]
    elif ring:
        who += [p.at(z=p.zp), p.at(z=p.zm)]
    for w in who:
        pl.semaphore_signal(bar, inc=1, device_id=w, device_id_type=MESH)
    return lambda: pl.semaphore_wait(bar, len(who))


def add(out, *terms):
    lead = out.shape[:-2]
    count = 1
    for s in lead:
        count *= s

    def one(i):
        at = []
        for s in reversed(lead):
            at.append(i % s)
            i = i // s
        at = tuple(reversed(at))
        v = terms[0][at].astype(F32) if at else terms[0][...].astype(F32)
        for t in terms[1:]:
            v = v + (t[at] if at else t[...]).astype(F32)
        if at:
            out[at] = v.astype(out.dtype)
        else:
            out[...] = v.astype(out.dtype)

    if not lead:

        def rows(i, _):
            at = pl.ds(pl.multiple_of(i * 16, 16), 16)
            v = terms[0][at].astype(F32)
            for t in terms[1:]:
                v = v + t[at].astype(F32)
            out[at] = v.astype(out.dtype)

        lax.fori_loop(0, out.shape[0] // 16, rows, None)
    else:
        lax.fori_loop(0, count, lambda i, _: one(i), None)


def ring_scratch(n):
    return [pltpu.VMEM((4, ROWS, n), BF), pltpu.VMEM((3, ROWS, n), BF)]


def shape(s, t=BF):
    return jax.ShapeDtypeStruct(s, t)


def slots(n):
    return shape((4, 2, 2, 96, n))


def gather_plane(net, sh, W, mine, far=False):
    p = net.p
    send = functools.partial(net.send, pending=mine)
    h = sh.shape[0] // 2
    HA, HB = pl.ds(0, h), pl.ds(h, h)
    i_own, f1, f2, f3, f4 = net.sem(), net.sem(2), net.sem(2), net.sem(2), net.sem(2)
    r1, r2, r3, r4, y1, y2, y3, y4, x1, x2, x3, x4 = (net.sem() for _ in range(12))
    f5, f6 = net.sem(2), net.sem(2)
    q = p.yl

    def pass_near():
        net.got(W.at[p.xm, p.yh, 0, HA], f1 + 0, p.own)
        net.got(W.at[p.x, p.yhm, 0, HB], f3 + 0, p.opp)
        send(W.at[p.xm, p.yh, 0, HA], W.at[p.xm, p.yh, 0, HA], r1, p.at(x=p.xp), p.own)
        send(W.at[p.x, p.yhm, 0, HB], W.at[p.x, p.yhm, 0, HB], r3, p.at(y=p.yp), p.opp)
        net.got(W.at[p.xp, p.yh, 1, HA], f2 + 1, p.own)
        net.got(W.at[p.x, p.yhp, 1, HB], f4 + 1, p.opp)
        send(W.at[p.xp, p.yh, 1, HA], W.at[p.xp, p.yh, 1, HA], r2, p.at(x=p.xm), p.own)
        send(W.at[p.x, p.yhp, 1, HB], W.at[p.x, p.yhp, 1, HB], r4, p.at(y=p.ym), p.opp)
        yield

    done = net.copy(sh, W.at[p.x, p.yh, p.c], p.own)
    send(sh.at[HA], W.at[p.x, p.yh, p.c, HA], f1 + p.c, p.at(x=p.xp, c=q))
    send(sh.at[HA], W.at[p.x, p.yh, p.c, HA], f2 + p.c, p.at(x=p.xm, c=q))
    send(sh.at[HB], W.at[p.x, p.yh, p.c, HB], f3 + p.c, p.at(y=p.yp, c=q))
    send(sh.at[HB], W.at[p.x, p.yh, p.c, HB], f4 + p.c, p.at(y=p.ym, c=q))
    send(sh, W.at[p.x, p.yh, p.c], i_own, p.at(c=p.o), p.opp)
    if far:
        send(sh.at[HA], W.at[p.x, p.yh, p.c, HA], f5 + p.c, p.at(x=p.x2, c=q))
        send(sh.at[HB], W.at[p.x, p.yh, p.c, HB], f6 + p.c, p.at(y=p.y2, c=q))
    yield
    if not far:
        yield from pass_near()
    done()
    net.got(W.at[p.x, p.yh, p.o], i_own, p.own)
    net.got(W.at[p.xm, p.yh, 1, HA], f1 + 1, p.own)
    net.got(W.at[p.xp, p.yh, 0, HA], f2 + 0, p.own)
    net.got(W.at[p.x, p.yhm, 1, HB], f3 + 1, p.opp)
    net.got(W.at[p.x, p.yhp, 0, HB], f4 + 0, p.opp)
    if far:
        net.got(W.at[p.xm, p.yh, 0, HA], f1 + 0, p.own)
        net.got(W.at[p.xp, p.yh, 1, HA], f2 + 1, p.own)
        net.got(W.at[p.x, p.yhm, 0, HB], f3 + 0, p.opp)
        net.got(W.at[p.x, p.yhp, 1, HB], f4 + 1, p.opp)
    for cc in range(2):
        net.got(W.at[p.x2, p.yh, cc, HA], f5 + cc if far else (r1, r2)[cc], p.own)
    send(W.at[:, p.yh, :, HA], W.at[:, p.yh, :, HA], y1, p.at(y=p.yp), p.own)
    send(W.at[:, p.yh, :, HA], W.at[:, p.yh, :, HA], y2, p.at(y=p.ym), p.own)
    for cc in range(2):
        net.got(W.at[p.x, 1 - p.yh, cc, HB], f6 + cc if far else (r3, r4)[cc], p.own)
    send(W.at[p.x, :, :, HB], W.at[p.x, :, :, HB], x1, p.at(x=p.xp))
    send(W.at[p.x, :, :, HB], W.at[p.x, :, :, HB], x2, p.at(x=p.xm))
    yield
    net.got(W.at[p.xm, :, :, HB], x1)
    send(W.at[p.xm, :, 0, HB], W.at[p.xm, :, 0, HB], x3, p.at(x=p.xp))
    net.got(W.at[p.xp, :, :, HB], x2)
    send(W.at[p.xp, :, 1, HB], W.at[p.xp, :, 1, HB], x4, p.at(x=p.xm))
    net.got(W.at[:, p.yhm, :, HA], y1, p.opp)
    send(W.at[:, p.yhm, 0, HA], W.at[:, p.yhm, 0, HA], y3, p.at(y=p.yp), p.opp)
    net.got(W.at[:, p.yhp, :, HA], y2, p.opp)
    send(W.at[:, p.yhp, 1, HA], W.at[:, p.yhp, 1, HA], y4, p.at(y=p.ym), p.opp)
    yield
    net.got(W.at[:, 1 - p.yh, 0, HA], y3, p.own)
    net.got(W.at[:, 1 - p.yh, 1, HA], y4, p.own)
    net.got(W.at[p.x2, :, 0, HB], x3)
    net.got(W.at[p.x2, :, 1, HB], x4)


PARTS = [pl.ds(0, 64), pl.ds(64, 64)]


def gather_ring(net, a, out, mine, late=False):
    p = net.p
    send = functools.partial(net.send, pending=mine)
    s1, s3, s2 = net.sem(2), net.sem(2), net.sem(2)
    k = net.sem(8)
    jf, jb = (p.zf - p.z + 4) % 4, (p.zb - p.z + 4) % 4
    for i, r in enumerate(PARTS):
        send(a.at[r], out.at[p.z, p.c, r], s1 + i, p.at(z=p.zf))
        send(a.at[r], out.at[p.z, p.c, r], s3 + i, p.at(z=p.zb))
    for i, r in enumerate(PARTS):
        send(a.at[r], out.at[p.z, p.c, r], k + 4 * i, p.at(c=p.o))
    yield
    for i, r in enumerate(PARTS):
        net.got(out.at[p.z, p.o, r], k + 4 * i)
    yield
    for i, r in enumerate(PARTS):
        net.got(out.at[p.zb, p.c, r], s1 + i)
        if not late:
            send(out.at[p.zb, p.c, r], out.at[p.zb, p.c, r], s2 + i, p.at(z=p.zf))
        send(out.at[p.zb, p.c, r], out.at[p.zb, p.c, r], k + 4 * i + jb, p.at(c=p.o))
        net.got(out.at[p.zf, p.c, r], s3 + i)
        send(out.at[p.zf, p.c, r], out.at[p.zf, p.c, r], k + 4 * i + jf, p.at(c=p.o))
        yield
    for i, r in enumerate(PARTS):
        net.got(out.at[p.zp, p.o, r], k + 4 * i + 1)
        net.got(out.at[p.zm, p.o, r], k + 4 * i + 3)
    yield
    if late:
        for i, r in enumerate(PARTS):
            send(out.at[p.zb, p.c, r], out.at[p.zb, p.c, r], s2 + i, p.at(z=p.zf))
        yield
    for i, r in enumerate(PARTS):
        net.got(out.at[p.z2, p.c, r], s2 + i)
        send(out.at[p.z2, p.c, r], out.at[p.z2, p.c, r], k + 4 * i + 2, p.at(c=p.o))
    yield
    for i, r in enumerate(PARTS):
        net.got(out.at[p.z2, p.o, r], k + 4 * i + 2)


class ReduceRing:
    def __init__(self, net, V, out, RC, RZ):
        self.net, self.V, self.out, self.RC, self.RZ = net, V, out, RC, RZ
        self.s2, self.sd, self.sr, self.k = net.sem(2), net.sem(2), net.sem(2), net.sem(8)
        self.mine = []
        self.send = functools.partial(net.send, pending=self.mine)

    def push(self, j):
        p = self.net.p
        for i, r in enumerate(PARTS):
            self.send(self.V.at[(p.z + j) % 4, p.o, r], self.RC.at[j, r], self.k + 4 * i + j, p.at(c=p.o))

    def rest(self):
        net, p, V, RC, RZ, k = self.net, self.net.p, self.V, self.RC, self.RZ, self.k
        jf, jb = (p.zf - p.z + 4) % 4, (p.zb - p.z + 4) % 4
        for i, r in enumerate(PARTS):
            net.got(RC.at[2, r], k + 4 * i + 2)
            add(RC.at[2, r], V.at[p.z2, p.c, r], RC.at[2, r])
            self.send(RC.at[2, r], RZ.at[0, r], self.s2 + i, p.at(z=p.zf))
        yield
        for i, r in enumerate(PARTS):
            net.got(RC.at[jb, r], k + 4 * i + jb)
            add(RC.at[jb, r], V.at[p.zb, p.c, r], RC.at[jb, r])
            self.send(RC.at[jb, r], RZ.at[1, r], self.sd + i, p.at(z=p.zb))
        for i, r in enumerate(PARTS):
            net.got(RC.at[jf, r], k + 4 * i + jf)
            add(RC.at[jf, r], V.at[p.zf, p.c, r], RC.at[jf, r])
        yield
        for i, r in enumerate(PARTS):
            net.got(RZ.at[0, r], self.s2 + i)
            add(RC.at[jf, r], RC.at[jf, r], RZ.at[0, r])
            self.send(RC.at[jf, r], RZ.at[2, r], self.sr + i, p.at(z=p.zf))
        yield
        for i, r in enumerate(PARTS):
            net.got(RC.at[0, r], k + 4 * i)
            add(RC.at[0, r], V.at[p.z, p.c, r], RC.at[0, r])
        yield
        for i, r in enumerate(PARTS):
            net.got(RZ.at[1, r], self.sd + i)
            net.got(RZ.at[2, r], self.sr + i)
            add(self.out.at[r], RC.at[0, r], RZ.at[1, r], RZ.at[2, r])


def step(job, times=1):
    for _ in range(times):
        next(job, None)


def dot(a, b, dims):
    return lax.dot_general(a, b, (dims, ((), ())), preferred_element_type=F32)


NN, NT, TN = ((1,), (0,)), ((1,), (1,)), ((0,), (0,))


def whole(ref, columns=slice(None)):
    v = ref[:, :, :, :, columns]
    return v.reshape(D, v.shape[-1])


def row_norm(src, dst, gain, rows=32):
    def one(i, _):
        at = pl.ds(pl.multiple_of(i * rows, rows), rows)
        v = src[at].astype(F32)
        inv = lax.rsqrt(jnp.mean(v * v, axis=1, keepdims=True) + epsilon)
        dst[at] = (v * inv * gain).astype(dst.dtype)

    lax.fori_loop(0, ROWS // rows, one, None, unroll=2)


def live_rows(lens, first=0, rows=ROWS):
    at = lax.axis_index("tensor") * ROWS + first + lax.broadcasted_iota(jnp.int32, (rows, 1), 0)
    return jnp.where(at < lens[...], 1.0, 0.0).astype(F32)


def plane_scratch(n, h=HALF):
    return [
        pltpu.VMEM((2, 4, h, n), BF),
        pltpu.VMEM((2, 4, 2, h, n), BF),
        pltpu.VMEM((2, h, n), BF),
        pltpu.VMEM((3, h, n), BF),
        pltpu.VMEM((2, 2, h, n), BF),
        pltpu.VMEM((2, 2, 2, h, n), BF),
        pltpu.VMEM((2, h, n), BF),
        pltpu.VMEM((3, h, n), BF),
    ]


def reduce_plane(net, G, out, RA, RB, RC, F, RX, RY, RZ, H):
    p = net.p
    h = out.shape[0] // 2
    HA, HB = pl.ds(0, h), pl.ds(h, h)
    mine = []
    send = functools.partial(net.send, pending=mine)
    a0, a1, bp0, bp1, bm0, bm1, c0, c1, g0, g1, g2 = (net.sem() for _ in range(11))
    u0, u1, vp0, vp1, vm0, vm1, w0, w1, h0, h1, h2 = (net.sem() for _ in range(11))
    send(G.at[:, 1 - p.yh, 0, HA], RA.at[0], a0, p.at(y=p.ym), p.own)
    send(G.at[:, 1 - p.yh, 1, HA], RA.at[1], a1, p.at(y=p.yp), p.own)
    send(G.at[p.x2, :, 0, HB], RX.at[0], u0, p.at(x=p.xm))
    send(G.at[p.x2, :, 1, HB], RX.at[1], u1, p.at(x=p.xp))
    yield
    send(G.at[:, p.yhm, 1, HA], RB.at[0, :, 1], bp1, p.at(y=p.ym), p.opp)
    send(G.at[:, p.yhp, 0, HA], RB.at[1, :, 0], bm0, p.at(y=p.yp), p.opp)
    send(G.at[p.xm, :, 1, HB], RY.at[0, :, 1], vp1, p.at(x=p.xm))
    send(G.at[p.xp, :, 0, HB], RY.at[1, :, 0], vm0, p.at(x=p.xp))
    yield

    net.got(RX.at[0], u0)
    add(RX.at[0], RX.at[0], G.at[p.xm, :, 0, HB])
    send(RX.at[0], RY.at[0, :, 0], vp0, p.at(x=p.xm))
    net.got(RX.at[1], u1)
    add(RX.at[1], RX.at[1], G.at[p.xp, :, 1, HB])
    send(RX.at[1], RY.at[1, :, 1], vm1, p.at(x=p.xp))
    net.got(RA.at[0], a0, p.opp)
    net.got(RA.at[1], a1, p.opp)

    @pl.when(p.opp)
    def _():
        add(RA.at[0], RA.at[0], G.at[:, p.yhm, 0, HA])
        add(RA.at[1], RA.at[1], G.at[:, p.yhp, 1, HA])

    send(RA.at[0], RB.at[0, :, 0], bp0, p.at(y=p.ym), p.opp)
    send(RA.at[1], RB.at[1, :, 1], bm1, p.at(y=p.yp), p.opp)
    yield

    net.got(RY.at[0, :, 1], vp1)
    net.got(RY.at[1, :, 0], vm0)
    net.got(RY.at[0, :, 0], vp0)
    net.got(RY.at[1, :, 1], vm1)
    add(RY.at[0], RY.at[0], RY.at[1], G.at[p.x, :, :, HB])
    T = RY.at[0]
    send(T.at[1 - p.yh, 0], RZ.at[0], w0, p.at(y=p.ym), p.own)
    send(T.at[1 - p.yh, 1], RZ.at[1], w1, p.at(y=p.yp), p.own)
    send(T.at[p.yhm, 1], H.at[1], h1, p.at(y=p.ym, c=1), p.opp)
    send(T.at[p.yhp, 0], H.at[2], h2, p.at(y=p.yp, c=0), p.opp)
    send(T.at[p.yh, p.o], H.at[0], h0, p.at(c=p.o), p.own)

    net.got(RB.at[0, :, 1], bp1, p.own)
    net.got(RB.at[1, :, 0], bm0, p.own)
    net.got(RB.at[0, :, 0], bp0, p.own)
    net.got(RB.at[1, :, 1], bm1, p.own)

    @pl.when(p.own)
    def _():
        add(RB.at[0], RB.at[0], RB.at[1], G.at[:, p.yh, :, HA])

    S = RB.at[0]
    send(S.at[p.x2, 0], RC.at[0], c0, p.at(x=p.xm), p.own)
    send(S.at[p.x2, 1], RC.at[1], c1, p.at(x=p.xp), p.own)
    send(S.at[p.xm, 1], F.at[1], g1, p.at(x=p.xm, c=1), p.own)
    send(S.at[p.xp, 0], F.at[2], g2, p.at(x=p.xp, c=0), p.own)
    send(S.at[p.x, p.o], F.at[0], g0, p.at(c=p.o), p.own)
    yield

    net.got(RC.at[0], c0, p.own)
    net.got(RC.at[1], c1, p.own)
    net.got(RZ.at[0], w0, p.opp)
    net.got(RZ.at[1], w1, p.opp)

    @pl.when(p.own)
    def _():
        add(RC.at[0], RC.at[0], S.at[p.xm, 0])
        add(RC.at[1], RC.at[1], S.at[p.xp, 1])

    @pl.when(p.opp)
    def _():
        add(RZ.at[0], RZ.at[0], T.at[p.yhm, 0])
        add(RZ.at[1], RZ.at[1], T.at[p.yhp, 1])

    send(RC.at[0], F.at[1], g1, p.at(x=p.xm, c=0), p.own)
    send(RC.at[1], F.at[2], g2, p.at(x=p.xp, c=1), p.own)
    send(RZ.at[0], H.at[1], h1, p.at(y=p.ym, c=0), p.opp)
    send(RZ.at[1], H.at[2], h2, p.at(y=p.yp, c=1), p.opp)
    yield

    net.got(F.at[0], g0, p.opp)
    net.got(F.at[1], g1)
    net.got(F.at[2], g2)
    net.got(H.at[0], h0, p.opp)
    net.got(H.at[1], h1)
    net.got(H.at[2], h2)
    net.finish(mine)

    @pl.when(p.own)
    def _():
        F[0] = S[p.x, p.c]
        H[0] = T[p.yh, p.c]

    add(out.at[HA], F.at[0], F.at[1], F.at[2])
    add(out.at[HB], H.at[0], H.at[1], H.at[2])


def direct_scratch(n, h=HALF):
    return [
        pltpu.VMEM((3, 4, 2, h, n), BF),
        pltpu.VMEM((3, 2, 2, h, n), BF),
        pltpu.VMEM((4, h, n), BF),
        pltpu.VMEM((4, h, n), BF),
    ]


def reduce_direct(net, G, out, YA, XB, F, H):
    p = net.p
    h = out.shape[0] // 2
    HA, HB = pl.ds(0, h), pl.ds(h, h)
    mine = []
    send = functools.partial(net.send, pending=mine)
    ya, xb, f, g = net.sem(3), net.sem(3), net.sem(4), net.sem(4)
    send(G.at[:, 1 - p.yh, :, HA], YA[2], ya + 2, p.at(y=p.y2), p.own)
    send(G.at[:, p.yhm, :, HA], YA[0], ya + 0, p.at(y=p.ym), p.opp)
    send(G.at[:, p.yhp, :, HA], YA[1], ya + 1, p.at(y=p.yp), p.opp)
    send(G.at[p.x2, :, :, HB], XB[2], xb + 2, p.at(x=p.x2))
    send(G.at[p.xm, :, :, HB], XB[0], xb + 0, p.at(x=p.xm))
    send(G.at[p.xp, :, :, HB], XB[1], xb + 1, p.at(x=p.xp))
    yield

    for i in range(3):
        net.got(XB[i], xb + i)
    T = XB[0]
    add(T, XB[0], XB[1], XB[2], G.at[p.x, :, :, HB])
    send(T.at[p.yh, p.o], H[0], g + 0, p.at(c=p.o), p.own)
    for cc in range(2):
        send(T.at[1 - p.yh, cc], H[3], g + 3, p.at(y=p.y2, c=cc), p.own)
        send(T.at[p.yhm, cc], H[1], g + 1, p.at(y=p.ym, c=cc), p.opp)
        send(T.at[p.yhp, cc], H[2], g + 2, p.at(y=p.yp, c=cc), p.opp)
    for i in range(3):
        net.got(YA[i], ya + i, p.own)
    S = YA[0]

    @pl.when(p.own)
    def _():
        add(S, YA[0], YA[1], YA[2], G.at[:, p.yh, :, HA])

    send(S.at[p.x, p.o], F[0], f + 0, p.at(c=p.o), p.own)
    for cc in range(2):
        send(S.at[p.x2, cc], F[3], f + 3, p.at(x=p.x2, c=cc), p.own)
        send(S.at[p.xm, cc], F[1], f + 1, p.at(x=p.xm, c=cc), p.own)
        send(S.at[p.xp, cc], F[2], f + 2, p.at(x=p.xp, c=cc), p.own)
    yield

    net.got(F[0], f + 0, p.opp)
    net.got(H[0], g + 0, p.opp)
    for i in range(1, 4):
        net.got(F[i], f + i)
        net.got(H[i], g + i)
    net.finish(mine)

    @pl.when(p.own)
    def _():
        F[0][...] = S[p.x, p.c]
        H[0][...] = T[p.yh, p.c]

    add(out.at[HA], *F)
    add(out.at[HB], *H)


def pieces(refs):
    return [[r.at[i] for i in range(r.shape[0])] for r in refs]


def train_kernel(*refs):
    (tok, cot, lens, in_w, out_w, gate_w, up_w, down_w, gm_w, gf_w, taps_w,
     layer_out, tokens_grad, SA, SB_, SD, SC, XR, spill,
     resid, gains, GR, MR, R1, conv_s, gu_s, down_s, small_s, flip, T, N, GO, WC, WG, WD, SM, B, C, V, BX, MX, GC, HID, GGU, PA, DD, KP, GM,
     *more) = refs
    sa, sb, sd = [more[8 * i : 8 * i + 8] for i in range(3)]
    sk, se = [pieces(more[24 + 4 * i : 28 + 4 * i]) for i in range(2)]
    ring_a, ring_b = more[32:34], more[34:36]
    KG, X, SK, free, send, recv, local = more[36:]
    p = Place()
    BX[0, :, 0:8] = jnp.zeros((2, 8, 256), F32)
    GC[4, :, 128:136] = jnp.zeros((2, 8, 256), F32)
    greeted = greet(p, True, True, True)
    net = Net(p, send, recv, local)
    block = lambda j: (p.z + j) % 4
    halo, halo_back = net.sem(), net.sem(4)
    partners = [p.at(c=p.o)]
    for cc in (0, 1):
        partners += [p.at(x=p.xp, c=cc), p.at(x=p.xm, c=cc), p.at(y=p.yp, c=cc), p.at(y=p.ym, c=cc)]
        partners += [p.at(x=p.x2, c=cc), p.at(y=p.y2, c=cc)]

    WA, WB = WG.at[:, :, :, :, 0:GA_N], WG.at[:, :, :, :, GA_N:]
    gt_sent, go_sent, g2_sent, g3_sent, gu_sent, w_sent = [], [], [], [], [], []
    gt = gather_ring(net, tok, T, gt_sent)
    go = gather_ring(net, GO.at[p.z, p.c], GO, go_sent)
    am = gather_plane(net, small_s, SM, w_sent, True)
    ac = gather_plane(net, conv_s.at[:, 0:384], WC.at[:, :, :, :, 0:384], w_sent, True)
    ae = gather_plane(net, conv_s.at[:, 384:768], WC.at[:, :, :, :, 384:768], w_sent, True)
    ad = gather_plane(net, down_s, WD, w_sent, True)
    au = gather_plane(net, gu_s.at[:, 0:GA_N], WA, gu_sent)
    av = gather_plane(net, gu_s.at[:, GA_N:], WB, gu_sent, True)

    flip[0:256] = jnp.zeros((256, 128), F32)
    flip[0:CH, 0:96] = out_w[...].astype(F32)
    o = flip[0:256].T[0:96]
    side = jnp.zeros((96, 64), F32)
    w = [jnp.concatenate([in_w[i].astype(F32), side], axis=1) for i in range(3)]
    parts = [
        w[1][:, 0:128],
        o[:, 0:128],
        o[:, 128:256] + pltpu.roll(w[1][:, 128:256], 64, 1),
        w[0][:, 0:128],
        w[2][:, 0:128],
        w[0][:, 128:256] + pltpu.roll(w[2][:, 128:256], 64, 1),
    ]
    conv_s[...] = jnp.concatenate(parts, axis=1).astype(BF)
    wide_row = lambda g: jnp.concatenate([g[...].astype(F32), jnp.zeros((1, 160), F32)], axis=1)
    gain = jnp.concatenate([wide_row(gm_w), wide_row(gf_w), jnp.zeros((6, 256), F32)], axis=0)
    small_s[0:16] = jnp.concatenate(
        [pltpu.roll(gain, lax.rem(96 * lax.axis_index("dp"), 128), 1), jnp.zeros((8, 256), F32)], axis=0
    ).astype(BF)
    taps_row = jnp.concatenate([taps_w[...].astype(F32), jnp.zeros((3, 64), F32)], axis=1)
    small_s[16:32] = jnp.concatenate([taps_row, jnp.zeros((13, 256), F32)], axis=0).astype(BF)
    greeted()
    step(gt)
    step(am), step(ac), step(ae)
    live = live_rows(lens)
    GO[p.z, p.c] = (live * cot[...].astype(F32)).astype(BF)
    down_s[:, 768:FP] = jnp.zeros((96, 128), BF)
    down_s[:, 0:FB] = down_w[...]
    for t in range(7):
        n = 96 if t == 6 else 128
        if t == 6:
            gu_s[:, 1536:1792] = jnp.zeros((96, 256), BF)
        gu_s[:, 256 * t : 256 * t + n] = gate_w[:, 128 * t : 128 * t + n]
        gu_s[:, 256 * t + 128 : 256 * t + 128 + n] = up_w[:, 128 * t : 128 * t + n]
    own_tok = net.copy(tok, T.at[p.z, p.c])
    step(am)
    step(au)
    step(ac), step(ae)
    step(gt, 3)
    step(am), step(ac), step(ae)
    step(go)
    step(au)
    step(av), step(ad)
    step(gt, 2)
    step(am)
    gains[...] = jnp.zeros(gains.shape, F32)
    for s in range(16):
        piece = SM[s // 4, (s // 2) % 2, s % 2, 0:16].astype(F32)
        at = (96 * s) // 128 * 128
        n = min(256, gains.shape[1] - at)
        gains[0:16, at : at + n] = gains[0:16, at : at + n] + piece[:, :n]
    gains[16:32, 0:256] = SM[0, 0, 0, 16:32].astype(F32)
    g_mix, g_ffn = gains[0:1, :D], gains[1:2, :D]
    taps = [gains[16 + i : 17 + i, 0:256] for i in range(3)]
    own_tok()

    def norm(j):
        zj = block(j)
        for cc in range(2):
            row_norm(T.at[zj, cc], N.at[zj, cc], g_mix)

    norm(0)
    norm(1)
    norm(3)
    step(gt)
    norm(2)
    step(ac), step(ae)
    lanes = lax.broadcasted_iota(jnp.int32, (256, 128), 1) < 64

    def project(j):
        zj = block(j)
        r = dot(N[zj].reshape(256, D), whole(WC), NN)
        b1 = jnp.where(lanes, r[:, 640:768], 0.0)
        c1 = jnp.where(lanes, pltpu.roll(r[:, 256:384], 64, 1), 0.0)
        v1 = jnp.where(lanes, pltpu.roll(r[:, 640:768], 64, 1), 0.0)
        b = jnp.concatenate([r[:, 384:512], b1], axis=1)
        v = jnp.concatenate([r[:, 512:640], v1], axis=1)
        BX[zj, :, 8:136] = (b * v).reshape(2, 128, 256)
        B[zj] = b.astype(BF).reshape(2, 128, 256)
        V[zj] = v.astype(BF).reshape(2, 128, 256)
        C[zj] = jnp.concatenate([r[:, 0:128], c1], axis=1).astype(BF).reshape(2, 128, 256)

    for j in range(4):
        project(j)
    spilled = net.copy(N, spill)
    net.send(BX.at[0:4, :, 128:136], BX.at[pl.ds(p.yl, 4), :, 0:8], halo, p.at(y=p.y + 1 - 2 * p.yl))
    step(au)
    step(go, 2)
    net.finish(gt_sent)
    spilled()
    net.got(BX.at[pl.ds(1 - p.yl, 4), :, 0:8], halo)

    step(go)
    r1 = ReduceRing(net, PA, resid, *ring_a)

    def conv(zj, cc):
        return taps[0] * BX[zj, cc, 8:136] + taps[1] * BX[zj, cc, 7:135] + taps[2] * BX[zj, cc, 6:134]

    def mix(j):
        zj = block(j)
        for cc in range(2):
            MX[zj, cc] = (C[zj, cc].astype(F32) * conv(zj, cc)).astype(BF)
        o = whole(WC, slice(128, 384))
        PA[zj] = dot(MX[zj].reshape(256, 256), o, NT).astype(BF).reshape(2, 128, D)
        r1.push(j)

    r1_sent, r1_rest = r1.mine, r1.rest()
    mix(2)
    mix(1)
    step(r1_rest)
    mix(3)
    mix(0)
    step(r1_rest)
    step(av)
    step(r1_rest, 2)
    step(au)
    step(av)
    step(ad)
    step(go, 2)
    step(r1_rest)
    net.finish(r1_sent)

    def second(i, _):
        at = pl.ds(pl.multiple_of(i * 16, 16), 16)
        v = tok[at].astype(F32) + resid[at]
        resid[at] = v
        inv = lax.rsqrt(jnp.mean(v * v, axis=1, keepdims=True) + epsilon)
        N[p.z, p.c, at] = (v * inv * g_ffn).astype(BF)

    lax.fori_loop(0, ROWS // 16, second, None, unroll=4)
    g2 = gather_ring(net, N.at[p.z, p.c], N, g2_sent)
    step(g2)
    step(go)
    step(au)
    step(g2)
    step(av)

    def grad_down(x0, blocks, more=False):
        a = [GO[block(j), :, :, 384 * x0 : 384 * x0 + 384].reshape(256, 384) for j in blocks]
        w = dot(jnp.concatenate(a, axis=0), jnp.concatenate([HID[block(j)] for j in blocks], axis=0), TN)
        w = w.reshape(2, 2, 96, FP)
        DD[x0] = (DD[x0].astype(F32) + w if more else w).astype(BF)

    def ahead(j):
        zj = block(j)
        n2 = N[zj].reshape(256, D)
        for t in range(7):
            r = dot(n2, whole(WG, slice(256 * t, 256 * t + 256)), NN)
            g, u = r[:, :128], r[:, 128:]
            HID[zj, :, 128 * t : 128 * t + 128] = (g * jax.nn.sigmoid(g) * u).astype(BF)
            GGU[zj, :, 256 * t : 256 * t + 256] = r.astype(BF)

    def act(j):
        zj = block(j)
        for t in range(0, 7, 2):
            n = min(2, 7 - t)
            a = dot(GO[zj].reshape(256, D), whole(WD, slice(128 * t, 128 * (t + n))), NN)
            for i in range(n):
                ga = a[:, 128 * i : 128 * i + 128]
                at = 256 * (t + i)
                g, u = GGU[zj, :, at : at + 128].astype(F32), GGU[zj, :, at + 128 : at + 256].astype(F32)
                s = jax.nn.sigmoid(g)
                GGU[zj, :, at : at + 128] = (ga * u * s * (1.0 + g * (1.0 - s))).astype(BF)
                GGU[zj, :, at + 128 : at + 256] = (ga * g * s).astype(BF)

    def back(j):
        zj = block(j)
        PA[zj] = dot(GGU[zj], whole(WG), NT).astype(BF).reshape(2, 128, D)

    def down(j):
        zj = block(j)
        N[zj] = dot(HID[zj], whole(WD), NT).astype(BF).reshape(2, 128, D)

    ahead(0)
    step(g2, 2)
    step(ad)
    step(g2)
    ahead(1)
    ahead(3)
    for x0 in range(4):
        grad_down(x0, (0, 1, 3))
    step(g2, 2)
    ahead(2)
    step(ad)
    net.finish(go_sent)
    r2 = ReduceRing(net, PA, GR, *ring_a)
    r2_sent, r2_rest = r2.mine, r2.rest()
    def weight_grad(out, lhs, rhs, x0, n):
        a = lhs[:, :, :, 384 * x0 : 384 * x0 + 384].reshape(1024, 384)
        out[x0] = dot(a, rhs.reshape(1024, n), TN).astype(BF).reshape(2, 2, 96, n)

    def grad_a(x0):
        weight_grad(WA, N, GGU[:, :, 0:GA_N], x0, GA_N)

    def grad_b(x0):
        weight_grad(WB, N, GGU[:, :, GA_N:], x0, 1792 - GA_N)

    jd = reduce_plane(net, DD, SD, *sd)
    ja = reduce_plane(net, WA, SA, *sa)
    jb = reduce_plane(net, WB, SB_, *sb)
    act(2)
    back(2)
    r2.push(2)
    for x0 in range(4):
        grad_down(x0, (2,), True)
    step(jd)
    step(r2_rest)
    act(1)
    back(1)
    r2.push(1)
    step(jd)
    act(3)
    back(3)
    r2.push(3)
    act(0)
    step(r2_rest, 2)
    back(0)
    r2.push(0)
    step(jd)
    net.finish(gu_sent)
    for x0 in range(4):
        grad_a(x0)
    step(ja)
    step(r2_rest, 2)
    net.finish(r2_sent)

    def third(i, _):
        at = pl.ds(pl.multiple_of(i * 16, 16), 16)
        v = resid[at]
        inv = lax.rsqrt(jnp.mean(v * v, axis=1, keepdims=True) + epsilon)
        x = v * inv
        w = g_ffn * GR[at]
        g = GO[p.z, p.c, at].astype(F32) + inv * (w - x * jnp.mean(w * x, axis=1, keepdims=True))
        GR[at] = g
        T[p.z, p.c, at] = g.astype(BF)

    lax.fori_loop(0, ROWS // 16, third, None, unroll=4)
    g3 = gather_ring(net, T.at[p.z, p.c], T, g3_sent)
    step(g3)
    reloaded = net.copy(spill, PA)
    step(ja)
    step(jd)
    for x0 in range(4):
        grad_b(x0)
    step(jb)
    KP[...] = jnp.zeros(KP.shape, F32)
    GM[...] = jnp.zeros(GM.shape, F32)

    def unmix(j):
        zj = block(j)
        o = whole(WC, slice(128, 384))
        gm = dot(T[zj].reshape(256, D), o, NN)
        gm = jnp.concatenate([gm[:, :128], jnp.where(lanes, gm[:, 128:], 0.0)], axis=1).reshape(2, 128, 256)
        for cc in range(2):
            gc = gm[cc] * conv(zj, cc)
            at = slice(128 * cc, 128 * cc + 128)
            GGU[zj, at, 0:128] = gc[:, :128].astype(BF)
            GGU[zj, at, 128:256] = jnp.zeros((128, 128), BF)
            GGU[zj, at, 256:384] = pltpu.roll(gc[:, 128:], 64, 1).astype(BF)
            gv = gm[cc] * C[zj, cc].astype(F32)
            GC[zj + 1, cc, 0:128] = gv
            for i in range(3):
                KP[i : i + 1] = KP[i : i + 1] + jnp.sum(gv * BX[zj, cc, 8 - i : 136 - i], axis=0, keepdims=True)
        net.send(GC.at[zj + 1, :, 0:8], GC.at[zj + p.yl, :, 128:136], halo_back + j, p.at(y=p.y + 1 - 2 * p.yl))

    step(g3)
    unmix(0)
    net.finish(g2_sent)
    step(jb)
    down(0)
    step(g3)
    step(ja)
    down(1)
    down(2)
    down(3)
    step(g3)
    step(jd)
    step(g3)
    unmix(1)
    unmix(3)
    step(jb)
    step(g3, 2)
    unmix(2)
    r4 = ReduceRing(net, N, MR, *ring_a)
    r4_sent, r4_rest = r4.mine, r4.rest()
    for j in (2, 1, 3, 0):
        r4.push(j)
    reloaded()
    net.finish(w_sent)
    DE = WD.at[:, :, :, :, 0:384]
    for x0 in range(4):
        at = slice(384 * x0, 384 * x0 + 384)
        w = dot(PA[:, :, :, at].reshape(1024, 384), GGU[:, :, 0:384].reshape(1024, 384), TN)
        m = dot(T[:, :, :, at].reshape(1024, 384), MX[...].reshape(1024, 256), TN)
        w = jnp.concatenate([w[:, :128], m[:, :128], w[:, 256:] + m[:, 128:]], axis=1)
        DE[x0] = w.astype(BF).reshape(2, 2, 96, 384)
        if x0 == 1:
            step(r4_rest)
    je = reduce_direct(net, DE, SC.at[:, 0:384], *se)
    step(je)
    step(r4_rest)
    step(ja)
    for j in range(4):
        net.got(GC.at[block(j) + 1 - p.yl, :, 128:136], halo_back + j)
    r3 = ReduceRing(net, GO, R1, *ring_b)
    r3_sent, r3_rest = r3.mine, r3.rest()

    def unproject(j):
        zj = block(j)
        for cc in range(2):
            at = slice(128 * cc, 128 * cc + 128)
            gb = taps[0] * GC[zj + 1, cc, 0:128] + taps[1] * GC[zj + 1, cc, 1:129] + taps[2] * GC[zj + 1, cc, 2:130]
            bb, vv = gb * V[zj, cc].astype(F32), gb * B[zj, cc].astype(F32)
            GGU[zj, at, 384:512] = bb[:, :128].astype(BF)
            GGU[zj, at, 512:640] = vv[:, :128].astype(BF)
            GGU[zj, at, 640:768] = (bb[:, 128:] + pltpu.roll(vv[:, 128:], 64, 1)).astype(BF)
        r = dot(GGU[zj, :, 0:768], whole(WC), NT)
        GO[zj] = r.astype(BF).reshape(2, 128, D)
        GM[...] += jnp.sum((r * PA[zj].reshape(256, D).astype(F32)).reshape(32, 8, D), axis=0)
        r3.push(j)

    unproject(2)
    step(jd)
    for who in partners:
        pl.semaphore_signal(free, inc=1, device_id=who, device_id_type=MESH)
    unproject(1)
    unproject(3)
    step(r3_rest)
    unproject(0)
    step(r4_rest)
    step(r3_rest)
    step(jb)
    jk = reduce_direct(net, KG, SK, *sk)

    mix_row = jnp.sum(GM[...], axis=0, keepdims=True)
    mix_row = jnp.concatenate([mix_row / g_mix, jnp.zeros((1, 128), F32)], axis=1)
    low = lax.broadcasted_iota(jnp.int32, (1, 256), 1) < 96
    for s in range(16):
        at = (96 * s) // 128 * 128
        row = mix_row[:, at : at + 256]
        row = row if 96 * s == at else pltpu.roll(row, 256 - (96 * s - at), 1)
        tile = jnp.concatenate([KP[...], jnp.where(low, row, 0.0), jnp.zeros((23, 256), F32)], axis=0)
        KG[s // 4, (s // 2) % 2, s % 2] = tile.astype(BF)
    step(jk)
    DC = DD.at[:, :, :, :, 0:384]
    for x0 in range(4):
        at = slice(384 * x0, 384 * x0 + 384)
        w = dot(PA[:, :, :, at].reshape(1024, 384), GGU[:, :, 384:768].reshape(1024, 384), TN)
        DC[x0] = w.astype(BF).reshape(2, 2, 96, 384)
        if x0 == 1:
            step(ja)
            step(je)
    pl.semaphore_wait(free, len(partners))
    low_half, high_half = slice(0, 384), slice(384, 768)
    RB, F, RY, H = sd[1], sd[3], sd[5], sd[7]
    views = [
        [RB.at[0, :, :, :, low_half], RB.at[0, :, :, :, high_half], RB.at[1, :, :, :, low_half]],
        [RY.at[0, :, :, :, low_half], RY.at[0, :, :, :, high_half], RY.at[1, :, :, :, low_half]],
        [F.at[i, :, at] for i in range(2) for at in (low_half, high_half)],
        [H.at[i, :, at] for i in range(2) for at in (low_half, high_half)],
    ]
    jc = reduce_direct(net, DC, SC.at[:, 384:768], *views)
    step(jc)
    step(jk)
    step(r3_rest)
    step(jb)
    step(r4_rest)
    step(ja)
    step(jc)
    step(jb)
    ffn_share = jnp.sum(SA[...] * gu_s[:, 0:GA_N].astype(F32), axis=1, keepdims=True)
    ffn_share += jnp.sum(SB_[...] * gu_s[:, GA_N:].astype(F32), axis=1, keepdims=True)
    both = jnp.concatenate([jnp.broadcast_to(ffn_share, (96, 128)), jnp.zeros((32, 128), F32)], axis=0).T
    step(jk)
    X[0:16] = SK[0:16]
    X[9:10, 0:96] = both[0:1, 0:96] / gf_w[...].astype(F32)
    me = lax.axis_index("tensor")
    done = net.copy(X, XR.at[me])
    base = net.sem(8)
    for i in range(1, 8):
        net.send(X, XR.at[me], base + i, (lax.axis_index("dp"), (me + i) % 8))
    step(r3_rest)
    step(r4_rest)
    step(je)
    step(r3_rest)

    def last(i, _):
        at = pl.ds(pl.multiple_of(i * 16, 16), 16)
        lv = live_rows(lens, i * 16, 16)
        layer_out[at] = (lv * (resid[at] + MR[at])).astype(BF)
        v = tok[at].astype(F32)
        inv = lax.rsqrt(jnp.mean(v * v, axis=1, keepdims=True) + epsilon)
        x = v * inv
        w = g_mix * R1[at]
        g = GR[at] + inv * (w - x * jnp.mean(w * x, axis=1, keepdims=True))
        tokens_grad[at] = g.astype(BF)

    lax.fori_loop(0, ROWS // 16, last, None, unroll=4)
    step(jc)
    for i in range(1, 8):
        net.got(XR.at[(me + 8 - i) % 8], base + i)
    done()
    for job in (gt, go, g2, g3, am, ac, ae, ad, au, av, r1_rest, r2_rest, r3_rest, r4_rest, ja, jb, jd, jc, je, jk):
        assert next(job, "end") == "end"
    assert max(net.ns, net.nr) <= SEMS and net.nl <= 24
    net.finish(r3_sent + r4_sent + g3_sent + w_sent)
    net.finish()


GA_N = 1024
SEMS = 480


def train_call(*args):
    any_, vm = pl.BlockSpec(memory_space=pl.ANY), pl.BlockSpec(memory_space=pltpu.VMEM)
    ring, wide = (4, 2, ROWS, D), (4, 2, ROWS, 256)
    outs = [shape((ROWS, D)), shape((ROWS, D))]
    outs += [shape((96, n), F32) for n in (GA_N, 1792 - GA_N, FP, 768)] + [shape((8, 16, 256), F32), shape(ring)]
    v = lambda s, t=BF: pltpu.VMEM(s, t)
    scratch = [v((ROWS, D), F32), v((32, D), F32)] + [v((ROWS, D), F32)] * 3
    scratch += [v((96, 768)), v((96, 1792)), v((96, FP)), v((32, 256)), v((256, 128), F32)]
    scratch += [v(ring)] * 3 + [v((4, 2, 2, 96, n)) for n in (768, 1792, FP)] + [v((4, 2, 2, 32, 256))]
    scratch += [v(wide)] * 3 + [v((5, 2, 136, 256), F32), v(wide), v((5, 2, 136, 256), F32)]
    scratch += [v((4, 256, FP)), v((4, 256, 1792)), v(ring), v((4, 2, 2, 96, FP)), v((8, 256), F32), v((8, D), F32)]
    scratch += plane_scratch(GA_N) + plane_scratch(1792 - GA_N) + plane_scratch(FP) + direct_scratch(256, 16) + direct_scratch(384)
    scratch += ring_scratch(D) * 2 + [v((4, 2, 2, 32, 256)), v((16, 256), F32), v((32, 256), F32)]
    scratch += [pltpu.SemaphoreType.REGULAR]
    scratch += [pltpu.SemaphoreType.DMA((SEMS,)), pltpu.SemaphoreType.DMA((SEMS,)), pltpu.SemaphoreType.DMA((24,))]
    *sums, _ = pl.pallas_call(
        train_kernel,
        out_shape=tuple(outs),
        in_specs=[vm] * 11,
        out_specs=tuple([vm] * 7 + [any_]),
        scratch_shapes=scratch,
        compiler_params=pltpu.CompilerParams(
            collective_id=0, has_side_effects=True, vmem_limit_bytes=64 << 20),
        name="train",
    )(*args)
    return sums


def finish_kernel(lo, tg, SA, SB, SD, SC, XR,
                  layer_out, tokens_grad, mix, in_grad, taps, out_grad, ffn, gate, up, down, flip):
    layer_out[...] = lo[...]
    tokens_grad[...] = tg[...]
    for t in range(7):
        n = 96 if t == 6 else 128
        src, at = (SA, 256 * t) if t < 4 else (SB, 256 * t - 1024)
        gate[:, 128 * t : 128 * t + n] = src[:, at : at + n]
        up[:, 128 * t : 128 * t + n] = src[:, at + 128 : at + 128 + n]
    down[...] = SD[:, 0:FB]
    flip[96:128] = jnp.zeros((32, 256), F32)
    flip[0:96] = SC[:, 128:384]
    out_grad[...] = flip[...].T[0:CH, 0:96]
    for i in range(3):
        at = (384, 0, 512)[i]
        in_grad[i, :, 0:128] = SC[:, at : at + 128]
    in_grad[0, :, 128:192] = SC[:, 640:704]
    in_grad[1, :, 128:192] = pltpu.roll(SC[:, 256:384], 64, 1)[:, :64]
    in_grad[2, :, 128:192] = pltpu.roll(SC[:, 640:768], 64, 1)[:, :64]
    dp, t = lax.axis_index("dp"), lax.axis_index("tensor")
    shares = XR[0, 8:16]
    for i in range(1, 8):
        shares = shares + XR[i, 8:16]
    shares = pltpu.roll(shares, 256 - 12 * t, 1)
    mix[...] = shares[0:1, 0:12]
    ffn[...] = shares[1:2, 0:12]
    k = pltpu.roll(XR[dp // 2, 0:8], lax.rem(256 - 12 * ((dp * 8 + t) % 16), 256), 1)
    taps[...] = k[0:3, 0:12]


def finish_call(*args):
    vm = pl.BlockSpec(memory_space=pltpu.VMEM)
    outs = [shape((ROWS, D)), shape((ROWS, D)), shape((1, 12), F32), shape((3, 96, CH), F32), shape((3, 12), F32)]
    outs += [shape((CH, 96), F32), shape((1, 12), F32), shape((96, FB), F32), shape((96, FB), F32), shape((96, FB), F32)]
    return pl.pallas_call(
        finish_kernel,
        out_shape=tuple(outs),
        in_specs=[vm] * 7,
        out_specs=tuple([vm] * 10),
        scratch_shapes=[pltpu.VMEM((128, 256), F32)],
        compiler_params=pltpu.CompilerParams(vmem_limit_bytes=VMEM_LIMIT),
        name="finish",
    )(*args)


def per_device(tokens, gain_mix, in_weight, conv_kernel, out_weight, gain_ffn, gate_weight, up_weight, down_weight, lengths, cotangent):
    gm, gf, lens = gain_mix.reshape(1, 96), gain_ffn.reshape(1, 96), lengths.reshape(1, 1)
    sums = train_call(
        tokens, cotangent, lens, in_weight.transpose(1, 0, 2), out_weight, gate_weight, up_weight,
        down_weight.T, gm, gf, conv_kernel)
    layer_out, tokens_grad, mix, in_grad, taps_grad, out_grad, ffn, gate, up, down = finish_call(*sums)
    return layer_out, tokens_grad, mix[0], in_grad.transpose(1, 0, 2), taps_grad, out_grad, ffn[0], gate, up, down.T


def solution(mesh):
    placed = (
        P(("dp", "tensor"), None),
        P("dp"),
        P("dp", None, "tensor"),
        P(None, "tensor"),
        P("tensor", "dp"),
        P("dp"),
        P("dp", "tensor"),
        P("dp", "tensor"),
        P("tensor", "dp"),
        P("dp"),
        P(("dp", "tensor"), None),
    )
    return jax.shard_map(
        per_device,
        mesh=mesh,
        in_specs=placed,
        out_specs=(
            P(("dp", "tensor"), None),
            P(("dp", "tensor"), None),
            P(("dp", "tensor")),
            P("dp", None, "tensor"),
            P(None, ("dp", "tensor")),
            P("tensor", "dp"),
            P(("dp", "tensor")),
            P("dp", "tensor"),
            P("dp", "tensor"),
            P("tensor", "dp"),
        ),
        check_vma=False,
    )
```

```python
import functools

import jax
import jax.numpy as jnp
from jax import lax
from jax.experimental import pallas as pl
from jax.experimental.pallas import tpu as pltpu
from jax.sharding import PartitionSpec as P

epsilon = 1e-05
MESH = pl.DeviceIdType.MESH
BF = jnp.bfloat16
F32 = jnp.float32
D = 1536
ROWS = 128
CH = 192
FB = 864
FP = 896
HALF = 48
VMEM_LIMIT = 60 << 20


class Place:
    def __init__(self):
        dp = lax.axis_index("dp")
        t = lax.axis_index("tensor")
        self.x, self.yh, self.c = dp // 4, (dp // 2) % 2, dp % 2
        self.z, self.yl = t // 2, t % 2
        self.y = self.yh * 2 + self.yl
        self.o = 1 - self.c
        self.xp, self.xm, self.x2 = (self.x + 1) % 4, (self.x + 3) % 4, (self.x + 2) % 4
        self.yp, self.ym = (self.y + 1) % 4, (self.y + 3) % 4
        self.y2 = (self.y + 2) % 4
        self.yhp, self.yhm = self.yp // 2, self.ym // 2
        self.way = 1 - 2 * self.c
        self.zf = (self.z + self.way + 4) % 4
        self.zb = (self.z - self.way + 4) % 4
        self.zp, self.zm, self.z2 = (self.z + 1) % 4, (self.z + 3) % 4, (self.z + 2) % 4
        self.own = self.c == self.yl
        self.opp = self.c != self.yl

    def at(self, x=None, y=None, z=None, c=None):
        x = self.x if x is None else x
        y = self.y if y is None else y
        z = self.z if z is None else z
        c = self.c if c is None else c
        return (x * 4 + (y // 2) * 2 + c, z * 2 + y % 2)


class Net:
    def __init__(self, place, send, recv, local=None):
        self.p, self.ss, self.rs, self.ls = place, send, recv, local
        self.ns = self.nr = self.nl = 0
        self.pending = []

    def sem(self, n=1):
        k = self.nr
        self.nr += n
        return k

    def send(self, src, dst, recv_index, target, cond=None, pending=None):
        k = self.ns
        self.ns += 1
        d = pltpu.make_async_remote_copy(
            src_ref=src, dst_ref=dst, send_sem=self.ss.at[k], recv_sem=self.rs.at[recv_index],
            device_id=target, device_id_type=MESH)
        run(cond, d.start)
        (self.pending if pending is None else pending).append((cond, d))

    def copy(self, src, dst, cond=None):
        k = self.nl
        self.nl += 1
        d = pltpu.make_async_copy(src, dst, self.ls.at[k])
        run(cond, d.start)
        return lambda: run(cond, d.wait)

    def got(self, dst, recv_index, cond=None):
        d = pltpu.make_async_remote_copy(
            src_ref=dst, dst_ref=dst, send_sem=self.ss.at[0], recv_sem=self.rs.at[recv_index],
            device_id=self.p.at(c=self.p.o), device_id_type=MESH)
        run(cond, d.wait_recv)

    def finish(self, pending=None):
        pending = self.pending if pending is None else pending
        for cond, d in pending:
            run(cond, d.wait_send)
        pending.clear()


def run(cond, f):
    if cond is None:
        f()
    else:
        pl.when(cond)(f)


def greet(p, plane, ring, group=False):
    bar = pltpu.get_barrier_semaphore()
    who = [p.at(c=p.o)]
    if plane:
        for c in (0, 1):
            who += [p.at(x=p.xp, c=c), p.at(x=p.xm, c=c), p.at(y=p.yp, c=c), p.at(y=p.ym, c=c)]
            who += [p.at(x=p.x2, c=c), p.at(y=p.y2, c=c)]
    if group:
        me = lax.axis_index("tensor")
        who += [(lax.axis_index("dp"), (me + i) % 8) for i in range(1, 8)]
    elif ring:
        who += [p.at(z=p.zp), p.at(z=p.zm)]
    for w in who:
        pl.semaphore_signal(bar, inc=1, device_id=w, device_id_type=MESH)
    return lambda: pl.semaphore_wait(bar, len(who))


def add(out, *terms):
    lead = out.shape[:-2]
    count = 1
    for s in lead:
        count *= s

    def one(i):
        at = []
        for s in reversed(lead):
            at.append(i % s)
            i = i // s
        at = tuple(reversed(at))
        v = terms[0][at].astype(F32) if at else terms[0][...].astype(F32)
        for t in terms[1:]:
            v = v + (t[at] if at else t[...]).astype(F32)
        if at:
            out[at] = v.astype(out.dtype)
        else:
            out[...] = v.astype(out.dtype)

    if not lead:

        def rows(i, _):
            at = pl.ds(pl.multiple_of(i * 16, 16), 16)
            v = terms[0][at].astype(F32)
            for t in terms[1:]:
                v = v + t[at].astype(F32)
            out[at] = v.astype(out.dtype)

        lax.fori_loop(0, out.shape[0] // 16, rows, None)
    else:
        lax.fori_loop(0, count, lambda i, _: one(i), None)


def ring_scratch(n):
    return [pltpu.VMEM((4, ROWS, n), BF), pltpu.VMEM((3, ROWS, n), BF)]


def shape(s, t=BF):
    return jax.ShapeDtypeStruct(s, t)


def slots(n):
    return shape((4, 2, 2, 96, n))


def gather_plane(net, sh, W, mine, far=False):
    p = net.p
    send = functools.partial(net.send, pending=mine)
    h = sh.shape[0] // 2
    HA, HB = pl.ds(0, h), pl.ds(h, h)
    i_own, f1, f2, f3, f4 = net.sem(), net.sem(2), net.sem(2), net.sem(2), net.sem(2)
    r1, r2, r3, r4, y1, y2, y3, y4, x1, x2, x3, x4 = (net.sem() for _ in range(12))
    f5, f6 = net.sem(2), net.sem(2)
    q = p.yl

    def pass_near():
        net.got(W.at[p.xm, p.yh, 0, HA], f1 + 0, p.own)
        net.got(W.at[p.x, p.yhm, 0, HB], f3 + 0, p.opp)
        send(W.at[p.xm, p.yh, 0, HA], W.at[p.xm, p.yh, 0, HA], r1, p.at(x=p.xp), p.own)
        send(W.at[p.x, p.yhm, 0, HB], W.at[p.x, p.yhm, 0, HB], r3, p.at(y=p.yp), p.opp)
        net.got(W.at[p.xp, p.yh, 1, HA], f2 + 1, p.own)
        net.got(W.at[p.x, p.yhp, 1, HB], f4 + 1, p.opp)
        send(W.at[p.xp, p.yh, 1, HA], W.at[p.xp, p.yh, 1, HA], r2, p.at(x=p.xm), p.own)
        send(W.at[p.x, p.yhp, 1, HB], W.at[p.x, p.yhp, 1, HB], r4, p.at(y=p.ym), p.opp)
        yield

    done = net.copy(sh, W.at[p.x, p.yh, p.c], p.own)
    send(sh.at[HA], W.at[p.x, p.yh, p.c, HA], f1 + p.c, p.at(x=p.xp, c=q))
    send(sh.at[HA], W.at[p.x, p.yh, p.c, HA], f2 + p.c, p.at(x=p.xm, c=q))
    send(sh.at[HB], W.at[p.x, p.yh, p.c, HB], f3 + p.c, p.at(y=p.yp, c=q))
    send(sh.at[HB], W.at[p.x, p.yh, p.c, HB], f4 + p.c, p.at(y=p.ym, c=q))
    send(sh, W.at[p.x, p.yh, p.c], i_own, p.at(c=p.o), p.opp)
    if far:
        send(sh.at[HA], W.at[p.x, p.yh, p.c, HA], f5 + p.c, p.at(x=p.x2, c=q))
        send(sh.at[HB], W.at[p.x, p.yh, p.c, HB], f6 + p.c, p.at(y=p.y2, c=q))
    yield
    if not far:
        yield from pass_near()
    done()
    net.got(W.at[p.x, p.yh, p.o], i_own, p.own)
    net.got(W.at[p.xm, p.yh, 1, HA], f1 + 1, p.own)
    net.got(W.at[p.xp, p.yh, 0, HA], f2 + 0, p.own)
    net.got(W.at[p.x, p.yhm, 1, HB], f3 + 1, p.opp)
    net.got(W.at[p.x, p.yhp, 0, HB], f4 + 0, p.opp)
    if far:
        net.got(W.at[p.xm, p.yh, 0, HA], f1 + 0, p.own)
        net.got(W.at[p.xp, p.yh, 1, HA], f2 + 1, p.own)
        net.got(W.at[p.x, p.yhm, 0, HB], f3 + 0, p.opp)
        net.got(W.at[p.x, p.yhp, 1, HB], f4 + 1, p.opp)
    for cc in range(2):
        net.got(W.at[p.x2, p.yh, cc, HA], f5 + cc if far else (r1, r2)[cc], p.own)
    send(W.at[:, p.yh, :, HA], W.at[:, p.yh, :, HA], y1, p.at(y=p.yp), p.own)
    send(W.at[:, p.yh, :, HA], W.at[:, p.yh, :, HA], y2, p.at(y=p.ym), p.own)
    for cc in range(2):
        net.got(W.at[p.x, 1 - p.yh, cc, HB], f6 + cc if far else (r3, r4)[cc], p.own)
    send(W.at[p.x, :, :, HB], W.at[p.x, :, :, HB], x1, p.at(x=p.xp))
    send(W.at[p.x, :, :, HB], W.at[p.x, :, :, HB], x2, p.at(x=p.xm))
    yield
    net.got(W.at[p.xm, :, :, HB], x1)
    send(W.at[p.xm, :, 0, HB], W.at[p.xm, :, 0, HB], x3, p.at(x=p.xp))
    net.got(W.at[p.xp, :, :, HB], x2)
    send(W.at[p.xp, :, 1, HB], W.at[p.xp, :, 1, HB], x4, p.at(x=p.xm))
    net.got(W.at[:, p.yhm, :, HA], y1, p.opp)
    send(W.at[:, p.yhm, 0, HA], W.at[:, p.yhm, 0, HA], y3, p.at(y=p.yp), p.opp)
    net.got(W.at[:, p.yhp, :, HA], y2, p.opp)
    send(W.at[:, p.yhp, 1, HA], W.at[:, p.yhp, 1, HA], y4, p.at(y=p.ym), p.opp)
    yield
    net.got(W.at[:, 1 - p.yh, 0, HA], y3, p.own)
    net.got(W.at[:, 1 - p.yh, 1, HA], y4, p.own)
    net.got(W.at[p.x2, :, 0, HB], x3)
    net.got(W.at[p.x2, :, 1, HB], x4)


PARTS = [pl.ds(0, 64), pl.ds(64, 64)]


def gather_ring(net, a, out, mine, late=False):
    p = net.p
    send = functools.partial(net.send, pending=mine)
    s1, s3, s2 = net.sem(2), net.sem(2), net.sem(2)
    k = net.sem(8)
    jf, jb = (p.zf - p.z + 4) % 4, (p.zb - p.z + 4) % 4
    for i, r in enumerate(PARTS):
        send(a.at[r], out.at[p.z, p.c, r], s1 + i, p.at(z=p.zf))
        send(a.at[r], out.at[p.z, p.c, r], s3 + i, p.at(z=p.zb))
    for i, r in enumerate(PARTS):
        send(a.at[r], out.at[p.z, p.c, r], k + 4 * i, p.at(c=p.o))
    yield
    for i, r in enumerate(PARTS):
        net.got(out.at[p.z, p.o, r], k + 4 * i)
    yield
    for i, r in enumerate(PARTS):
        net.got(out.at[p.zb, p.c, r], s1 + i)
        if not late:
            send(out.at[p.zb, p.c, r], out.at[p.zb, p.c, r], s2 + i, p.at(z=p.zf))
        send(out.at[p.zb, p.c, r], out.at[p.zb, p.c, r], k + 4 * i + jb, p.at(c=p.o))
        net.got(out.at[p.zf, p.c, r], s3 + i)
        send(out.at[p.zf, p.c, r], out.at[p.zf, p.c, r], k + 4 * i + jf, p.at(c=p.o))
        yield
    for i, r in enumerate(PARTS):
        net.got(out.at[p.zp, p.o, r], k + 4 * i + 1)
        net.got(out.at[p.zm, p.o, r], k + 4 * i + 3)
    yield
    if late:
        for i, r in enumerate(PARTS):
            send(out.at[p.zb, p.c, r], out.at[p.zb, p.c, r], s2 + i, p.at(z=p.zf))
        yield
    for i, r in enumerate(PARTS):
        net.got(out.at[p.z2, p.c, r], s2 + i)
        send(out.at[p.z2, p.c, r], out.at[p.z2, p.c, r], k + 4 * i + 2, p.at(c=p.o))
    yield
    for i, r in enumerate(PARTS):
        net.got(out.at[p.z2, p.o, r], k + 4 * i + 2)


class ReduceRing:
    def __init__(self, net, V, out, RC, RZ):
        self.net, self.V, self.out, self.RC, self.RZ = net, V, out, RC, RZ
        self.s2, self.sd, self.sr, self.k = net.sem(2), net.sem(2), net.sem(2), net.sem(8)
        self.mine = []
        self.send = functools.partial(net.send, pending=self.mine)

    def push(self, j):
        p = self.net.p
        for i, r in enumerate(PARTS):
            self.send(self.V.at[(p.z + j) % 4, p.o, r], self.RC.at[j, r], self.k + 4 * i + j, p.at(c=p.o))

    def rest(self):
        net, p, V, RC, RZ, k = self.net, self.net.p, self.V, self.RC, self.RZ, self.k
        jf, jb = (p.zf - p.z + 4) % 4, (p.zb - p.z + 4) % 4
        for i, r in enumerate(PARTS):
            net.got(RC.at[2, r], k + 4 * i + 2)
            add(RC.at[2, r], V.at[p.z2, p.c, r], RC.at[2, r])
            self.send(RC.at[2, r], RZ.at[0, r], self.s2 + i, p.at(z=p.zf))
        yield
        for i, r in enumerate(PARTS):
            net.got(RC.at[jb, r], k + 4 * i + jb)
            add(RC.at[jb, r], V.at[p.zb, p.c, r], RC.at[jb, r])
            self.send(RC.at[jb, r], RZ.at[1, r], self.sd + i, p.at(z=p.zb))
        for i, r in enumerate(PARTS):
            net.got(RC.at[jf, r], k + 4 * i + jf)
            add(RC.at[jf, r], V.at[p.zf, p.c, r], RC.at[jf, r])
        yield
        for i, r in enumerate(PARTS):
            net.got(RZ.at[0, r], self.s2 + i)
            add(RC.at[jf, r], RC.at[jf, r], RZ.at[0, r])
            self.send(RC.at[jf, r], RZ.at[2, r], self.sr + i, p.at(z=p.zf))
        yield
        for i, r in enumerate(PARTS):
            net.got(RC.at[0, r], k + 4 * i)
            add(RC.at[0, r], V.at[p.z, p.c, r], RC.at[0, r])
        yield
        for i, r in enumerate(PARTS):
            net.got(RZ.at[1, r], self.sd + i)
            net.got(RZ.at[2, r], self.sr + i)
            add(self.out.at[r], RC.at[0, r], RZ.at[1, r], RZ.at[2, r])


def step(job, times=1):
    for _ in range(times):
        next(job, None)


def dot(a, b, dims):
    return lax.dot_general(a, b, (dims, ((), ())), preferred_element_type=F32)


NN, NT, TN = ((1,), (0,)), ((1,), (1,)), ((0,), (0,))


def whole(ref, columns=slice(None)):
    v = ref[:, :, :, :, columns]
    return v.reshape(D, v.shape[-1])


def row_norm(src, dst, gain, rows=32):
    def one(i, _):
        at = pl.ds(pl.multiple_of(i * rows, rows), rows)
        v = src[at].astype(F32)
        inv = lax.rsqrt(jnp.mean(v * v, axis=1, keepdims=True) + epsilon)
        dst[at] = (v * inv * gain).astype(dst.dtype)

    lax.fori_loop(0, ROWS // rows, one, None, unroll=2)


def live_rows(lens, first=0, rows=ROWS):
    at = lax.axis_index("tensor") * ROWS + first + lax.broadcasted_iota(jnp.int32, (rows, 1), 0)
    return jnp.where(at < lens[...], 1.0, 0.0).astype(F32)


def plane_scratch(n, h=HALF):
    return [
        pltpu.VMEM((2, 4, h, n), BF),
        pltpu.VMEM((2, 4, 2, h, n), BF),
        pltpu.VMEM((2, h, n), BF),
        pltpu.VMEM((3, h, n), BF),
        pltpu.VMEM((2, 2, h, n), BF),
        pltpu.VMEM((2, 2, 2, h, n), BF),
        pltpu.VMEM((2, h, n), BF),
        pltpu.VMEM((3, h, n), BF),
    ]


def reduce_plane(net, G, out, RA, RB, RC, F, RX, RY, RZ, H):
    p = net.p
    h = out.shape[0] // 2
    HA, HB = pl.ds(0, h), pl.ds(h, h)
    mine = []
    send = functools.partial(net.send, pending=mine)
    a0, a1, bp0, bp1, bm0, bm1, c0, c1, g0, g1, g2 = (net.sem() for _ in range(11))
    u0, u1, vp0, vp1, vm0, vm1, w0, w1, h0, h1, h2 = (net.sem() for _ in range(11))
    send(G.at[:, 1 - p.yh, 0, HA], RA.at[0], a0, p.at(y=p.ym), p.own)
    send(G.at[:, 1 - p.yh, 1, HA], RA.at[1], a1, p.at(y=p.yp), p.own)
    send(G.at[p.x2, :, 0, HB], RX.at[0], u0, p.at(x=p.xm))
    send(G.at[p.x2, :, 1, HB], RX.at[1], u1, p.at(x=p.xp))
    yield
    send(G.at[:, p.yhm, 1, HA], RB.at[0, :, 1], bp1, p.at(y=p.ym), p.opp)
    send(G.at[:, p.yhp, 0, HA], RB.at[1, :, 0], bm0, p.at(y=p.yp), p.opp)
    send(G.at[p.xm, :, 1, HB], RY.at[0, :, 1], vp1, p.at(x=p.xm))
    send(G.at[p.xp, :, 0, HB], RY.at[1, :, 0], vm0, p.at(x=p.xp))
    yield

    net.got(RX.at[0], u0)
    add(RX.at[0], RX.at[0], G.at[p.xm, :, 0, HB])
    send(RX.at[0], RY.at[0, :, 0], vp0, p.at(x=p.xm))
    net.got(RX.at[1], u1)
    add(RX.at[1], RX.at[1], G.at[p.xp, :, 1, HB])
    send(RX.at[1], RY.at[1, :, 1], vm1, p.at(x=p.xp))
    net.got(RA.at[0], a0, p.opp)
    net.got(RA.at[1], a1, p.opp)

    @pl.when(p.opp)
    def _():
        add(RA.at[0], RA.at[0], G.at[:, p.yhm, 0, HA])
        add(RA.at[1], RA.at[1], G.at[:, p.yhp, 1, HA])

    send(RA.at[0], RB.at[0, :, 0], bp0, p.at(y=p.ym), p.opp)
    send(RA.at[1], RB.at[1, :, 1], bm1, p.at(y=p.yp), p.opp)
    yield

    net.got(RY.at[0, :, 1], vp1)
    net.got(RY.at[1, :, 0], vm0)
    net.got(RY.at[0, :, 0], vp0)
    net.got(RY.at[1, :, 1], vm1)
    add(RY.at[0], RY.at[0], RY.at[1], G.at[p.x, :, :, HB])
    T = RY.at[0]
    send(T.at[1 - p.yh, 0], RZ.at[0], w0, p.at(y=p.ym), p.own)
    send(T.at[1 - p.yh, 1], RZ.at[1], w1, p.at(y=p.yp), p.own)
    send(T.at[p.yhm, 1], H.at[1], h1, p.at(y=p.ym, c=1), p.opp)
    send(T.at[p.yhp, 0], H.at[2], h2, p.at(y=p.yp, c=0), p.opp)
    send(T.at[p.yh, p.o], H.at[0], h0, p.at(c=p.o), p.own)

    net.got(RB.at[0, :, 1], bp1, p.own)
    net.got(RB.at[1, :, 0], bm0, p.own)
    net.got(RB.at[0, :, 0], bp0, p.own)
    net.got(RB.at[1, :, 1], bm1, p.own)

    @pl.when(p.own)
    def _():
        add(RB.at[0], RB.at[0], RB.at[1], G.at[:, p.yh, :, HA])

    S = RB.at[0]
    send(S.at[p.x2, 0], RC.at[0], c0, p.at(x=p.xm), p.own)
    send(S.at[p.x2, 1], RC.at[1], c1, p.at(x=p.xp), p.own)
    send(S.at[p.xm, 1], F.at[1], g1, p.at(x=p.xm, c=1), p.own)
    send(S.at[p.xp, 0], F.at[2], g2, p.at(x=p.xp, c=0), p.own)
    send(S.at[p.x, p.o], F.at[0], g0, p.at(c=p.o), p.own)
    yield

    net.got(RC.at[0], c0, p.own)
    net.got(RC.at[1], c1, p.own)
    net.got(RZ.at[0], w0, p.opp)
    net.got(RZ.at[1], w1, p.opp)

    @pl.when(p.own)
    def _():
        add(RC.at[0], RC.at[0], S.at[p.xm, 0])
        add(RC.at[1], RC.at[1], S.at[p.xp, 1])

    @pl.when(p.opp)
    def _():
        add(RZ.at[0], RZ.at[0], T.at[p.yhm, 0])
        add(RZ.at[1], RZ.at[1], T.at[p.yhp, 1])

    send(RC.at[0], F.at[1], g1, p.at(x=p.xm, c=0), p.own)
    send(RC.at[1], F.at[2], g2, p.at(x=p.xp, c=1), p.own)
    send(RZ.at[0], H.at[1], h1, p.at(y=p.ym, c=0), p.opp)
    send(RZ.at[1], H.at[2], h2, p.at(y=p.yp, c=1), p.opp)
    yield

    net.got(F.at[0], g0, p.opp)
    net.got(F.at[1], g1)
    net.got(F.at[2], g2)
    net.got(H.at[0], h0, p.opp)
    net.got(H.at[1], h1)
    net.got(H.at[2], h2)
    net.finish(mine)

    @pl.when(p.own)
    def _():
        F[0] = S[p.x, p.c]
        H[0] = T[p.yh, p.c]

    add(out.at[HA], F.at[0], F.at[1], F.at[2])
    add(out.at[HB], H.at[0], H.at[1], H.at[2])


def direct_scratch(n, h=HALF):
    return [
        pltpu.VMEM((3, 4, 2, h, n), BF),
        pltpu.VMEM((3, 2, 2, h, n), BF),
        pltpu.VMEM((4, h, n), BF),
        pltpu.VMEM((4, h, n), BF),
    ]


def reduce_direct(net, G, out, YA, XB, F, H):
    p = net.p
    h = out.shape[0] // 2
    HA, HB = pl.ds(0, h), pl.ds(h, h)
    mine = []
    send = functools.partial(net.send, pending=mine)
    ya, xb, f, g = net.sem(3), net.sem(3), net.sem(4), net.sem(4)
    send(G.at[:, 1 - p.yh, :, HA], YA[2], ya + 2, p.at(y=p.y2), p.own)
    send(G.at[:, p.yhm, :, HA], YA[0], ya + 0, p.at(y=p.ym), p.opp)
    send(G.at[:, p.yhp, :, HA], YA[1], ya + 1, p.at(y=p.yp), p.opp)
    send(G.at[p.x2, :, :, HB], XB[2], xb + 2, p.at(x=p.x2))
    send(G.at[p.xm, :, :, HB], XB[0], xb + 0, p.at(x=p.xm))
    send(G.at[p.xp, :, :, HB], XB[1], xb + 1, p.at(x=p.xp))
    yield

    for i in range(3):
        net.got(XB[i], xb + i)
    T = XB[0]
    add(T, XB[0], XB[1], XB[2], G.at[p.x, :, :, HB])
    send(T.at[p.yh, p.o], H[0], g + 0, p.at(c=p.o), p.own)
    for cc in range(2):
        send(T.at[1 - p.yh, cc], H[3], g + 3, p.at(y=p.y2, c=cc), p.own)
        send(T.at[p.yhm, cc], H[1], g + 1, p.at(y=p.ym, c=cc), p.opp)
        send(T.at[p.yhp, cc], H[2], g + 2, p.at(y=p.yp, c=cc), p.opp)
    for i in range(3):
        net.got(YA[i], ya + i, p.own)
    S = YA[0]

    @pl.when(p.own)
    def _():
        add(S, YA[0], YA[1], YA[2], G.at[:, p.yh, :, HA])

    send(S.at[p.x, p.o], F[0], f + 0, p.at(c=p.o), p.own)
    for cc in range(2):
        send(S.at[p.x2, cc], F[3], f + 3, p.at(x=p.x2, c=cc), p.own)
        send(S.at[p.xm, cc], F[1], f + 1, p.at(x=p.xm, c=cc), p.own)
        send(S.at[p.xp, cc], F[2], f + 2, p.at(x=p.xp, c=cc), p.own)
    yield

    net.got(F[0], f + 0, p.opp)
    net.got(H[0], g + 0, p.opp)
    for i in range(1, 4):
        net.got(F[i], f + i)
        net.got(H[i], g + i)
    net.finish(mine)

    @pl.when(p.own)
    def _():
        F[0][...] = S[p.x, p.c]
        H[0][...] = T[p.yh, p.c]

    add(out.at[HA], *F)
    add(out.at[HB], *H)


def pieces(refs):
    return [[r.at[i] for i in range(r.shape[0])] for r in refs]


def train_kernel(*refs):
    (lens, gm_w, gf_w, taps_w, tok_h, cot_h, in_h, out_h, gate_h, up_h, down_h,
     layer_out, tokens_grad, SC, XR, sa_h, sb_h, sd_h, spill,
     tok, in_w, out_w, gate_w, up_w, down_w, SA, SB_, SD, resid, gains, GR, MR, R1, conv_s, gu_s, down_s, small_s, flip, T, N, GO, WC, WG, WD, SM, B, C, V, BX, MX, GC, HID, GGU, PA, DD, KP, GM,
     *more) = refs
    sa, sb, sd = [more[8 * i : 8 * i + 8] for i in range(3)]
    sk, se = [pieces(more[24 + 4 * i : 28 + 4 * i]) for i in range(2)]
    ring_a, ring_b = more[32:34], more[34:36]
    KG, X, SK, free, send, recv, local = more[36:]
    p = Place()
    BX[0, :, 0:8] = jnp.zeros((2, 8, 256), F32)
    GC[4, :, 128:136] = jnp.zeros((2, 8, 256), F32)
    greeted = greet(p, True, True, True)
    net = Net(p, send, recv, local)
    pairs = ((in_h, in_w), (out_h, out_w), (tok_h, tok), (cot_h, GO.at[p.z, p.c]), (gate_h, gate_w), (up_h, up_w), (down_h, down_w))
    arrived = [net.copy(a, b) for a, b in pairs]
    block = lambda j: (p.z + j) % 4
    halo, halo_back = net.sem(), net.sem(4)
    partners = [p.at(c=p.o)]
    for cc in (0, 1):
        partners += [p.at(x=p.xp, c=cc), p.at(x=p.xm, c=cc), p.at(y=p.yp, c=cc), p.at(y=p.ym, c=cc)]
        partners += [p.at(x=p.x2, c=cc), p.at(y=p.y2, c=cc)]

    WA, WB = WG.at[:, :, :, :, 0:GA_N], WG.at[:, :, :, :, GA_N:]
    gt_sent, go_sent, g2_sent, g3_sent, gu_sent, w_sent = [], [], [], [], [], []
    gt = gather_ring(net, tok_h, T, gt_sent)
    go = gather_ring(net, GO.at[p.z, p.c], GO, go_sent)
    am = gather_plane(net, small_s, SM, w_sent, True)
    ac = gather_plane(net, conv_s.at[:, 0:384], WC.at[:, :, :, :, 0:384], w_sent, True)
    ae = gather_plane(net, conv_s.at[:, 384:768], WC.at[:, :, :, :, 384:768], w_sent, True)
    ad = gather_plane(net, down_s, WD, w_sent, True)
    au = gather_plane(net, gu_s.at[:, 0:GA_N], WA, gu_sent)
    av = gather_plane(net, gu_s.at[:, GA_N:], WB, gu_sent, True)

    arrived[0](), arrived[1]()
    flip[0:256] = jnp.zeros((256, 128), F32)
    flip[0:CH, 0:96] = out_w[...].astype(F32)
    o = flip[0:256].T[0:96]
    side = jnp.zeros((96, 64), F32)
    w = [jnp.concatenate([in_w[i].astype(F32), side], axis=1) for i in range(3)]
    parts = [
        w[1][:, 0:128],
        o[:, 0:128],
        o[:, 128:256] + pltpu.roll(w[1][:, 128:256], 64, 1),
        w[0][:, 0:128],
        w[2][:, 0:128],
        w[0][:, 128:256] + pltpu.roll(w[2][:, 128:256], 64, 1),
    ]
    conv_s[...] = jnp.concatenate(parts, axis=1).astype(BF)
    wide_row = lambda g: jnp.concatenate([g[...].astype(F32), jnp.zeros((1, 160), F32)], axis=1)
    gain = jnp.concatenate([wide_row(gm_w), wide_row(gf_w), jnp.zeros((6, 256), F32)], axis=0)
    small_s[0:16] = jnp.concatenate(
        [pltpu.roll(gain, lax.rem(96 * lax.axis_index("dp"), 128), 1), jnp.zeros((8, 256), F32)], axis=0
    ).astype(BF)
    taps_row = jnp.concatenate([taps_w[...].astype(F32), jnp.zeros((3, 64), F32)], axis=1)
    small_s[16:32] = jnp.concatenate([taps_row, jnp.zeros((13, 256), F32)], axis=0).astype(BF)
    greeted()
    step(gt)
    step(am), step(ac), step(ae)
    live = live_rows(lens)
    for f in arrived[2:]:
        f()
    GO[p.z, p.c] = (live * GO[p.z, p.c].astype(F32)).astype(BF)
    down_s[:, 768:FP] = jnp.zeros((96, 128), BF)
    down_s[:, 0:FB] = down_w[...]
    for t in range(7):
        n = 96 if t == 6 else 128
        if t == 6:
            gu_s[:, 1536:1792] = jnp.zeros((96, 256), BF)
        gu_s[:, 256 * t : 256 * t + n] = gate_w[:, 128 * t : 128 * t + n]
        gu_s[:, 256 * t + 128 : 256 * t + 128 + n] = up_w[:, 128 * t : 128 * t + n]
    own_tok = net.copy(tok, T.at[p.z, p.c])
    step(am)
    step(au)
    step(ac), step(ae)
    step(gt, 3)
    step(am), step(ac), step(ae)
    step(go)
    step(au)
    step(av), step(ad)
    step(gt, 2)
    step(am)
    gains[...] = jnp.zeros(gains.shape, F32)
    for s in range(16):
        piece = SM[s // 4, (s // 2) % 2, s % 2, 0:16].astype(F32)
        at = (96 * s) // 128 * 128
        n = min(256, gains.shape[1] - at)
        gains[0:16, at : at + n] = gains[0:16, at : at + n] + piece[:, :n]
    gains[16:32, 0:256] = SM[0, 0, 0, 16:32].astype(F32)
    g_mix, g_ffn = gains[0:1, :D], gains[1:2, :D]
    taps = [gains[16 + i : 17 + i, 0:256] for i in range(3)]
    own_tok()

    def norm(j):
        zj = block(j)
        for cc in range(2):
            row_norm(T.at[zj, cc], N.at[zj, cc], g_mix)

    norm(0)
    norm(1)
    norm(3)
    step(gt)
    norm(2)
    step(ac), step(ae)
    lanes = lax.broadcasted_iota(jnp.int32, (256, 128), 1) < 64

    def project(j):
        zj = block(j)
        r = dot(N[zj].reshape(256, D), whole(WC), NN)
        b1 = jnp.where(lanes, r[:, 640:768], 0.0)
        c1 = jnp.where(lanes, pltpu.roll(r[:, 256:384], 64, 1), 0.0)
        v1 = jnp.where(lanes, pltpu.roll(r[:, 640:768], 64, 1), 0.0)
        b = jnp.concatenate([r[:, 384:512], b1], axis=1)
        v = jnp.concatenate([r[:, 512:640], v1], axis=1)
        BX[zj, :, 8:136] = (b * v).reshape(2, 128, 256)
        B[zj] = b.astype(BF).reshape(2, 128, 256)
        V[zj] = v.astype(BF).reshape(2, 128, 256)
        C[zj] = jnp.concatenate([r[:, 0:128], c1], axis=1).astype(BF).reshape(2, 128, 256)

    for j in range(4):
        project(j)
    spilled = net.copy(N, spill)
    net.send(BX.at[0:4, :, 128:136], BX.at[pl.ds(p.yl, 4), :, 0:8], halo, p.at(y=p.y + 1 - 2 * p.yl))
    step(au)
    step(go, 2)
    net.finish(gt_sent)
    spilled()
    net.got(BX.at[pl.ds(1 - p.yl, 4), :, 0:8], halo)

    step(go)
    r1 = ReduceRing(net, PA, resid, *ring_a)

    def conv(zj, cc):
        return taps[0] * BX[zj, cc, 8:136] + taps[1] * BX[zj, cc, 7:135] + taps[2] * BX[zj, cc, 6:134]

    def mix(j):
        zj = block(j)
        for cc in range(2):
            MX[zj, cc] = (C[zj, cc].astype(F32) * conv(zj, cc)).astype(BF)
        o = whole(WC, slice(128, 384))
        PA[zj] = dot(MX[zj].reshape(256, 256), o, NT).astype(BF).reshape(2, 128, D)
        r1.push(j)

    r1_sent, r1_rest = r1.mine, r1.rest()
    mix(2)
    mix(1)
    step(r1_rest)
    mix(3)
    mix(0)
    step(r1_rest)
    step(av)
    step(r1_rest, 2)
    step(au)
    step(av)
    step(ad)
    step(go, 2)
    step(r1_rest)
    net.finish(r1_sent)

    def second(i, _):
        at = pl.ds(pl.multiple_of(i * 16, 16), 16)
        v = tok[at].astype(F32) + resid[at]
        resid[at] = v
        inv = lax.rsqrt(jnp.mean(v * v, axis=1, keepdims=True) + epsilon)
        N[p.z, p.c, at] = (v * inv * g_ffn).astype(BF)

    lax.fori_loop(0, ROWS // 16, second, None, unroll=4)
    g2 = gather_ring(net, N.at[p.z, p.c], N, g2_sent)
    step(g2)
    step(go)
    step(au)
    step(g2)
    step(av)

    def grad_down(x0, blocks, more=False):
        a = [GO[block(j), :, :, 384 * x0 : 384 * x0 + 384].reshape(256, 384) for j in blocks]
        w = dot(jnp.concatenate(a, axis=0), jnp.concatenate([HID[block(j)] for j in blocks], axis=0), TN)
        w = w.reshape(2, 2, 96, FP)
        DD[x0] = (DD[x0].astype(F32) + w if more else w).astype(BF)

    def ahead(j):
        zj = block(j)
        n2 = N[zj].reshape(256, D)
        for t in range(7):
            r = dot(n2, whole(WG, slice(256 * t, 256 * t + 256)), NN)
            g, u = r[:, :128], r[:, 128:]
            HID[zj, :, 128 * t : 128 * t + 128] = (g * jax.nn.sigmoid(g) * u).astype(BF)
            GGU[zj, :, 256 * t : 256 * t + 256] = r.astype(BF)

    def act(j):
        zj = block(j)
        for t in range(0, 7, 2):
            n = min(2, 7 - t)
            a = dot(GO[zj].reshape(256, D), whole(WD, slice(128 * t, 128 * (t + n))), NN)
            for i in range(n):
                ga = a[:, 128 * i : 128 * i + 128]
                at = 256 * (t + i)
                g, u = GGU[zj, :, at : at + 128].astype(F32), GGU[zj, :, at + 128 : at + 256].astype(F32)
                s = jax.nn.sigmoid(g)
                GGU[zj, :, at : at + 128] = (ga * u * s * (1.0 + g * (1.0 - s))).astype(BF)
                GGU[zj, :, at + 128 : at + 256] = (ga * g * s).astype(BF)

    def back(j):
        zj = block(j)
        PA[zj] = dot(GGU[zj], whole(WG), NT).astype(BF).reshape(2, 128, D)

    def down(j):
        zj = block(j)
        N[zj] = dot(HID[zj], whole(WD), NT).astype(BF).reshape(2, 128, D)

    ahead(0)
    step(g2, 2)
    step(ad)
    step(g2)
    ahead(1)
    ahead(3)
    for x0 in range(4):
        grad_down(x0, (0, 1, 3))
    step(g2, 2)
    ahead(2)
    step(ad)
    net.finish(go_sent)
    r2 = ReduceRing(net, PA, GR, *ring_a)
    r2_sent, r2_rest = r2.mine, r2.rest()
    def weight_grad(out, lhs, rhs, x0, n):
        a = lhs[:, :, :, 384 * x0 : 384 * x0 + 384].reshape(1024, 384)
        out[x0] = dot(a, rhs.reshape(1024, n), TN).astype(BF).reshape(2, 2, 96, n)

    def grad_a(x0):
        weight_grad(WA, N, GGU[:, :, 0:GA_N], x0, GA_N)

    def grad_b(x0):
        weight_grad(WB, N, GGU[:, :, GA_N:], x0, 1792 - GA_N)

    jd = reduce_plane(net, DD, SD, *sd)
    ja = reduce_plane(net, WA, SA, *sa)
    jb = reduce_plane(net, WB, SB_, *sb)
    act(2)
    back(2)
    r2.push(2)
    for x0 in range(4):
        grad_down(x0, (2,), True)
    step(jd)
    step(r2_rest)
    act(1)
    back(1)
    r2.push(1)
    step(jd)
    act(3)
    back(3)
    r2.push(3)
    act(0)
    step(r2_rest, 2)
    step(jd)
    back(0)
    r2.push(0)
    net.finish(gu_sent)
    for x0 in range(4):
        grad_a(x0)
    step(ja)
    step(ja)
    for x0 in range(4):
        grad_b(x0)
    step(jd)
    step(r2_rest, 2)
    net.finish(r2_sent)

    def third(i, _):
        at = pl.ds(pl.multiple_of(i * 16, 16), 16)
        v = resid[at]
        inv = lax.rsqrt(jnp.mean(v * v, axis=1, keepdims=True) + epsilon)
        x = v * inv
        w = g_ffn * GR[at]
        g = GO[p.z, p.c, at].astype(F32) + inv * (w - x * jnp.mean(w * x, axis=1, keepdims=True))
        GR[at] = g
        T[p.z, p.c, at] = g.astype(BF)

    lax.fori_loop(0, ROWS // 16, third, None, unroll=4)
    g3 = gather_ring(net, T.at[p.z, p.c], T, g3_sent)
    step(g3)
    reloaded = net.copy(spill, PA)
    step(jb)
    KP[...] = jnp.zeros(KP.shape, F32)
    GM[...] = jnp.zeros(GM.shape, F32)

    def unmix(j):
        zj = block(j)
        o = whole(WC, slice(128, 384))
        gm = dot(T[zj].reshape(256, D), o, NN)
        gm = jnp.concatenate([gm[:, :128], jnp.where(lanes, gm[:, 128:], 0.0)], axis=1).reshape(2, 128, 256)
        for cc in range(2):
            gc = gm[cc] * conv(zj, cc)
            at = slice(128 * cc, 128 * cc + 128)
            GGU[zj, at, 0:128] = gc[:, :128].astype(BF)
            GGU[zj, at, 128:256] = jnp.zeros((128, 128), BF)
            GGU[zj, at, 256:384] = pltpu.roll(gc[:, 128:], 64, 1).astype(BF)
            gv = gm[cc] * C[zj, cc].astype(F32)
            GC[zj + 1, cc, 0:128] = gv
            for i in range(3):
                KP[i : i + 1] = KP[i : i + 1] + jnp.sum(gv * BX[zj, cc, 8 - i : 136 - i], axis=0, keepdims=True)
        net.send(GC.at[zj + 1, :, 0:8], GC.at[zj + p.yl, :, 128:136], halo_back + j, p.at(y=p.y + 1 - 2 * p.yl))

    step(g3)
    unmix(0)
    net.finish(g2_sent)
    step(jb)
    down(0)
    step(g3)
    step(ja)
    down(1)
    down(2)
    down(3)
    step(g3)
    step(jd)
    step(g3)
    unmix(1)
    unmix(3)
    step(jb)
    step(g3, 2)
    unmix(2)
    r4 = ReduceRing(net, N, MR, *ring_a)
    r4_sent, r4_rest = r4.mine, r4.rest()
    for j in (2, 1, 3, 0):
        r4.push(j)
    reloaded()
    net.finish(w_sent)
    DE = WD.at[:, :, :, :, 0:384]
    for x0 in range(4):
        at = slice(384 * x0, 384 * x0 + 384)
        w = dot(PA[:, :, :, at].reshape(1024, 384), GGU[:, :, 0:384].reshape(1024, 384), TN)
        m = dot(T[:, :, :, at].reshape(1024, 384), MX[...].reshape(1024, 256), TN)
        w = jnp.concatenate([w[:, :128], m[:, :128], w[:, 256:] + m[:, 128:]], axis=1)
        DE[x0] = w.astype(BF).reshape(2, 2, 96, 384)
        if x0 == 1:
            step(r4_rest)
    je = reduce_direct(net, DE, SC.at[:, 0:384], *se)
    step(je)
    step(r4_rest)
    step(ja)
    for j in range(4):
        net.got(GC.at[block(j) + 1 - p.yl, :, 128:136], halo_back + j)
    r3 = ReduceRing(net, GO, R1, *ring_b)
    r3_sent, r3_rest = r3.mine, r3.rest()

    def unproject(j):
        zj = block(j)
        for cc in range(2):
            at = slice(128 * cc, 128 * cc + 128)
            gb = taps[0] * GC[zj + 1, cc, 0:128] + taps[1] * GC[zj + 1, cc, 1:129] + taps[2] * GC[zj + 1, cc, 2:130]
            bb, vv = gb * V[zj, cc].astype(F32), gb * B[zj, cc].astype(F32)
            GGU[zj, at, 384:512] = bb[:, :128].astype(BF)
            GGU[zj, at, 512:640] = vv[:, :128].astype(BF)
            GGU[zj, at, 640:768] = (bb[:, 128:] + pltpu.roll(vv[:, 128:], 64, 1)).astype(BF)
        r = dot(GGU[zj, :, 0:768], whole(WC), NT)
        GO[zj] = r.astype(BF).reshape(2, 128, D)
        GM[...] += jnp.sum((r * PA[zj].reshape(256, D).astype(F32)).reshape(32, 8, D), axis=0)
        r3.push(j)

    unproject(2)
    step(jd)
    for who in partners:
        pl.semaphore_signal(free, inc=1, device_id=who, device_id_type=MESH)
    unproject(1)
    unproject(3)
    step(r3_rest)
    unproject(0)
    step(r4_rest)
    step(r3_rest)
    step(jb)
    jk = reduce_direct(net, KG, SK, *sk)

    mix_row = jnp.sum(GM[...], axis=0, keepdims=True)
    mix_row = jnp.concatenate([mix_row / g_mix, jnp.zeros((1, 128), F32)], axis=1)
    low = lax.broadcasted_iota(jnp.int32, (1, 256), 1) < 96
    for s in range(16):
        at = (96 * s) // 128 * 128
        row = mix_row[:, at : at + 256]
        row = row if 96 * s == at else pltpu.roll(row, 256 - (96 * s - at), 1)
        tile = jnp.concatenate([KP[...], jnp.where(low, row, 0.0), jnp.zeros((23, 256), F32)], axis=0)
        KG[s // 4, (s // 2) % 2, s % 2] = tile.astype(BF)
    step(jk)
    DC = DD.at[:, :, :, :, 0:384]
    for x0 in range(4):
        at = slice(384 * x0, 384 * x0 + 384)
        w = dot(PA[:, :, :, at].reshape(1024, 384), GGU[:, :, 384:768].reshape(1024, 384), TN)
        DC[x0] = w.astype(BF).reshape(2, 2, 96, 384)
        if x0 == 1:
            step(ja)
            step(je)
    pl.semaphore_wait(free, len(partners))
    low_half, high_half = slice(0, 384), slice(384, 768)
    RB, F, RY, H = sd[1], sd[3], sd[5], sd[7]
    views = [
        [RB.at[0, :, :, :, low_half], RB.at[0, :, :, :, high_half], RB.at[1, :, :, :, low_half]],
        [RY.at[0, :, :, :, low_half], RY.at[0, :, :, :, high_half], RY.at[1, :, :, :, low_half]],
        [F.at[i, :, at] for i in range(2) for at in (low_half, high_half)],
        [H.at[i, :, at] for i in range(2) for at in (low_half, high_half)],
    ]
    jc = reduce_direct(net, DC, SC.at[:, 384:768], *views)
    step(jc)
    step(jk)
    step(r3_rest)
    step(jb)
    step(r4_rest)
    step(ja)
    step(jc)
    step(jb)
    ffn_share = jnp.sum(SA[...] * gu_s[:, 0:GA_N].astype(F32), axis=1, keepdims=True)
    ffn_share += jnp.sum(SB_[...] * gu_s[:, GA_N:].astype(F32), axis=1, keepdims=True)
    both = jnp.concatenate([jnp.broadcast_to(ffn_share, (96, 128)), jnp.zeros((32, 128), F32)], axis=0).T
    step(jk)
    written = [net.copy(a, b) for a, b in ((SA, sa_h), (SB_, sb_h), (SD, sd_h))]
    X[0:16] = SK[0:16]
    X[9:10, 0:96] = both[0:1, 0:96] / gf_w[...].astype(F32)
    me = lax.axis_index("tensor")
    done = net.copy(X, XR.at[me])
    base = net.sem(8)
    for i in range(1, 8):
        net.send(X, XR.at[me], base + i, (lax.axis_index("dp"), (me + i) % 8))
    step(r3_rest)
    step(r4_rest)
    step(je)
    step(r3_rest)

    def last(i, _):
        at = pl.ds(pl.multiple_of(i * 16, 16), 16)
        lv = live_rows(lens, i * 16, 16)
        layer_out[at] = (lv * (resid[at] + MR[at])).astype(BF)
        v = tok[at].astype(F32)
        inv = lax.rsqrt(jnp.mean(v * v, axis=1, keepdims=True) + epsilon)
        x = v * inv
        w = g_mix * R1[at]
        g = GR[at] + inv * (w - x * jnp.mean(w * x, axis=1, keepdims=True))
        tokens_grad[at] = g.astype(BF)

    lax.fori_loop(0, ROWS // 16, last, None, unroll=4)
    step(jc)
    for i in range(1, 8):
        net.got(XR.at[(me + 8 - i) % 8], base + i)
    done()
    for f in written:
        f()
    for job in (gt, go, g2, g3, am, ac, ae, ad, au, av, r1_rest, r2_rest, r3_rest, r4_rest, ja, jb, jd, jc, je, jk):
        assert next(job, "end") == "end"
    assert max(net.ns, net.nr) <= SEMS and net.nl <= 24
    net.finish(r3_sent + r4_sent + g3_sent + w_sent)
    net.finish()


GA_N = 1024
SEMS = 480


def train_call(*args):
    any_, vm = pl.BlockSpec(memory_space=pl.ANY), pl.BlockSpec(memory_space=pltpu.VMEM)
    ring, wide = (4, 2, ROWS, D), (4, 2, ROWS, 256)
    sums = [(96, n) for n in (GA_N, 1792 - GA_N, FP)]
    outs = [shape((ROWS, D)), shape((ROWS, D)), shape((96, 768), F32), shape((8, 16, 256), F32)]
    outs += [shape(n, F32) for n in sums] + [shape(ring)]
    v = lambda s, t=BF: pltpu.VMEM(s, t)
    scratch = [v((ROWS, D)), v((3, 96, CH)), v((CH, 96))] + [v((96, FB))] * 3 + [v(n, F32) for n in sums]
    scratch += [v((ROWS, D), F32), v((32, D), F32)] + [v((ROWS, D), F32)] * 3
    scratch += [v((96, 768)), v((96, 1792)), v((96, FP)), v((32, 256)), v((256, 128), F32)]
    scratch += [v(ring)] * 3 + [v((4, 2, 2, 96, n)) for n in (768, 1792, FP)] + [v((4, 2, 2, 32, 256))]
    scratch += [v(wide)] * 3 + [v((5, 2, 136, 256), F32), v(wide), v((5, 2, 136, 256), F32)]
    scratch += [v((4, 256, FP)), v((4, 256, 1792)), v(ring), v((4, 2, 2, 96, FP)), v((8, 256), F32), v((8, D), F32)]
    scratch += plane_scratch(GA_N) + plane_scratch(1792 - GA_N) + plane_scratch(FP) + direct_scratch(256, 16) + direct_scratch(384)
    scratch += ring_scratch(D) * 2 + [v((4, 2, 2, 32, 256)), v((16, 256), F32), v((32, 256), F32)]
    scratch += [pltpu.SemaphoreType.REGULAR]
    scratch += [pltpu.SemaphoreType.DMA((SEMS,)), pltpu.SemaphoreType.DMA((SEMS,)), pltpu.SemaphoreType.DMA((24,))]
    layer_out, tokens_grad, sc, xr, sa, sb, sd, _ = pl.pallas_call(
        train_kernel,
        out_shape=tuple(outs),
        in_specs=[vm] * 4 + [any_] * 7,
        out_specs=tuple([vm] * 4 + [any_] * 4),
        scratch_shapes=scratch,
        compiler_params=pltpu.CompilerParams(
            collective_id=0, has_side_effects=True, vmem_limit_bytes=64 << 20),
        name="train",
    )(*args)
    return layer_out, tokens_grad, sa, sb, sd, sc, xr


def finish_kernel(lo, tg, SA, SB, SD, SC, XR,
                  layer_out, tokens_grad, mix, in_grad, taps, out_grad, ffn, gate, up, down, flip):
    layer_out[...] = lo[...]
    tokens_grad[...] = tg[...]
    for t in range(7):
        n = 96 if t == 6 else 128
        src, at = (SA, 256 * t) if t < 4 else (SB, 256 * t - 1024)
        gate[:, 128 * t : 128 * t + n] = src[:, at : at + n]
        up[:, 128 * t : 128 * t + n] = src[:, at + 128 : at + 128 + n]
    down[...] = SD[:, 0:FB]
    flip[96:128] = jnp.zeros((32, 256), F32)
    flip[0:96] = SC[:, 128:384]
    out_grad[...] = flip[...].T[0:CH, 0:96]
    for i in range(3):
        at = (384, 0, 512)[i]
        in_grad[i, :, 0:128] = SC[:, at : at + 128]
    in_grad[0, :, 128:192] = SC[:, 640:704]
    in_grad[1, :, 128:192] = pltpu.roll(SC[:, 256:384], 64, 1)[:, :64]
    in_grad[2, :, 128:192] = pltpu.roll(SC[:, 640:768], 64, 1)[:, :64]
    dp, t = lax.axis_index("dp"), lax.axis_index("tensor")
    shares = XR[0, 8:16]
    for i in range(1, 8):
        shares = shares + XR[i, 8:16]
    shares = pltpu.roll(shares, 256 - 12 * t, 1)
    mix[...] = shares[0:1, 0:12]
    ffn[...] = shares[1:2, 0:12]
    k = pltpu.roll(XR[dp // 2, 0:8], lax.rem(256 - 12 * ((dp * 8 + t) % 16), 256), 1)
    taps[...] = k[0:3, 0:12]


def finish_call(*args):
    vm = pl.BlockSpec(memory_space=pltpu.VMEM)
    outs = [shape((ROWS, D)), shape((ROWS, D)), shape((1, 12), F32), shape((3, 96, CH), F32), shape((3, 12), F32)]
    outs += [shape((CH, 96), F32), shape((1, 12), F32), shape((96, FB), F32), shape((96, FB), F32), shape((96, FB), F32)]
    return pl.pallas_call(
        finish_kernel,
        out_shape=tuple(outs),
        in_specs=[vm] * 7,
        out_specs=tuple([vm] * 10),
        scratch_shapes=[pltpu.VMEM((128, 256), F32)],
        compiler_params=pltpu.CompilerParams(vmem_limit_bytes=VMEM_LIMIT),
        name="finish",
    )(*args)


def per_device(tokens, gain_mix, in_weight, conv_kernel, out_weight, gain_ffn, gate_weight, up_weight, down_weight, lengths, cotangent):
    gm, gf, lens = gain_mix.reshape(1, 96), gain_ffn.reshape(1, 96), lengths.reshape(1, 1)
    sums = train_call(
        lens, gm, gf, conv_kernel, tokens, cotangent, in_weight.transpose(1, 0, 2), out_weight, gate_weight,
        up_weight, down_weight.T)
    layer_out, tokens_grad, mix, in_grad, taps_grad, out_grad, ffn, gate, up, down = finish_call(*sums)
    return layer_out, tokens_grad, mix[0], in_grad.transpose(1, 0, 2), taps_grad, out_grad, ffn[0], gate, up, down.T


def solution(mesh):
    placed = (
        P(("dp", "tensor"), None),
        P("dp"),
        P("dp", None, "tensor"),
        P(None, "tensor"),
        P("tensor", "dp"),
        P("dp"),
        P("dp", "tensor"),
        P("dp", "tensor"),
        P("tensor", "dp"),
        P("dp"),
        P(("dp", "tensor"), None),
    )
    return jax.shard_map(
        per_device,
        mesh=mesh,
        in_specs=placed,
        out_specs=(
            P(("dp", "tensor"), None),
            P(("dp", "tensor"), None),
            P(("dp", "tensor")),
            P("dp", None, "tensor"),
            P(None, ("dp", "tensor")),
            P("tensor", "dp"),
            P(("dp", "tensor")),
            P("dp", "tensor"),
            P("dp", "tensor"),
            P("tensor", "dp"),
        ),
        check_vma=False,
    )
```

```python
import functools

import jax
import jax.numpy as jnp
from jax import lax
from jax.experimental import pallas as pl
from jax.experimental.pallas import tpu as pltpu
from jax.sharding import PartitionSpec as P

epsilon = 1e-05
MESH = pl.DeviceIdType.MESH
BF = jnp.bfloat16
F32 = jnp.float32
D = 1536
ROWS = 128
CH = 192
FB = 864
FP = 896
HALF = 48
VMEM_LIMIT = 60 << 20


class Place:
    def __init__(self):
        dp = lax.axis_index("dp")
        t = lax.axis_index("tensor")
        self.x, self.yh, self.c = dp // 4, (dp // 2) % 2, dp % 2
        self.z, self.yl = t // 2, t % 2
        self.y = self.yh * 2 + self.yl
        self.o = 1 - self.c
        self.xp, self.xm, self.x2 = (self.x + 1) % 4, (self.x + 3) % 4, (self.x + 2) % 4
        self.yp, self.ym = (self.y + 1) % 4, (self.y + 3) % 4
        self.y2 = (self.y + 2) % 4
        self.yhp, self.yhm = self.yp // 2, self.ym // 2
        self.way = 1 - 2 * self.c
        self.zf = (self.z + self.way + 4) % 4
        self.zb = (self.z - self.way + 4) % 4
        self.zp, self.zm, self.z2 = (self.z + 1) % 4, (self.z + 3) % 4, (self.z + 2) % 4
        self.own = self.c == self.yl
        self.opp = self.c != self.yl

    def at(self, x=None, y=None, z=None, c=None):
        x = self.x if x is None else x
        y = self.y if y is None else y
        z = self.z if z is None else z
        c = self.c if c is None else c
        return (x * 4 + (y // 2) * 2 + c, z * 2 + y % 2)


class Net:
    def __init__(self, place, send, recv, local=None):
        self.p, self.ss, self.rs, self.ls = place, send, recv, local
        self.ns = self.nr = self.nl = 0
        self.pending = []

    def sem(self, n=1):
        k = self.nr
        self.nr += n
        return k

    def send(self, src, dst, recv_index, target, cond=None, pending=None):
        k = self.ns
        self.ns += 1
        d = pltpu.make_async_remote_copy(
            src_ref=src, dst_ref=dst, send_sem=self.ss.at[k], recv_sem=self.rs.at[recv_index],
            device_id=target, device_id_type=MESH)
        run(cond, d.start)
        (self.pending if pending is None else pending).append((cond, d))

    def copy(self, src, dst, cond=None):
        k = self.nl
        self.nl += 1
        d = pltpu.make_async_copy(src, dst, self.ls.at[k])
        run(cond, d.start)
        return lambda: run(cond, d.wait)

    def got(self, dst, recv_index, cond=None):
        d = pltpu.make_async_remote_copy(
            src_ref=dst, dst_ref=dst, send_sem=self.ss.at[0], recv_sem=self.rs.at[recv_index],
            device_id=self.p.at(c=self.p.o), device_id_type=MESH)
        run(cond, d.wait_recv)

    def finish(self, pending=None):
        pending = self.pending if pending is None else pending
        for cond, d in pending:
            run(cond, d.wait_send)
        pending.clear()


def run(cond, f):
    if cond is None:
        f()
    else:
        pl.when(cond)(f)


def greet(p, plane, ring, group=False):
    bar = pltpu.get_barrier_semaphore()
    who = [p.at(c=p.o)]
    if plane:
        for c in (0, 1):
            who += [p.at(x=p.xp, c=c), p.at(x=p.xm, c=c), p.at(y=p.yp, c=c), p.at(y=p.ym, c=c)]
            who += [p.at(x=p.x2, c=c), p.at(y=p.y2, c=c)]
    if group:
        me = lax.axis_index("tensor")
        who += [(lax.axis_index("dp"), (me + i) % 8) for i in range(1, 8)]
    elif ring:
        who += [p.at(z=p.zp), p.at(z=p.zm)]
    for w in who:
        pl.semaphore_signal(bar, inc=1, device_id=w, device_id_type=MESH)
    return lambda: pl.semaphore_wait(bar, len(who))


def add(out, *terms):
    plain = len(terms) == 2 and all(t.dtype == BF for t in (out, *terms))
    lead = out.shape[:-2]
    count = 1
    for s in lead:
        count *= s

    def total(at):
        v = terms[0][at] if plain else terms[0][at].astype(F32)
        for t in terms[1:]:
            v = v + (t[at] if plain else t[at].astype(F32))
        out[at] = v.astype(out.dtype)

    def one(i):
        at = []
        for s in reversed(lead):
            at.append(i % s)
            i = i // s
        total(tuple(reversed(at)))

    if not lead:

        def rows(i, _):
            total(pl.ds(pl.multiple_of(i * 16, 16), 16))

        lax.fori_loop(0, out.shape[0] // 16, rows, None, unroll=2)
    else:
        lax.fori_loop(0, count, lambda i, _: one(i), None, unroll=2)


def ring_scratch(n):
    return [pltpu.VMEM((4, ROWS, n), BF), pltpu.VMEM((3, ROWS, n), BF)]


def shape(s, t=BF):
    return jax.ShapeDtypeStruct(s, t)


def slots(n):
    return shape((4, 2, 2, 96, n))


def gather_plane(net, sh, W, mine, far=False):
    p = net.p
    send = functools.partial(net.send, pending=mine)
    h = sh.shape[0] // 2
    HA, HB = pl.ds(0, h), pl.ds(h, h)
    i_own, f1, f2, f3, f4 = net.sem(), net.sem(2), net.sem(2), net.sem(2), net.sem(2)
    r1, r2, r3, r4, y1, y2, y3, y4, x1, x2, x3, x4 = (net.sem() for _ in range(12))
    f5, f6 = net.sem(2), net.sem(2)
    q = p.yl

    def pass_near():
        net.got(W.at[p.xm, p.yh, 0, HA], f1 + 0, p.own)
        net.got(W.at[p.x, p.yhm, 0, HB], f3 + 0, p.opp)
        send(W.at[p.xm, p.yh, 0, HA], W.at[p.xm, p.yh, 0, HA], r1, p.at(x=p.xp), p.own)
        send(W.at[p.x, p.yhm, 0, HB], W.at[p.x, p.yhm, 0, HB], r3, p.at(y=p.yp), p.opp)
        net.got(W.at[p.xp, p.yh, 1, HA], f2 + 1, p.own)
        net.got(W.at[p.x, p.yhp, 1, HB], f4 + 1, p.opp)
        send(W.at[p.xp, p.yh, 1, HA], W.at[p.xp, p.yh, 1, HA], r2, p.at(x=p.xm), p.own)
        send(W.at[p.x, p.yhp, 1, HB], W.at[p.x, p.yhp, 1, HB], r4, p.at(y=p.ym), p.opp)
        yield

    done = net.copy(sh, W.at[p.x, p.yh, p.c], p.own)
    send(sh.at[HA], W.at[p.x, p.yh, p.c, HA], f1 + p.c, p.at(x=p.xp, c=q))
    send(sh.at[HA], W.at[p.x, p.yh, p.c, HA], f2 + p.c, p.at(x=p.xm, c=q))
    send(sh.at[HB], W.at[p.x, p.yh, p.c, HB], f3 + p.c, p.at(y=p.yp, c=q))
    send(sh.at[HB], W.at[p.x, p.yh, p.c, HB], f4 + p.c, p.at(y=p.ym, c=q))
    send(sh, W.at[p.x, p.yh, p.c], i_own, p.at(c=p.o), p.opp)
    if far:
        send(sh.at[HA], W.at[p.x, p.yh, p.c, HA], f5 + p.c, p.at(x=p.x2, c=q))
        send(sh.at[HB], W.at[p.x, p.yh, p.c, HB], f6 + p.c, p.at(y=p.y2, c=q))
    yield
    if not far:
        yield from pass_near()
    done()
    net.got(W.at[p.x, p.yh, p.o], i_own, p.own)
    net.got(W.at[p.xm, p.yh, 1, HA], f1 + 1, p.own)
    net.got(W.at[p.xp, p.yh, 0, HA], f2 + 0, p.own)
    net.got(W.at[p.x, p.yhm, 1, HB], f3 + 1, p.opp)
    net.got(W.at[p.x, p.yhp, 0, HB], f4 + 0, p.opp)
    if far:
        net.got(W.at[p.xm, p.yh, 0, HA], f1 + 0, p.own)
        net.got(W.at[p.xp, p.yh, 1, HA], f2 + 1, p.own)
        net.got(W.at[p.x, p.yhm, 0, HB], f3 + 0, p.opp)
        net.got(W.at[p.x, p.yhp, 1, HB], f4 + 1, p.opp)
    for cc in range(2):
        net.got(W.at[p.x2, p.yh, cc, HA], f5 + cc if far else (r1, r2)[cc], p.own)
    send(W.at[:, p.yh, :, HA], W.at[:, p.yh, :, HA], y1, p.at(y=p.yp), p.own)
    send(W.at[:, p.yh, :, HA], W.at[:, p.yh, :, HA], y2, p.at(y=p.ym), p.own)
    for cc in range(2):
        net.got(W.at[p.x, 1 - p.yh, cc, HB], f6 + cc if far else (r3, r4)[cc], p.own)
    send(W.at[p.x, :, :, HB], W.at[p.x, :, :, HB], x1, p.at(x=p.xp))
    send(W.at[p.x, :, :, HB], W.at[p.x, :, :, HB], x2, p.at(x=p.xm))
    yield
    net.got(W.at[p.xm, :, :, HB], x1)
    send(W.at[p.xm, :, 0, HB], W.at[p.xm, :, 0, HB], x3, p.at(x=p.xp))
    net.got(W.at[p.xp, :, :, HB], x2)
    send(W.at[p.xp, :, 1, HB], W.at[p.xp, :, 1, HB], x4, p.at(x=p.xm))
    net.got(W.at[:, p.yhm, :, HA], y1, p.opp)
    send(W.at[:, p.yhm, 0, HA], W.at[:, p.yhm, 0, HA], y3, p.at(y=p.yp), p.opp)
    net.got(W.at[:, p.yhp, :, HA], y2, p.opp)
    send(W.at[:, p.yhp, 1, HA], W.at[:, p.yhp, 1, HA], y4, p.at(y=p.ym), p.opp)
    yield
    net.got(W.at[:, 1 - p.yh, 0, HA], y3, p.own)
    net.got(W.at[:, 1 - p.yh, 1, HA], y4, p.own)
    net.got(W.at[p.x2, :, 0, HB], x3)
    net.got(W.at[p.x2, :, 1, HB], x4)


PARTS = [pl.ds(0, 64), pl.ds(64, 64)]


def gather_ring(net, a, out, mine, late=False):
    p = net.p
    send = functools.partial(net.send, pending=mine)
    s1, s3, s2 = net.sem(2), net.sem(2), net.sem(2)
    k = net.sem(8)
    jf, jb = (p.zf - p.z + 4) % 4, (p.zb - p.z + 4) % 4
    for i, r in enumerate(PARTS):
        send(a.at[r], out.at[p.z, p.c, r], s1 + i, p.at(z=p.zf))
        send(a.at[r], out.at[p.z, p.c, r], s3 + i, p.at(z=p.zb))
    for i, r in enumerate(PARTS):
        send(a.at[r], out.at[p.z, p.c, r], k + 4 * i, p.at(c=p.o))
    yield
    for i, r in enumerate(PARTS):
        net.got(out.at[p.z, p.o, r], k + 4 * i)
    yield
    for i, r in enumerate(PARTS):
        net.got(out.at[p.zb, p.c, r], s1 + i)
        if not late:
            send(out.at[p.zb, p.c, r], out.at[p.zb, p.c, r], s2 + i, p.at(z=p.zf))
        send(out.at[p.zb, p.c, r], out.at[p.zb, p.c, r], k + 4 * i + jb, p.at(c=p.o))
        net.got(out.at[p.zf, p.c, r], s3 + i)
        send(out.at[p.zf, p.c, r], out.at[p.zf, p.c, r], k + 4 * i + jf, p.at(c=p.o))
        yield
    for i, r in enumerate(PARTS):
        net.got(out.at[p.zp, p.o, r], k + 4 * i + 1)
        net.got(out.at[p.zm, p.o, r], k + 4 * i + 3)
    yield
    if late:
        for i, r in enumerate(PARTS):
            send(out.at[p.zb, p.c, r], out.at[p.zb, p.c, r], s2 + i, p.at(z=p.zf))
        yield
    for i, r in enumerate(PARTS):
        net.got(out.at[p.z2, p.c, r], s2 + i)
        send(out.at[p.z2, p.c, r], out.at[p.z2, p.c, r], k + 4 * i + 2, p.at(c=p.o))
    yield
    for i, r in enumerate(PARTS):
        net.got(out.at[p.z2, p.o, r], k + 4 * i + 2)


class ReduceRing:
    def __init__(self, net, V, out, RC, RZ):
        self.net, self.V, self.out, self.RC, self.RZ = net, V, out, RC, RZ
        self.s2, self.sd, self.sr, self.k = net.sem(2), net.sem(2), net.sem(2), net.sem(8)
        self.mine = []
        self.send = functools.partial(net.send, pending=self.mine)

    def push(self, j):
        p = self.net.p
        for i, r in enumerate(PARTS):
            self.send(self.V.at[(p.z + j) % 4, p.o, r], self.RC.at[j, r], self.k + 4 * i + j, p.at(c=p.o))

    def rest(self):
        net, p, V, RC, RZ, k = self.net, self.net.p, self.V, self.RC, self.RZ, self.k
        jf, jb = (p.zf - p.z + 4) % 4, (p.zb - p.z + 4) % 4
        for i, r in enumerate(PARTS):
            net.got(RC.at[2, r], k + 4 * i + 2)
            add(RC.at[2, r], V.at[p.z2, p.c, r], RC.at[2, r])
            self.send(RC.at[2, r], RZ.at[0, r], self.s2 + i, p.at(z=p.zf))
        yield
        for i, r in enumerate(PARTS):
            net.got(RC.at[jb, r], k + 4 * i + jb)
            add(RC.at[jb, r], V.at[p.zb, p.c, r], RC.at[jb, r])
            self.send(RC.at[jb, r], RZ.at[1, r], self.sd + i, p.at(z=p.zb))
        for i, r in enumerate(PARTS):
            net.got(RC.at[jf, r], k + 4 * i + jf)
            add(RC.at[jf, r], V.at[p.zf, p.c, r], RC.at[jf, r])
        yield
        for i, r in enumerate(PARTS):
            net.got(RZ.at[0, r], self.s2 + i)
            add(RC.at[jf, r], RC.at[jf, r], RZ.at[0, r])
            self.send(RC.at[jf, r], RZ.at[2, r], self.sr + i, p.at(z=p.zf))
        yield
        for i, r in enumerate(PARTS):
            net.got(RC.at[0, r], k + 4 * i)
            add(RC.at[0, r], V.at[p.z, p.c, r], RC.at[0, r])
        yield
        for i, r in enumerate(PARTS):
            net.got(RZ.at[1, r], self.sd + i)
            net.got(RZ.at[2, r], self.sr + i)
            add(self.out.at[r], RC.at[0, r], RZ.at[1, r], RZ.at[2, r])


def step(job, times=1):
    for _ in range(times):
        next(job, None)


def dot(a, b, dims):
    return lax.dot_general(a, b, (dims, ((), ())), preferred_element_type=F32)


NN, NT, TN = ((1,), (0,)), ((1,), (1,)), ((0,), (0,))


def whole(ref, columns=slice(None)):
    v = ref[:, :, :, :, columns]
    return v.reshape(D, v.shape[-1])


def row_norm(src, dst, gain, rows=32):
    def one(i, _):
        at = pl.ds(pl.multiple_of(i * rows, rows), rows)
        v = src[at].astype(F32)
        inv = lax.rsqrt(jnp.mean(v * v, axis=1, keepdims=True) + epsilon)
        dst[at] = (v * inv * gain).astype(dst.dtype)

    lax.fori_loop(0, ROWS // rows, one, None, unroll=2)


def live_rows(lens, first=0, rows=ROWS):
    at = lax.axis_index("tensor") * ROWS + first + lax.broadcasted_iota(jnp.int32, (rows, 1), 0)
    return jnp.where(at < lens[...], 1.0, 0.0).astype(F32)


def plane_scratch(n, h=HALF):
    return [
        pltpu.VMEM((2, 4, h, n), BF),
        pltpu.VMEM((2, 4, 2, h, n), BF),
        pltpu.VMEM((2, h, n), BF),
        pltpu.VMEM((3, h, n), BF),
        pltpu.VMEM((2, 2, h, n), BF),
        pltpu.VMEM((2, 2, 2, h, n), BF),
        pltpu.VMEM((2, h, n), BF),
        pltpu.VMEM((3, h, n), BF),
    ]


def reduce_plane(net, G, out, RA, RB, RC, F, RX, RY, RZ, H):
    p = net.p
    h = out.shape[0] // 2
    HA, HB = pl.ds(0, h), pl.ds(h, h)
    mine = []
    send = functools.partial(net.send, pending=mine)
    a0, a1, bp0, bp1, bm0, bm1, c0, c1, g0, g1, g2 = (net.sem() for _ in range(11))
    u0, u1, vp0, vp1, vm0, vm1, w0, w1, h0, h1, h2 = (net.sem() for _ in range(11))
    send(G.at[:, 1 - p.yh, 0, HA], RA.at[0], a0, p.at(y=p.ym), p.own)
    send(G.at[:, 1 - p.yh, 1, HA], RA.at[1], a1, p.at(y=p.yp), p.own)
    send(G.at[p.x2, :, 0, HB], RX.at[0], u0, p.at(x=p.xm))
    send(G.at[p.x2, :, 1, HB], RX.at[1], u1, p.at(x=p.xp))
    yield
    send(G.at[:, p.yhm, 1, HA], RB.at[0, :, 1], bp1, p.at(y=p.ym), p.opp)
    send(G.at[:, p.yhp, 0, HA], RB.at[1, :, 0], bm0, p.at(y=p.yp), p.opp)
    send(G.at[p.xm, :, 1, HB], RY.at[0, :, 1], vp1, p.at(x=p.xm))
    send(G.at[p.xp, :, 0, HB], RY.at[1, :, 0], vm0, p.at(x=p.xp))
    yield

    net.got(RX.at[0], u0)
    add(RX.at[0], RX.at[0], G.at[p.xm, :, 0, HB])
    send(RX.at[0], RY.at[0, :, 0], vp0, p.at(x=p.xm))
    net.got(RX.at[1], u1)
    add(RX.at[1], RX.at[1], G.at[p.xp, :, 1, HB])
    send(RX.at[1], RY.at[1, :, 1], vm1, p.at(x=p.xp))
    net.got(RA.at[0], a0, p.opp)
    net.got(RA.at[1], a1, p.opp)

    @pl.when(p.opp)
    def _():
        add(RA.at[0], RA.at[0], G.at[:, p.yhm, 0, HA])
        add(RA.at[1], RA.at[1], G.at[:, p.yhp, 1, HA])

    send(RA.at[0], RB.at[0, :, 0], bp0, p.at(y=p.ym), p.opp)
    send(RA.at[1], RB.at[1, :, 1], bm1, p.at(y=p.yp), p.opp)
    yield

    net.got(RY.at[0, :, 1], vp1)
    net.got(RY.at[1, :, 0], vm0)
    net.got(RY.at[0, :, 0], vp0)
    net.got(RY.at[1, :, 1], vm1)
    add(RY.at[0], RY.at[0], RY.at[1], G.at[p.x, :, :, HB])
    T = RY.at[0]
    send(T.at[1 - p.yh, 0], RZ.at[0], w0, p.at(y=p.ym), p.own)
    send(T.at[1 - p.yh, 1], RZ.at[1], w1, p.at(y=p.yp), p.own)
    send(T.at[p.yhm, 1], H.at[1], h1, p.at(y=p.ym, c=1), p.opp)
    send(T.at[p.yhp, 0], H.at[2], h2, p.at(y=p.yp, c=0), p.opp)
    send(T.at[p.yh, p.o], H.at[0], h0, p.at(c=p.o), p.own)

    net.got(RB.at[0, :, 1], bp1, p.own)
    net.got(RB.at[1, :, 0], bm0, p.own)
    net.got(RB.at[0, :, 0], bp0, p.own)
    net.got(RB.at[1, :, 1], bm1, p.own)

    @pl.when(p.own)
    def _():
        add(RB.at[0], RB.at[0], RB.at[1], G.at[:, p.yh, :, HA])

    S = RB.at[0]
    send(S.at[p.x2, 0], RC.at[0], c0, p.at(x=p.xm), p.own)
    send(S.at[p.x2, 1], RC.at[1], c1, p.at(x=p.xp), p.own)
    send(S.at[p.xm, 1], F.at[1], g1, p.at(x=p.xm, c=1), p.own)
    send(S.at[p.xp, 0], F.at[2], g2, p.at(x=p.xp, c=0), p.own)
    send(S.at[p.x, p.o], F.at[0], g0, p.at(c=p.o), p.own)
    yield

    net.got(RC.at[0], c0, p.own)
    net.got(RC.at[1], c1, p.own)
    net.got(RZ.at[0], w0, p.opp)
    net.got(RZ.at[1], w1, p.opp)

    @pl.when(p.own)
    def _():
        add(RC.at[0], RC.at[0], S.at[p.xm, 0])
        add(RC.at[1], RC.at[1], S.at[p.xp, 1])

    @pl.when(p.opp)
    def _():
        add(RZ.at[0], RZ.at[0], T.at[p.yhm, 0])
        add(RZ.at[1], RZ.at[1], T.at[p.yhp, 1])

    send(RC.at[0], F.at[1], g1, p.at(x=p.xm, c=0), p.own)
    send(RC.at[1], F.at[2], g2, p.at(x=p.xp, c=1), p.own)
    send(RZ.at[0], H.at[1], h1, p.at(y=p.ym, c=0), p.opp)
    send(RZ.at[1], H.at[2], h2, p.at(y=p.yp, c=1), p.opp)
    yield

    net.got(F.at[0], g0, p.opp)
    net.got(F.at[1], g1)
    net.got(F.at[2], g2)
    net.got(H.at[0], h0, p.opp)
    net.got(H.at[1], h1)
    net.got(H.at[2], h2)
    net.finish(mine)

    @pl.when(p.own)
    def _():
        F[0] = S[p.x, p.c]
        H[0] = T[p.yh, p.c]

    add(out.at[HA], F.at[0], F.at[1], F.at[2])
    add(out.at[HB], H.at[0], H.at[1], H.at[2])


def direct_scratch(n, h=HALF):
    return [
        pltpu.VMEM((3, 4, 2, h, n), BF),
        pltpu.VMEM((3, 2, 2, h, n), BF),
        pltpu.VMEM((4, h, n), BF),
        pltpu.VMEM((4, h, n), BF),
    ]


def reduce_direct(net, G, out, YA, XB, F, H):
    p = net.p
    h = out.shape[0] // 2
    HA, HB = pl.ds(0, h), pl.ds(h, h)
    mine = []
    send = functools.partial(net.send, pending=mine)
    ya, xb, f, g = net.sem(3), net.sem(3), net.sem(4), net.sem(4)
    send(G.at[:, 1 - p.yh, :, HA], YA[2], ya + 2, p.at(y=p.y2), p.own)
    send(G.at[:, p.yhm, :, HA], YA[0], ya + 0, p.at(y=p.ym), p.opp)
    send(G.at[:, p.yhp, :, HA], YA[1], ya + 1, p.at(y=p.yp), p.opp)
    send(G.at[p.x2, :, :, HB], XB[2], xb + 2, p.at(x=p.x2))
    send(G.at[p.xm, :, :, HB], XB[0], xb + 0, p.at(x=p.xm))
    send(G.at[p.xp, :, :, HB], XB[1], xb + 1, p.at(x=p.xp))
    yield

    for i in range(3):
        net.got(XB[i], xb + i)
    T = XB[0]
    add(T, XB[0], XB[1], XB[2], G.at[p.x, :, :, HB])
    send(T.at[p.yh, p.o], H[0], g + 0, p.at(c=p.o), p.own)
    for cc in range(2):
        send(T.at[1 - p.yh, cc], H[3], g + 3, p.at(y=p.y2, c=cc), p.own)
        send(T.at[p.yhm, cc], H[1], g + 1, p.at(y=p.ym, c=cc), p.opp)
        send(T.at[p.yhp, cc], H[2], g + 2, p.at(y=p.yp, c=cc), p.opp)
    for i in range(3):
        net.got(YA[i], ya + i, p.own)
    S = YA[0]

    @pl.when(p.own)
    def _():
        add(S, YA[0], YA[1], YA[2], G.at[:, p.yh, :, HA])

    send(S.at[p.x, p.o], F[0], f + 0, p.at(c=p.o), p.own)
    for cc in range(2):
        send(S.at[p.x2, cc], F[3], f + 3, p.at(x=p.x2, c=cc), p.own)
        send(S.at[p.xm, cc], F[1], f + 1, p.at(x=p.xm, c=cc), p.own)
        send(S.at[p.xp, cc], F[2], f + 2, p.at(x=p.xp, c=cc), p.own)
    yield

    net.got(F[0], f + 0, p.opp)
    net.got(H[0], g + 0, p.opp)
    for i in range(1, 4):
        net.got(F[i], f + i)
        net.got(H[i], g + i)
    net.finish(mine)

    @pl.when(p.own)
    def _():
        F[0][...] = S[p.x, p.c]
        H[0][...] = T[p.yh, p.c]

    add(out.at[HA], *F)
    add(out.at[HB], *H)


def pieces(refs):
    return [[r.at[i] for i in range(r.shape[0])] for r in refs]


def train_kernel(*refs):
    (lens, gm_w, gf_w, taps_w, tok_h, cot_h, in_h, out_h, gate_h, up_h, down_h,
     layer_out, tokens_grad, SC, XR, sa_h, sb_h, sd_h, spill,
     tok, in_w, out_w, gate_w, up_w, down_w, SA, SB_, SD, resid, gains, GR, MR, R1, conv_s, gu_s, down_s, small_s, flip, T, N, GO, WC, WG, WD, SM, B, C, V, BX, MX, GC, HID, GGU, PA, DD, KP, GM,
     *more) = refs
    sa, sb, sd = [more[8 * i : 8 * i + 8] for i in range(3)]
    sk, se = [pieces(more[24 + 4 * i : 28 + 4 * i]) for i in range(2)]
    ring_a, ring_b = more[32:34], more[34:36]
    KG, X, SK, free, send, recv, local = more[36:]
    p = Place()
    BX[0, :, 0:8] = jnp.zeros((2, 8, 256), F32)
    GC[4, :, 128:136] = jnp.zeros((2, 8, 256), F32)
    greeted = greet(p, True, True, True)
    net = Net(p, send, recv, local)
    pairs = ((in_h, in_w), (out_h, out_w), (tok_h, tok), (cot_h, GO.at[p.z, p.c]), (gate_h, gate_w), (up_h, up_w), (down_h, down_w))
    arrived = [net.copy(a, b) for a, b in pairs]
    block = lambda j: (p.z + j) % 4
    halo, halo_back = net.sem(), net.sem(4)
    partners = [p.at(c=p.o)]
    for cc in (0, 1):
        partners += [p.at(x=p.xp, c=cc), p.at(x=p.xm, c=cc), p.at(y=p.yp, c=cc), p.at(y=p.ym, c=cc)]
        partners += [p.at(x=p.x2, c=cc), p.at(y=p.y2, c=cc)]

    WA, WB = WG.at[:, :, :, :, 0:GA_N], WG.at[:, :, :, :, GA_N:]
    gt_sent, go_sent, g2_sent, g3_sent, gu_sent, w_sent = [], [], [], [], [], []
    gt = gather_ring(net, tok_h, T, gt_sent)
    go = gather_ring(net, GO.at[p.z, p.c], GO, go_sent)
    am = gather_plane(net, small_s, SM, w_sent, True)
    ac = gather_plane(net, conv_s.at[:, 0:384], WC.at[:, :, :, :, 0:384], w_sent, True)
    ae = gather_plane(net, conv_s.at[:, 384:768], WC.at[:, :, :, :, 384:768], w_sent, True)
    ad = gather_plane(net, down_s, WD, w_sent, True)
    au = gather_plane(net, gu_s.at[:, 0:GA_N], WA, gu_sent)
    av = gather_plane(net, gu_s.at[:, GA_N:], WB, gu_sent, True)

    arrived[0](), arrived[1]()
    flip[0:256] = jnp.zeros((256, 128), F32)
    flip[0:CH, 0:96] = out_w[...].astype(F32)
    o = flip[0:256].T[0:96]
    side = jnp.zeros((96, 64), F32)
    w = [jnp.concatenate([in_w[i].astype(F32), side], axis=1) for i in range(3)]
    parts = [
        w[1][:, 0:128],
        o[:, 0:128],
        o[:, 128:256] + pltpu.roll(w[1][:, 128:256], 64, 1),
        w[0][:, 0:128],
        w[2][:, 0:128],
        w[0][:, 128:256] + pltpu.roll(w[2][:, 128:256], 64, 1),
    ]
    conv_s[...] = jnp.concatenate(parts, axis=1).astype(BF)
    wide_row = lambda g: jnp.concatenate([g[...].astype(F32), jnp.zeros((1, 160), F32)], axis=1)
    gain = jnp.concatenate([wide_row(gm_w), wide_row(gf_w), jnp.zeros((6, 256), F32)], axis=0)
    small_s[0:16] = jnp.concatenate(
        [pltpu.roll(gain, lax.rem(96 * lax.axis_index("dp"), 128), 1), jnp.zeros((8, 256), F32)], axis=0
    ).astype(BF)
    taps_row = jnp.concatenate([taps_w[...].astype(F32), jnp.zeros((3, 64), F32)], axis=1)
    small_s[16:32] = jnp.concatenate([taps_row, jnp.zeros((13, 256), F32)], axis=0).astype(BF)
    greeted()
    step(gt)
    step(am), step(ac), step(ae)
    live = live_rows(lens)
    for f in arrived[2:]:
        f()
    GO[p.z, p.c] = (live * GO[p.z, p.c].astype(F32)).astype(BF)
    down_s[:, 768:FP] = jnp.zeros((96, 128), BF)
    down_s[:, 0:FB] = down_w[...]
    for t in range(7):
        n = 96 if t == 6 else 128
        if t == 6:
            gu_s[:, 1536:1792] = jnp.zeros((96, 256), BF)
        gu_s[:, 256 * t : 256 * t + n] = gate_w[:, 128 * t : 128 * t + n]
        gu_s[:, 256 * t + 128 : 256 * t + 128 + n] = up_w[:, 128 * t : 128 * t + n]
    own_tok = net.copy(tok, T.at[p.z, p.c])
    step(am)
    step(au)
    step(ac), step(ae)
    step(gt, 3)
    step(am), step(ac), step(ae)
    step(go)
    step(au)
    step(av), step(ad)
    step(gt, 2)
    step(am)
    gains[...] = jnp.zeros(gains.shape, F32)
    for s in range(16):
        piece = SM[s // 4, (s // 2) % 2, s % 2, 0:16].astype(F32)
        at = (96 * s) // 128 * 128
        n = min(256, gains.shape[1] - at)
        gains[0:16, at : at + n] = gains[0:16, at : at + n] + piece[:, :n]
    gains[16:32, 0:256] = SM[0, 0, 0, 16:32].astype(F32)
    g_mix, g_ffn = gains[0:1, :D], gains[1:2, :D]
    taps = [gains[16 + i : 17 + i, 0:256] for i in range(3)]
    own_tok()

    def norm(j):
        zj = block(j)
        for cc in range(2):
            row_norm(T.at[zj, cc], N.at[zj, cc], g_mix)

    norm(0)
    norm(1)
    norm(3)
    step(gt)
    norm(2)
    step(ac), step(ae)
    lanes = lax.broadcasted_iota(jnp.int32, (256, 128), 1) < 64

    def project(j):
        zj = block(j)
        r = dot(N[zj].reshape(256, D), whole(WC), NN)
        b1 = jnp.where(lanes, r[:, 640:768], 0.0)
        c1 = jnp.where(lanes, pltpu.roll(r[:, 256:384], 64, 1), 0.0)
        v1 = jnp.where(lanes, pltpu.roll(r[:, 640:768], 64, 1), 0.0)
        b = jnp.concatenate([r[:, 384:512], b1], axis=1)
        v = jnp.concatenate([r[:, 512:640], v1], axis=1)
        BX[zj, :, 8:136] = (b * v).reshape(2, 128, 256)
        B[zj] = b.astype(BF).reshape(2, 128, 256)
        V[zj] = v.astype(BF).reshape(2, 128, 256)
        C[zj] = jnp.concatenate([r[:, 0:128], c1], axis=1).astype(BF).reshape(2, 128, 256)

    for j in range(4):
        project(j)
    spilled = net.copy(N, spill)
    net.send(BX.at[0:4, :, 128:136], BX.at[pl.ds(p.yl, 4), :, 0:8], halo, p.at(y=p.y + 1 - 2 * p.yl))
    step(au)
    step(go, 2)
    net.finish(gt_sent)
    spilled()
    net.got(BX.at[pl.ds(1 - p.yl, 4), :, 0:8], halo)

    step(go)
    r1 = ReduceRing(net, PA, resid, *ring_a)

    def conv(zj, cc):
        return taps[0] * BX[zj, cc, 8:136] + taps[1] * BX[zj, cc, 7:135] + taps[2] * BX[zj, cc, 6:134]

    def mix(j):
        zj = block(j)
        for cc in range(2):
            MX[zj, cc] = (C[zj, cc].astype(F32) * conv(zj, cc)).astype(BF)
        o = whole(WC, slice(128, 384))
        PA[zj] = dot(MX[zj].reshape(256, 256), o, NT).astype(BF).reshape(2, 128, D)
        r1.push(j)

    r1_sent, r1_rest = r1.mine, r1.rest()
    mix(2)
    mix(1)
    step(r1_rest)
    mix(3)
    mix(0)
    step(r1_rest)
    step(av)
    step(r1_rest, 2)
    step(au)
    step(av)
    step(ad)
    step(go, 2)
    step(r1_rest)
    net.finish(r1_sent)

    def second(i, _):
        at = pl.ds(pl.multiple_of(i * 16, 16), 16)
        v = tok[at].astype(F32) + resid[at]
        resid[at] = v
        inv = lax.rsqrt(jnp.mean(v * v, axis=1, keepdims=True) + epsilon)
        N[p.z, p.c, at] = (v * inv * g_ffn).astype(BF)

    lax.fori_loop(0, ROWS // 16, second, None, unroll=4)
    g2 = gather_ring(net, N.at[p.z, p.c], N, g2_sent)
    step(g2)
    step(go)
    step(au)
    step(g2)
    step(av)

    def grad_down(x0, blocks, more=False):
        a = [GO[block(j), :, :, 384 * x0 : 384 * x0 + 384].reshape(256, 384) for j in blocks]
        w = dot(jnp.concatenate(a, axis=0), jnp.concatenate([HID[block(j)] for j in blocks], axis=0), TN)
        w = w.reshape(2, 2, 96, FP)
        DD[x0] = (DD[x0].astype(F32) + w if more else w).astype(BF)

    def ahead(j):
        zj = block(j)
        n2 = N[zj].reshape(256, D)
        for t in range(7):
            r = dot(n2, whole(WG, slice(256 * t, 256 * t + 256)), NN)
            g, u = r[:, :128], r[:, 128:]
            HID[zj, :, 128 * t : 128 * t + 128] = (g * jax.nn.sigmoid(g) * u).astype(BF)
            GGU[zj, :, 256 * t : 256 * t + 256] = r.astype(BF)

    def act(j):
        zj = block(j)
        for t in range(0, 7, 2):
            n = min(2, 7 - t)
            a = dot(GO[zj].reshape(256, D), whole(WD, slice(128 * t, 128 * (t + n))), NN)
            for i in range(n):
                ga = a[:, 128 * i : 128 * i + 128]
                at = 256 * (t + i)
                g, u = GGU[zj, :, at : at + 128].astype(F32), GGU[zj, :, at + 128 : at + 256].astype(F32)
                s = jax.nn.sigmoid(g)
                GGU[zj, :, at : at + 128] = (ga * u * s * (1.0 + g * (1.0 - s))).astype(BF)
                GGU[zj, :, at + 128 : at + 256] = (ga * g * s).astype(BF)

    def back(j):
        zj = block(j)
        PA[zj] = dot(GGU[zj], whole(WG), NT).astype(BF).reshape(2, 128, D)

    def down(j):
        zj = block(j)
        N[zj] = dot(HID[zj], whole(WD), NT).astype(BF).reshape(2, 128, D)

    ahead(0)
    step(g2, 2)
    step(ad)
    step(g2)
    ahead(1)
    ahead(3)
    for x0 in range(4):
        grad_down(x0, (0, 1, 3))
    step(g2, 2)
    ahead(2)
    step(ad)
    net.finish(go_sent)
    r2 = ReduceRing(net, PA, GR, *ring_a)
    r2_sent, r2_rest = r2.mine, r2.rest()
    def weight_grad(out, lhs, rhs, x0, n):
        a = lhs[:, :, :, 384 * x0 : 384 * x0 + 384].reshape(1024, 384)
        out[x0] = dot(a, rhs.reshape(1024, n), TN).astype(BF).reshape(2, 2, 96, n)

    def grad_a(x0):
        weight_grad(WA, N, GGU[:, :, 0:GA_N], x0, GA_N)

    def grad_b(x0):
        weight_grad(WB, N, GGU[:, :, GA_N:], x0, 1792 - GA_N)

    jd = reduce_plane(net, DD, SD, *sd)
    ja = reduce_plane(net, WA, SA, *sa)
    jb = reduce_plane(net, WB, SB_, *sb)
    act(2)
    back(2)
    r2.push(2)
    for x0 in range(4):
        grad_down(x0, (2,), True)
    step(jd)
    step(r2_rest)
    act(1)
    back(1)
    r2.push(1)
    step(jd)
    act(3)
    back(3)
    r2.push(3)
    step(r2_rest, 2)
    act(0)
    step(jd)
    back(0)
    r2.push(0)
    net.finish(gu_sent)
    for x0 in range(4):
        grad_a(x0)
    step(ja)
    step(ja)
    for x0 in range(4):
        grad_b(x0)
    step(jd)
    step(r2_rest, 2)
    net.finish(r2_sent)

    def third(i, _):
        at = pl.ds(pl.multiple_of(i * 16, 16), 16)
        v = resid[at]
        inv = lax.rsqrt(jnp.mean(v * v, axis=1, keepdims=True) + epsilon)
        x = v * inv
        w = g_ffn * GR[at]
        g = GO[p.z, p.c, at].astype(F32) + inv * (w - x * jnp.mean(w * x, axis=1, keepdims=True))
        GR[at] = g
        T[p.z, p.c, at] = g.astype(BF)

    lax.fori_loop(0, ROWS // 16, third, None, unroll=4)
    g3 = gather_ring(net, T.at[p.z, p.c], T, g3_sent)
    step(g3)
    reloaded = net.copy(spill, PA)
    step(jb)
    KP[...] = jnp.zeros(KP.shape, F32)
    GM[...] = jnp.zeros(GM.shape, F32)

    def unmix(j):
        zj = block(j)
        o = whole(WC, slice(128, 384))
        gm = dot(T[zj].reshape(256, D), o, NN)
        gm = jnp.concatenate([gm[:, :128], jnp.where(lanes, gm[:, 128:], 0.0)], axis=1).reshape(2, 128, 256)
        for cc in range(2):
            gc = gm[cc] * conv(zj, cc)
            at = slice(128 * cc, 128 * cc + 128)
            GGU[zj, at, 0:128] = gc[:, :128].astype(BF)
            GGU[zj, at, 128:256] = jnp.zeros((128, 128), BF)
            GGU[zj, at, 256:384] = pltpu.roll(gc[:, 128:], 64, 1).astype(BF)
            gv = gm[cc] * C[zj, cc].astype(F32)
            GC[zj + 1, cc, 0:128] = gv
            for i in range(3):
                KP[i : i + 1] = KP[i : i + 1] + jnp.sum(gv * BX[zj, cc, 8 - i : 136 - i], axis=0, keepdims=True)
        net.send(GC.at[zj + 1, :, 0:8], GC.at[zj + p.yl, :, 128:136], halo_back + j, p.at(y=p.y + 1 - 2 * p.yl))

    step(g3)
    unmix(0)
    net.finish(g2_sent)
    step(jb)
    down(0)
    step(g3)
    step(ja)
    down(1)
    down(2)
    down(3)
    step(g3)
    step(jd)
    step(g3)
    unmix(1)
    unmix(3)
    step(jb)
    step(g3, 2)
    unmix(2)
    r4 = ReduceRing(net, N, MR, *ring_a)
    r4_sent, r4_rest = r4.mine, r4.rest()
    for j in (2, 1, 3, 0):
        r4.push(j)
    reloaded()
    net.finish(w_sent)
    DE = WD.at[:, :, :, :, 0:384]
    for x0 in range(4):
        at = slice(384 * x0, 384 * x0 + 384)
        w = dot(PA[:, :, :, at].reshape(1024, 384), GGU[:, :, 0:384].reshape(1024, 384), TN)
        m = dot(T[:, :, :, at].reshape(1024, 384), MX[...].reshape(1024, 256), TN)
        w = jnp.concatenate([w[:, :128], m[:, :128], w[:, 256:] + m[:, 128:]], axis=1)
        DE[x0] = w.astype(BF).reshape(2, 2, 96, 384)
        if x0 == 1:
            step(r4_rest)
    je = reduce_direct(net, DE, SC.at[:, 0:384], *se)
    step(je)
    step(r4_rest)
    step(ja)
    for j in range(4):
        net.got(GC.at[block(j) + 1 - p.yl, :, 128:136], halo_back + j)
    r3 = ReduceRing(net, GO, R1, *ring_b)
    r3_sent, r3_rest = r3.mine, r3.rest()

    def unproject(j):
        zj = block(j)
        for cc in range(2):
            at = slice(128 * cc, 128 * cc + 128)
            gb = taps[0] * GC[zj + 1, cc, 0:128] + taps[1] * GC[zj + 1, cc, 1:129] + taps[2] * GC[zj + 1, cc, 2:130]
            bb, vv = gb * V[zj, cc].astype(F32), gb * B[zj, cc].astype(F32)
            GGU[zj, at, 384:512] = bb[:, :128].astype(BF)
            GGU[zj, at, 512:640] = vv[:, :128].astype(BF)
            GGU[zj, at, 640:768] = (bb[:, 128:] + pltpu.roll(vv[:, 128:], 64, 1)).astype(BF)
        r = dot(GGU[zj, :, 0:768], whole(WC), NT)
        GO[zj] = r.astype(BF).reshape(2, 128, D)
        GM[...] += jnp.sum((r * PA[zj].reshape(256, D).astype(F32)).reshape(32, 8, D), axis=0)
        r3.push(j)

    unproject(2)
    step(jd)
    for who in partners:
        pl.semaphore_signal(free, inc=1, device_id=who, device_id_type=MESH)
    unproject(1)
    unproject(3)
    step(r3_rest)
    unproject(0)
    step(r4_rest)
    step(r3_rest)
    step(jb)
    jk = reduce_direct(net, KG, SK, *sk)

    mix_row = jnp.sum(GM[...], axis=0, keepdims=True)
    mix_row = jnp.concatenate([mix_row / g_mix, jnp.zeros((1, 128), F32)], axis=1)
    low = lax.broadcasted_iota(jnp.int32, (1, 256), 1) < 96
    for s in range(16):
        at = (96 * s) // 128 * 128
        row = mix_row[:, at : at + 256]
        row = row if 96 * s == at else pltpu.roll(row, 256 - (96 * s - at), 1)
        tile = jnp.concatenate([KP[...], jnp.where(low, row, 0.0), jnp.zeros((23, 256), F32)], axis=0)
        KG[s // 4, (s // 2) % 2, s % 2] = tile.astype(BF)
    step(jk)
    DC = DD.at[:, :, :, :, 0:384]
    for x0 in range(4):
        at = slice(384 * x0, 384 * x0 + 384)
        w = dot(PA[:, :, :, at].reshape(1024, 384), GGU[:, :, 384:768].reshape(1024, 384), TN)
        DC[x0] = w.astype(BF).reshape(2, 2, 96, 384)
        if x0 == 1:
            step(ja)
            step(je)
    pl.semaphore_wait(free, len(partners))
    low_half, high_half = slice(0, 384), slice(384, 768)
    RB, F, RY, H = sd[1], sd[3], sd[5], sd[7]
    views = [
        [RB.at[0, :, :, :, low_half], RB.at[0, :, :, :, high_half], RB.at[1, :, :, :, low_half]],
        [RY.at[0, :, :, :, low_half], RY.at[0, :, :, :, high_half], RY.at[1, :, :, :, low_half]],
        [F.at[i, :, at] for i in range(2) for at in (low_half, high_half)],
        [H.at[i, :, at] for i in range(2) for at in (low_half, high_half)],
    ]
    jc = reduce_direct(net, DC, SC.at[:, 384:768], *views)
    step(jc)
    step(jk)
    step(r3_rest)
    step(jb)
    step(r4_rest)
    step(ja)
    step(jc)
    step(jb)
    ffn_share = jnp.sum(SA[...] * gu_s[:, 0:GA_N].astype(F32), axis=1, keepdims=True)
    ffn_share += jnp.sum(SB_[...] * gu_s[:, GA_N:].astype(F32), axis=1, keepdims=True)
    both = jnp.concatenate([jnp.broadcast_to(ffn_share, (96, 128)), jnp.zeros((32, 128), F32)], axis=0).T
    step(jk)
    written = [net.copy(a, b) for a, b in ((SA, sa_h), (SB_, sb_h), (SD, sd_h))]
    X[0:16] = SK[0:16]
    X[9:10, 0:96] = both[0:1, 0:96] / gf_w[...].astype(F32)
    me = lax.axis_index("tensor")
    done = net.copy(X, XR.at[me])
    base = net.sem(8)
    for i in range(1, 8):
        net.send(X, XR.at[me], base + i, (lax.axis_index("dp"), (me + i) % 8))
    step(r3_rest)
    step(r4_rest)
    step(je)
    step(r3_rest)

    def last(i, _):
        at = pl.ds(pl.multiple_of(i * 16, 16), 16)
        lv = live_rows(lens, i * 16, 16)
        layer_out[at] = (lv * (resid[at] + MR[at])).astype(BF)
        v = tok[at].astype(F32)
        inv = lax.rsqrt(jnp.mean(v * v, axis=1, keepdims=True) + epsilon)
        x = v * inv
        w = g_mix * R1[at]
        g = GR[at] + inv * (w - x * jnp.mean(w * x, axis=1, keepdims=True))
        tokens_grad[at] = g.astype(BF)

    lax.fori_loop(0, ROWS // 16, last, None, unroll=4)
    step(jc)
    for i in range(1, 8):
        net.got(XR.at[(me + 8 - i) % 8], base + i)
    done()
    for f in written:
        f()
    for job in (gt, go, g2, g3, am, ac, ae, ad, au, av, r1_rest, r2_rest, r3_rest, r4_rest, ja, jb, jd, jc, je, jk):
        assert next(job, "end") == "end"
    assert max(net.ns, net.nr) <= SEMS and net.nl <= 24
    net.finish(r3_sent + r4_sent + g3_sent + w_sent)
    net.finish()


GA_N = 1024
SEMS = 480


def train_call(*args):
    any_, vm = pl.BlockSpec(memory_space=pl.ANY), pl.BlockSpec(memory_space=pltpu.VMEM)
    ring, wide = (4, 2, ROWS, D), (4, 2, ROWS, 256)
    sums = [(96, n) for n in (GA_N, 1792 - GA_N, FP)]
    outs = [shape((ROWS, D)), shape((ROWS, D)), shape((96, 768), F32), shape((8, 16, 256), F32)]
    outs += [shape(n, F32) for n in sums] + [shape(ring)]
    v = lambda s, t=BF: pltpu.VMEM(s, t)
    scratch = [v((ROWS, D)), v((3, 96, CH)), v((CH, 96))] + [v((96, FB))] * 3 + [v(n, F32) for n in sums]
    scratch += [v((ROWS, D), F32), v((32, D), F32)] + [v((ROWS, D), F32)] * 3
    scratch += [v((96, 768)), v((96, 1792)), v((96, FP)), v((32, 256)), v((256, 128), F32)]
    scratch += [v(ring)] * 3 + [v((4, 2, 2, 96, n)) for n in (768, 1792, FP)] + [v((4, 2, 2, 32, 256))]
    scratch += [v(wide)] * 3 + [v((5, 2, 136, 256), F32), v(wide), v((5, 2, 136, 256), F32)]
    scratch += [v((4, 256, FP)), v((4, 256, 1792)), v(ring), v((4, 2, 2, 96, FP)), v((8, 256), F32), v((8, D), F32)]
    scratch += plane_scratch(GA_N) + plane_scratch(1792 - GA_N) + plane_scratch(FP) + direct_scratch(256, 16) + direct_scratch(384)
    scratch += ring_scratch(D) * 2 + [v((4, 2, 2, 32, 256)), v((16, 256), F32), v((32, 256), F32)]
    scratch += [pltpu.SemaphoreType.REGULAR]
    scratch += [pltpu.SemaphoreType.DMA((SEMS,)), pltpu.SemaphoreType.DMA((SEMS,)), pltpu.SemaphoreType.DMA((24,))]
    layer_out, tokens_grad, sc, xr, sa, sb, sd, _ = pl.pallas_call(
        train_kernel,
        out_shape=tuple(outs),
        in_specs=[vm] * 4 + [any_] * 7,
        out_specs=tuple([vm] * 4 + [any_] * 4),
        scratch_shapes=scratch,
        compiler_params=pltpu.CompilerParams(
            collective_id=0, has_side_effects=True, vmem_limit_bytes=64 << 20),
        name="train",
    )(*args)
    return layer_out, tokens_grad, sa, sb, sd, sc, xr


def finish_kernel(lo, tg, SA, SB, SD, SC, XR,
                  layer_out, tokens_grad, mix, in_grad, taps, out_grad, ffn, gate, up, down, flip):
    layer_out[...] = lo[...]
    tokens_grad[...] = tg[...]
    for t in range(7):
        n = 96 if t == 6 else 128
        src, at = (SA, 256 * t) if t < 4 else (SB, 256 * t - 1024)
        gate[:, 128 * t : 128 * t + n] = src[:, at : at + n]
        up[:, 128 * t : 128 * t + n] = src[:, at + 128 : at + 128 + n]
    down[...] = SD[:, 0:FB]
    flip[96:128] = jnp.zeros((32, 256), F32)
    flip[0:96] = SC[:, 128:384]
    out_grad[...] = flip[...].T[0:CH, 0:96]
    for i in range(3):
        at = (384, 0, 512)[i]
        in_grad[i, :, 0:128] = SC[:, at : at + 128]
    in_grad[0, :, 128:192] = SC[:, 640:704]
    in_grad[1, :, 128:192] = pltpu.roll(SC[:, 256:384], 64, 1)[:, :64]
    in_grad[2, :, 128:192] = pltpu.roll(SC[:, 640:768], 64, 1)[:, :64]
    dp, t = lax.axis_index("dp"), lax.axis_index("tensor")
    shares = XR[0, 8:16]
    for i in range(1, 8):
        shares = shares + XR[i, 8:16]
    shares = pltpu.roll(shares, 256 - 12 * t, 1)
    mix[...] = shares[0:1, 0:12]
    ffn[...] = shares[1:2, 0:12]
    k = pltpu.roll(XR[dp // 2, 0:8], lax.rem(256 - 12 * ((dp * 8 + t) % 16), 256), 1)
    taps[...] = k[0:3, 0:12]


def finish_call(*args):
    vm = pl.BlockSpec(memory_space=pltpu.VMEM)
    outs = [shape((ROWS, D)), shape((ROWS, D)), shape((1, 12), F32), shape((3, 96, CH), F32), shape((3, 12), F32)]
    outs += [shape((CH, 96), F32), shape((1, 12), F32), shape((96, FB), F32), shape((96, FB), F32), shape((96, FB), F32)]
    return pl.pallas_call(
        finish_kernel,
        out_shape=tuple(outs),
        in_specs=[vm] * 7,
        out_specs=tuple([vm] * 10),
        scratch_shapes=[pltpu.VMEM((128, 256), F32)],
        compiler_params=pltpu.CompilerParams(vmem_limit_bytes=VMEM_LIMIT),
        name="finish",
    )(*args)


def per_device(tokens, gain_mix, in_weight, conv_kernel, out_weight, gain_ffn, gate_weight, up_weight, down_weight, lengths, cotangent):
    gm, gf, lens = gain_mix.reshape(1, 96), gain_ffn.reshape(1, 96), lengths.reshape(1, 1)
    sums = train_call(
        lens, gm, gf, conv_kernel, tokens, cotangent, in_weight.transpose(1, 0, 2), out_weight, gate_weight,
        up_weight, down_weight.T)
    layer_out, tokens_grad, mix, in_grad, taps_grad, out_grad, ffn, gate, up, down = finish_call(*sums)
    return layer_out, tokens_grad, mix[0], in_grad.transpose(1, 0, 2), taps_grad, out_grad, ffn[0], gate, up, down.T


def solution(mesh):
    placed = (
        P(("dp", "tensor"), None),
        P("dp"),
        P("dp", None, "tensor"),
        P(None, "tensor"),
        P("tensor", "dp"),
        P("dp"),
        P("dp", "tensor"),
        P("dp", "tensor"),
        P("tensor", "dp"),
        P("dp"),
        P(("dp", "tensor"), None),
    )
    return jax.shard_map(
        per_device,
        mesh=mesh,
        in_specs=placed,
        out_specs=(
            P(("dp", "tensor"), None),
            P(("dp", "tensor"), None),
            P(("dp", "tensor")),
            P("dp", None, "tensor"),
            P(None, ("dp", "tensor")),
            P("tensor", "dp"),
            P(("dp", "tensor")),
            P("dp", "tensor"),
            P("dp", "tensor"),
            P("tensor", "dp"),
        ),
        check_vma=False,
    )
```
